256 devices in a mesh: rep: 4 (over z_lo, core), exp: 64 (over z_hi, x, y).
Axes of the slice: x: 4, y: 4, z: 8 (z_hi: 4, z_lo: 2; z = z_hi * 2 + z_lo), core: 2. Of those that a mesh axis runs over, the one named last changes fastest.
Arguments:
- trainer_weight: bfloat16 [4, 64, 4, 64, 3584], P('rep', 'exp'), may hold values from -0.1875 to 0.1875
- owner: int32 [64], replicated, may hold values from 0 to 63, each once
- expert_ids: int32 [16384, 8], P(('rep', 'exp')), may hold values from 0 to 63, all different within a row; in each aligned block of 64 rows (0 to 63, 64 to 127, ...) at most 16 rows name the same one
- gates: float32 [16384, 8], P(('rep', 'exp')), may hold values from 0.1 to 1
- hidden: bfloat16 [16384, 8, 1024], P(('rep', 'exp')), may hold values from -6 to 6
Outputs:
- mixed: bfloat16 [16384, 3584], P(('rep', 'exp'))
The draws below stay inside these ranges and needn't reach their ends.
Inputs may be any that keep to these rules, and one draw needn't show every extreme that they name: `expert_ids`: each row names 8 different slots; within the rows of one device no slot is named by more than 16 rows, and some slot reaches 16 on some device. `owner`: each slot once.
All inputs are finite; a program needn't handle non-finite values.
Results may differ from the reference program's by a relative error of at most 0.0049.
Values may be sent and summed in bfloat16 or wider, within the bound.
No kernel may reach another device: no remote copies, remote signals or barrier semaphores. Data moves between devices by JAX's collectives and lax.ppermute only.
A program may use at most 128 MiB of HBM per device.

```python
import math
import jax
import jax.numpy as jnp
import numpy as np
from jax import lax

D = 3584
H = 1024
TOP = 8
ROWS_DEV = 64
EXPERTS = 64
TP = 16
GROUPS = 4
EXP_TRAIN = 4
CAP = 16
ROWS = 16384
N_REP = 4
N_EXP = 64


def shard_levels(stream_key, extent, split, low, top_value):
    level, own = 1.0, jax.random.fold_in(stream_key, 6)
    for dim, blocks in split:
        heights = jnp.exp(jax.random.uniform(jax.random.fold_in(own, dim), (blocks,), jnp.float32, low / len(split), top_value / len(split)))
        level = level * jnp.repeat(heights, extent[dim] // blocks).reshape([-1 if axis == dim else 1 for axis in range(len(extent))])
    return level


def assign_block(own_key, own, number, rows, count, top, most, slope):
    ranking = jax.random.permutation(own_key, count)
    crowded, common = portions_of(count, rows * top, most, slope, True), portions_of(count, rows * top, most, slope, False)
    places = jnp.arange(count)

    def named(lengths, turn):
        used = int((lengths > 0).sum())
        fixed = max(1, used // 4)
        shifted = fixed + (places - fixed + turn * (used - fixed)) % max(1, count - fixed)
        return jnp.zeros((count,), jnp.int32).at[ranking[jnp.where(places < fixed, places, shifted)]].set(jnp.asarray(lengths, jnp.int32))

    lengths = jnp.where(number % 4 == 0, named(crowded, number // 4), named(common, number - number // 4 - 1))
    mixed = jax.random.permutation(jax.random.fold_in(own, 3), count)
    donor, taker = mixed[0:count // 2 * 2:2], mixed[1:count // 2 * 2:2]
    room = jnp.minimum(lengths[donor] - 1, most - lengths[taker]) // 2
    room = jnp.where((donor == ranking[0]) | (taker == ranking[0]) | (lengths[taker] == 0), 0, jnp.maximum(room, 0))
    shifted = jax.random.randint(jax.random.fold_in(own, 4), (count // 2,), 0, 1 << 20) % (room + 1)
    lengths = lengths.at[donor].add(-shifted).at[taker].add(shifted)
    members = jnp.searchsorted(jnp.cumsum(lengths), jnp.arange(rows * top), side="right").astype(jnp.int32)
    table = members.reshape(top, rows).T
    table = table[jax.random.permutation(jax.random.fold_in(own, 1), rows)]
    turn = jax.random.randint(jax.random.fold_in(own, 2), (rows, 1), 0, top)
    return jnp.take_along_axis(table, (jnp.arange(top)[None, :] + turn) % top, axis=1)


def portions_of(amount, total, bound, lean, full):
    loads = [(1 << 20) // math.isqrt(standing ** lean) + 1 for standing in range(1, amount + 1)]
    largest = bound if full else min(bound, max(-(-total // amount), total * loads[0] // sum(loads)))
    least = 1 if total - largest >= amount - 1 else 0
    counts, rest = [largest] + [least] * (amount - 1), total - largest - least * (amount - 1)
    while rest > 0:
        free = [i for i in range(1, amount) if counts[i] < largest] or [i for i in range(1, amount) if counts[i] < bound]
        pool, left = sum([loads[i] for i in free]), rest
        for i in free:
            extra = min(bound - counts[i], max(1, left * loads[i] // pool), rest)
            counts[i] = counts[i] + extra
            rest = rest - extra
    return np.array(counts)


def normal_values(stream_key, shape, deviation, reach, shards=(), kind=jnp.bfloat16):
    values = jax.random.normal(stream_key, shape, jnp.float32) * deviation
    if len(shards) > 0:
        values = shard_levels(stream_key, shape, shards, -0.22, 0.18) * values
    return jnp.clip(values, min=-reach, max=reach).astype(kind)


def setup_inputs(seed: int = 0) -> dict:
    splits = jax.random.split(jax.random.key(seed), 6)
    trainer_weight = normal_values(splits[0], (N_REP, N_EXP, EXP_TRAIN, H // TP, D), H ** -0.5, 0.1875, ((0, 4), (1, 64)))
    owner = jax.random.permutation(splits[1], EXPERTS).astype(jnp.int32)
    expert_ids_keys = jax.random.split(jax.random.fold_in(splits[2], 1), ROWS // ROWS_DEV)
    expert_ids_turns = jax.random.permutation(jax.random.fold_in(splits[2], 3), ROWS // ROWS_DEV)
    expert_ids = jax.vmap(lambda own, number: assign_block(jax.random.fold_in(splits[2], 2), own, number, ROWS_DEV, EXPERTS, TOP, CAP, 1))(expert_ids_keys, expert_ids_turns).reshape((ROWS, TOP))
    gates = jnp.clip(0.1 + 0.9 * jax.random.uniform(splits[3], (ROWS, TOP), jnp.float32) ** shard_levels(splits[3], (ROWS, TOP), ((0, 256),), -0.2, 0.2), 0.1, 1.0)
    hidden = normal_values(splits[4], (ROWS, TOP, H), 1.0, 6.0, ((0, 256),))
    return {"trainer_weight": trainer_weight, "owner": owner, "expert_ids": expert_ids, "gates": gates, "hidden": hidden}


def reference(trainer_weight, owner, expert_ids, gates, hidden):
    groups = N_REP * N_EXP
    pairs = ROWS_DEV * TOP
    full_weight = trainer_weight.reshape(N_REP, GROUPS, TP, EXP_TRAIN, H // TP, D)
    full_weight = jnp.transpose(full_weight, (0, 1, 3, 2, 4, 5)).reshape(EXPERTS, H, D)
    inverse = jnp.zeros((EXPERTS,), jnp.int32).at[owner].set(jnp.arange(EXPERTS, dtype=jnp.int32))
    sampler_weight = full_weight[inverse]
    routed = expert_ids.reshape(groups, pairs)
    matches = (routed[:, :, None] == jnp.arange(EXPERTS, dtype=jnp.int32)[None, None, :]).astype(jnp.int32)
    position = jnp.sum(jnp.cumsum(matches, axis=1) * matches, axis=2) - 1
    group_index = jnp.broadcast_to(jnp.arange(groups, dtype=jnp.int32)[:, None], (groups, pairs))
    buffer = jnp.zeros((groups, EXPERTS, CAP, H), jnp.bfloat16)
    buffer = buffer.at[group_index, routed, position].set(hidden.reshape(groups, pairs, H))

    def per_expert(operands):
        block, weight = operands
        product = jnp.dot(block.reshape(groups * CAP, H), weight, preferred_element_type=jnp.float32)
        return product.astype(jnp.bfloat16).reshape(groups, CAP, D)

    products = lax.map(per_expert, (jnp.moveaxis(buffer, 1, 0), sampler_weight))
    picked = products[routed, group_index, position].astype(jnp.float32).reshape(ROWS, TOP, D)
    return jnp.sum(picked * gates[:, :, None], axis=1).astype(jnp.bfloat16)
```

```python
import functools
import jax
import jax.numpy as jnp
from jax import lax
from jax.experimental import pallas as pl
from jax.experimental.pallas import tpu as pltpu
from jax.sharding import Mesh, PartitionSpec as P

AXES = ("zl", "c", "zh", "x", "y")
ZC = ("zh", "zl", "c")


def shifted(value, axis, steps):
    count = lax.axis_size(axis)
    return lax.ppermute(value, axis, [(i, (i + steps) % count) for i in range(count)])


def experts_kernel(x_ref, w_ref, gate_ref, row_ref, out_ref, p_ref):
    sources, slots, hidden_width = x_ref.shape
    blocks, experts, depth, width = w_ref.shape
    rows = out_ref.shape[1]
    capacity = slots // experts
    for k in range(experts):
        block = x_ref[:, k * capacity:(k + 1) * capacity, :].reshape(sources * capacity, hidden_width)
        total = jnp.dot(block[:, :depth], w_ref[0, k], preferred_element_type=jnp.float32)
        for b in range(1, blocks):
            total += jnp.dot(
                block[:, b * depth:(b + 1) * depth], w_ref[b, k], preferred_element_type=jnp.float32
            )
        high = total.astype(jnp.bfloat16)
        low = (total - high.astype(jnp.float32)).astype(jnp.bfloat16)
        p_ref[:, k * capacity:(k + 1) * capacity, :] = high.reshape(sources, capacity, width)
        p_ref[:, slots + k * capacity:slots + (k + 1) * capacity, :] = low.reshape(sources, capacity, width)

    def combine(s, _):
        gate = gate_ref[pl.ds(s, 1), :]
        gate_high = gate.astype(jnp.bfloat16).astype(jnp.float32)
        number = lax.broadcasted_iota(jnp.int32, (rows, slots), 0).astype(jnp.float32)
        mine = number == row_ref[pl.ds(s, 1), :]
        c_high = jnp.where(mine, gate_high, 0.0).astype(jnp.bfloat16)
        c_low = jnp.where(mine, gate - gate_high, 0.0).astype(jnp.bfloat16)
        high, low = p_ref[s, :slots], p_ref[s, slots:]
        mixed = jnp.dot(c_high, high, preferred_element_type=jnp.float32)
        mixed += jnp.dot(c_low, high, preferred_element_type=jnp.float32)
        mixed += jnp.dot(c_high, low, preferred_element_type=jnp.float32)
        out_ref[s] = mixed.astype(out_ref.dtype)
        return 0

    lax.fori_loop(0, sources, combine, 0)


def experts_call(x, w, gate, row, rows):
    sources, slots, hidden_width = x.shape
    width = w.shape[3]
    vmem = pl.BlockSpec(memory_space=pltpu.VMEM)
    flops = 2 * sources * slots * hidden_width * width
    return pl.pallas_call(
        experts_kernel,
        out_shape=jax.ShapeDtypeStruct((sources, rows, width), jnp.bfloat16),
        in_specs=[vmem] * 4,
        out_specs=vmem,
        scratch_shapes=[pltpu.VMEM((sources, 2 * slots, width), jnp.bfloat16)],
        compiler_params=pltpu.CompilerParams(vmem_limit_bytes=48 << 20),
        cost_estimate=pl.CostEstimate(
            flops=flops, bytes_accessed=2 * (x.size + w.size + sources * rows * width), transcendentals=0
        ),
    )(x, w, gate, row)


def per_device(trainer_weight, owner, expert_ids, gates, hidden):
    experts = owner.shape[0]
    rows, fanout = expert_ids.shape
    hidden_width = hidden.shape[2]
    capacity = min(rows, 2 * rows * fanout // experts)
    own = trainer_weight[0, 0]
    exp_train, slice_rows, width = own.shape
    ny, nx = lax.axis_size("y"), lax.axis_size("x")
    groups = experts // exp_train
    block_width = width // ny
    y = lax.axis_index("y")

    blocks = own.reshape(exp_train, slice_rows, ny, block_width).transpose(2, 0, 1, 3)
    blocks = lax.all_to_all(blocks, "y", 0, 0, tiled=True)
    blocks = blocks.transpose(1, 0, 2, 3).reshape(exp_train, ny * slice_rows, block_width)
    weight = lax.all_gather(blocks, "x")

    zl, c, zh = (lax.axis_size(a) for a in ("zl", "c", "zh"))
    slot_of = owner.reshape(zl, c, zh, exp_train).transpose(2, 0, 1, 3).reshape(experts)
    match = expert_ids[:, :, None] == slot_of[None, None, :]
    named = jnp.any(match, axis=1)
    position = jnp.cumsum(named.astype(jnp.int32), axis=0) - 1
    place = jnp.arange(experts, dtype=jnp.int32)[None, :] * capacity + position
    flat = jnp.sum(jnp.where(match, place[:, None, :], 0), axis=2).reshape(-1)
    chosen = jnp.arange(experts * capacity, dtype=jnp.int32)[:, None] == flat[None, :]
    pair_row = jnp.arange(rows * fanout, dtype=jnp.int32) // fanout
    slot_gate = jnp.sum(jnp.where(chosen, gates.reshape(-1)[None, :], 0.0), axis=1)
    slot_row = jnp.sum(jnp.where(chosen, pair_row[None, :] + 1, 0), axis=1) - 1
    outbound = jnp.dot(
        chosen.astype(jnp.bfloat16), hidden.reshape(-1, hidden_width), preferred_element_type=jnp.float32
    ).astype(jnp.bfloat16)
    slots = exp_train * capacity
    info = jnp.stack([slot_gate.reshape(groups, slots), slot_row.astype(jnp.float32).reshape(groups, slots)], 1)
    info = lax.all_to_all(info, ZC, 0, 0, tiled=True)
    arrived = lax.all_to_all(outbound.reshape(groups, slots, hidden_width), ZC, 0, 0, tiled=True)

    partials = []
    for step in range(ny):
        x_step = arrived if step == 0 else shifted(arrived, "y", step)
        info_step = info if step == 0 else shifted(info, "y", step)
        partials.append(experts_call(x_step, weight, info_step[:, 0], info_step[:, 1], rows))
    partial = jnp.stack(partials, 1)
    summed = lax.psum_scatter(partial.reshape(-1, block_width), ZC, scatter_dimension=0, tiled=True)
    summed = summed.reshape(ny, rows, block_width)
    summed = jnp.take(summed, (y - jnp.arange(ny)) % ny, axis=0)
    final = lax.all_to_all(summed, "y", 0, 0, tiled=True)
    return final.transpose(1, 0, 2).reshape(rows, width)


def solution(mesh):
    devices = mesh.devices.reshape(2, 2, 4, 4, 4)
    inner = Mesh(devices, AXES)
    rep, exp = ("zl", "c"), ("zh", "x", "y")
    return jax.shard_map(
        per_device,
        mesh=inner,
        in_specs=(
            P(rep, exp, None, None, None),
            P(),
            P(rep + exp, None),
            P(rep + exp, None),
            P(rep + exp, None, None),
        ),
        out_specs=P(rep + exp, None),
        check_vma=False,
    )
```

```python
import functools
import jax
import jax.numpy as jnp
from jax import lax
from jax.experimental import pallas as pl
from jax.experimental.pallas import tpu as pltpu
from jax.sharding import Mesh, PartitionSpec as P

AXES = ("zl", "c", "zh", "x", "y")
Z = ("zh", "zl")
NZ = 8
NEAR = 3
VMEM = pl.BlockSpec(memory_space=pltpu.VMEM)
SMEM = pl.BlockSpec(memory_space=pltpu.SMEM)
PARAMS = pltpu.CompilerParams(vmem_limit_bytes=48 << 20)


def shifted(value, axis, steps):
    count = lax.axis_size(axis)
    return lax.ppermute(value, axis, [(i, (i + steps) % count) for i in range(count)])


def shifted_z(value, steps):
    low, high = lax.axis_size("zl"), lax.axis_size("zh")
    number = lambda z: z % NZ % low * high + z % NZ // low
    return lax.ppermute(value, ("zl", "zh"), [(number(z), number(z + steps)) for z in range(NZ)])


def cost(flops, *arrays):
    size = sum(a.size * a.dtype.itemsize for a in arrays)
    return pl.CostEstimate(flops=flops, bytes_accessed=size, transcendentals=0)


def split_kernel(pos_ref, w_ref, *out_refs):
    count = len(out_refs)
    width = out_refs[0].shape[2]
    for d, out_ref in enumerate(out_refs):
        start = pl.multiple_of(lax.rem(pos_ref[2] + d, count) * width, 128)
        out_ref[...] = w_ref[:, :, pl.ds(start, width)]


def split_blocks(pos, own, count):
    exp_train, depth, width = own.shape
    shape = jax.ShapeDtypeStruct((exp_train, depth, width // count), own.dtype)
    return pl.pallas_call(
        split_kernel, out_shape=[shape] * count, in_specs=[SMEM, VMEM], out_specs=[VMEM] * count,
        compiler_params=PARAMS, cost_estimate=cost(0, own, own),
    )(pos, own)


def join_kernel(pos_ref, *refs):
    in_refs, out_ref = refs[:-1], refs[-1]
    count, depth = len(in_refs), in_refs[0].shape[1]
    for d, in_ref in enumerate(in_refs):
        start = pl.multiple_of(lax.rem(pos_ref[2] + count - d, count) * depth, depth)
        out_ref[:, pl.ds(start, depth), :] = in_ref[...]


def join_blocks(pos, blocks):
    exp_train, depth, width = blocks[0].shape
    shape = jax.ShapeDtypeStruct((exp_train, depth * len(blocks), width), blocks[0].dtype)
    return pl.pallas_call(
        join_kernel, out_shape=shape, in_specs=[SMEM] + [VMEM] * len(blocks), out_specs=VMEM,
        compiler_params=PARAMS, cost_estimate=cost(0, shape, shape),
    )(pos, *blocks)


def dispatch_kernel(pos_ref, flat_ref, hidden_own_ref, hidden_other_ref, *out_refs):
    slots = out_refs[0].shape[1]
    pairs = flat_ref.shape[1]
    numbers = []
    for d in range(NZ):
        base = (lax.rem(pos_ref[0] + d, NZ) * 2 + pos_ref[1]) * slots
        numbers.append(base + lax.broadcasted_iota(jnp.int32, (slots, pairs), 0))
    numbers = jnp.concatenate(numbers, 0)
    for source, ref in enumerate((hidden_own_ref, hidden_other_ref)):
        chosen = jnp.where(numbers == flat_ref[source:source + 1, :], 1.0, 0.0).astype(jnp.bfloat16)
        rows = jnp.dot(chosen, ref[...], preferred_element_type=jnp.float32).astype(jnp.bfloat16)
        for d, out_ref in enumerate(out_refs):
            out_ref[source] = rows[d * slots:(d + 1) * slots]


def dispatch(pos, flat, own, other, slots):
    shape = jax.ShapeDtypeStruct((2, slots, own.shape[1]), own.dtype)
    return pl.pallas_call(
        dispatch_kernel, out_shape=[shape] * NZ, in_specs=[SMEM] + [VMEM] * 3, out_specs=[VMEM] * NZ,
        compiler_params=PARAMS, cost_estimate=cost(4 * NZ * slots * own.size, own, other, own, own, own, own),
    )(pos, flat, own, other)


def experts_kernel(pos_ref, near_ref, far_ref, w_ref, gate_ref, row_ref, mine_ref, other_ref, p_ref):
    _, _, slots, hidden_width = near_ref.shape
    width = w_ref.shape[3]
    experts = w_ref.shape[1]
    rows = mine_ref.shape[1]
    capacity = slots // experts
    planes = NEAR * 2
    for k in range(experts):
        part = slice(k * capacity, (k + 1) * capacity)
        block = jnp.concatenate(
            [ref[:, :, part, :].reshape(-1, hidden_width) for ref in (near_ref, far_ref)], 0
        )
        total = jnp.dot(block, w_ref[:, k].reshape(hidden_width, width), preferred_element_type=jnp.float32)
        high = total.astype(jnp.bfloat16)
        low = (total - high.astype(jnp.float32)).astype(jnp.bfloat16)
        high, low = (v.reshape(-1, capacity, width) for v in (high, low))
        p_ref[:, part, :] = high
        p_ref[:, slots + part.start:slots + part.stop, :] = high
        p_ref[:, 2 * slots + part.start:2 * slots + part.stop, :] = low
    z, c, y = pos_ref[0], pos_ref[1], pos_ref[2]
    number = lax.broadcasted_iota(jnp.int32, (rows, 3 * slots), 0).astype(jnp.float32)
    column = lax.broadcasted_iota(jnp.int32, (rows, 3 * slots), 1)
    middle = (column >= slots) & (column < 2 * slots)

    def combine(plane, _):
        source = lax.rem(z + NZ + 1 - plane, NZ)
        for core, out_ref in enumerate((mine_ref, other_ref)):
            index = (source * 2 + lax.rem(c + core, 2)) * 4 + y
            gate = gate_ref[pl.ds(index, 1), :]
            gate_high = gate.astype(jnp.bfloat16).astype(jnp.float32)
            value = jnp.where(middle, gate - gate_high, gate_high)
            weights = jnp.where(number == row_ref[pl.ds(index, 1), :], value, 0.0).astype(jnp.bfloat16)
            mixed = jnp.dot(weights, p_ref[plane * 2 + core], preferred_element_type=jnp.float32)
            out_ref[source] = mixed.astype(out_ref.dtype)
        return 0

    lax.fori_loop(0, NZ, combine, 0)


def experts_call(pos, near, far, w, gate, row, rows):
    slots, hidden_width = near.shape[2:]
    width = w.shape[3]
    mine = jax.ShapeDtypeStruct((NZ, rows, width), jnp.float32)
    other = jax.ShapeDtypeStruct((NZ, rows, width), jnp.bfloat16)
    return pl.pallas_call(
        experts_kernel,
        out_shape=[mine, other],
        in_specs=[SMEM] + [VMEM] * 5,
        out_specs=[VMEM] * 2,
        scratch_shapes=[pltpu.VMEM((2 * NZ, 3 * slots, width), jnp.bfloat16)],
        compiler_params=PARAMS,
        cost_estimate=cost(4 * NZ * slots * hidden_width * width, near, far, w, mine, other),
    )(pos, near, far, w, gate, row)


def place_kernel(pos_ref, *refs):
    in_refs, out_ref = refs[:-1], refs[-1]
    width = in_refs[0].shape[1]
    for d, in_ref in enumerate(in_refs):
        start = pl.multiple_of(lax.rem(pos_ref[2] + d, len(in_refs)) * width, 128)
        out_ref[:, pl.ds(start, width)] = in_ref[...]


def place_blocks(pos, blocks):
    rows, width = blocks[0].shape
    shape = jax.ShapeDtypeStruct((rows, width * len(blocks)), blocks[0].dtype)
    return pl.pallas_call(
        place_kernel, out_shape=shape, in_specs=[SMEM] + [VMEM] * len(blocks), out_specs=VMEM,
        compiler_params=PARAMS, cost_estimate=cost(0, shape, shape),
    )(pos, *blocks)


def per_device(trainer_weight, owner, expert_ids, gates, hidden):
    experts = owner.shape[0]
    rows, fanout = expert_ids.shape
    hidden_width = hidden.shape[2]
    capacity = min(rows, 2 * rows * fanout // experts)
    own = trainer_weight[0, 0]
    exp_train, slice_rows, width = own.shape
    ny = lax.axis_size("y")
    groups = experts // exp_train
    slots = exp_train * capacity
    block_width = width // ny
    low = lax.axis_size("zl")
    z, c, y = lax.axis_index("zh") * low + lax.axis_index("zl"), lax.axis_index("c"), lax.axis_index("y")
    pos = jnp.stack([z, c, y]).astype(jnp.int32)

    zl, cs, zh = (lax.axis_size(a) for a in ("zl", "c", "zh"))
    slot_of = owner.reshape(zl, cs, zh, exp_train).transpose(2, 0, 1, 3).reshape(experts)
    match = expert_ids[:, :, None] == slot_of[None, None, :]
    named = jnp.any(match, axis=1)
    position = jnp.cumsum(named.astype(jnp.int32), axis=0) - 1
    place = jnp.arange(experts, dtype=jnp.int32)[None, :] * capacity + position
    flat = jnp.sum(jnp.where(match, place[:, None, :], 0), axis=2).reshape(1, -1)
    pairs = hidden.reshape(-1, hidden_width)
    other_pairs = shifted(pairs, "c", 1)
    other_flat = shifted(flat, "c", 1)

    blocks = split_blocks(pos, own, ny)
    blocks = [blocks[0]] + [shifted(blocks[d], "y", d) for d in range(1, ny)]
    weight = lax.all_gather(join_blocks(pos, blocks), "x")

    outbound = dispatch(pos, jnp.concatenate([flat, other_flat], 0), pairs, other_pairs, slots)
    arrived = [outbound[0]] + [shifted_z(outbound[d], d) for d in range(1, NZ)]
    near = jnp.stack([arrived[NZ - 1], arrived[0], arrived[1]])
    far = jnp.stack(arrived[2:NZ - 1])

    chosen = jnp.arange(experts * capacity, dtype=jnp.int32)[:, None] == flat
    pair_row = jnp.arange(rows * fanout, dtype=jnp.int32) // fanout
    slot_gate = jnp.sum(jnp.where(chosen, gates.reshape(-1)[None, :], 0.0), axis=1).reshape(groups, 1, slots)
    slot_row = jnp.sum(jnp.where(chosen, pair_row[None, :] + 1, 0), axis=1).reshape(groups, 1, slots) - 1
    info = jnp.concatenate([slot_gate, slot_row.astype(jnp.float32)], 2)
    info = jnp.broadcast_to(info, (groups, ny, 2 * slots)).reshape(groups * ny, 2 * slots)
    info = lax.all_to_all(info, Z + ("c", "y"), 0, 0, tiled=True)
    gate = jnp.tile(info[:, :slots], (1, 3))
    row = jnp.tile(info[:, slots:], (1, 3))

    partials = []
    for step in (0, 1, ny - 1, 2):
        near_step = near if step == 0 else shifted(near, "y", step)
        far_step = far if step == 0 else shifted(far, "y", step)
        pos_step = jnp.stack([z, c, (y + ny - step) % ny]).astype(jnp.int32)
        mine, other = experts_call(pos_step, near_step, far_step, weight, gate, row, rows)
        other = shifted(other, "c", 1)
        partials.append((mine + other.astype(jnp.float32)).astype(jnp.bfloat16))
    partial = jnp.stack(partials, 1).reshape(-1, block_width)
    summed = lax.psum_scatter(partial, Z, scatter_dimension=0, tiled=True).reshape(ny, rows, block_width)
    final = [summed[0], shifted(summed[1], "y", -1), shifted(summed[3], "y", 2), shifted(summed[2], "y", 1)]
    return place_blocks(pos, final)


def solution(mesh):
    devices = mesh.devices.reshape(2, 2, 4, 4, 4)
    inner = Mesh(devices, AXES)
    rep, exp = ("zl", "c"), ("zh", "x", "y")
    return jax.shard_map(
        per_device,
        mesh=inner,
        in_specs=(
            P(rep, exp, None, None, None),
            P(),
            P(rep + exp, None),
            P(rep + exp, None),
            P(rep + exp, None, None),
        ),
        out_specs=P(rep + exp, None),
        check_vma=False,
    )
```

```python
import functools
import jax
import jax.numpy as jnp
from jax import lax
from jax.experimental import pallas as pl
from jax.experimental.pallas import tpu as pltpu
from jax.sharding import Mesh, PartitionSpec as P

AXES = ("zl", "c", "zh", "x", "y")
Z = ("zh", "zl")
VMEM = pl.BlockSpec(memory_space=pltpu.VMEM)
SMEM = pl.BlockSpec(memory_space=pltpu.SMEM)
PARAMS = pltpu.CompilerParams(vmem_limit_bytes=48 << 20)


def shifted(value, axis, steps):
    count = lax.axis_size(axis)
    return lax.ppermute(value, axis, [(i, (i + steps) % count) for i in range(count)])


def after(value, *others):
    return lax.optimization_barrier((value, *others))[0]


def cost(flops, *arrays):
    size = sum(a.size * a.dtype.itemsize for a in arrays)
    return pl.CostEstimate(flops=flops, bytes_accessed=size, transcendentals=0)


def split_kernel(pos_ref, w_ref, *out_refs):
    count = len(out_refs)
    width = out_refs[0].shape[2]
    for d, out_ref in enumerate(out_refs):
        start = pl.multiple_of(lax.rem(pos_ref[2] + d, count) * width, 128)
        out_ref[...] = w_ref[:, :, pl.ds(start, width)]


def split_blocks(pos, own, count):
    exp_train, depth, width = own.shape
    shape = jax.ShapeDtypeStruct((exp_train, depth, width // count), own.dtype)
    return pl.pallas_call(
        split_kernel, out_shape=[shape] * count, in_specs=[SMEM, VMEM], out_specs=[VMEM] * count,
        compiler_params=PARAMS, cost_estimate=cost(0, own, own),
    )(pos, own)


def join_kernel(pos_ref, *refs):
    in_refs, out_ref = refs[:-1], refs[-1]
    count, depth = len(in_refs), in_refs[0].shape[1]
    for d, in_ref in enumerate(in_refs):
        start = pl.multiple_of(lax.rem(pos_ref[2] + count - d, count) * depth, depth)
        out_ref[:, pl.ds(start, depth), :] = in_ref[...]


def join_blocks(pos, blocks):
    exp_train, depth, width = blocks[0].shape
    shape = jax.ShapeDtypeStruct((exp_train, depth * len(blocks), width), blocks[0].dtype)
    return pl.pallas_call(
        join_kernel, out_shape=shape, in_specs=[SMEM] + [VMEM] * len(blocks), out_specs=VMEM,
        compiler_params=PARAMS, cost_estimate=cost(0, shape, shape),
    )(pos, *blocks)


def dispatch_kernel(groups, first_ref, flat_ref, hidden_ref, out_ref):
    slots, pairs = out_ref.shape[1], flat_ref.shape[1]
    whole = 2 * slots
    number = lax.broadcasted_iota(jnp.int32, (groups * slots, pairs), 0)
    number = number // slots * whole + lax.rem(number, slots) + first_ref[0]
    chosen = jnp.where(number == flat_ref[...], 1.0, 0.0).astype(jnp.bfloat16)
    rows = jnp.dot(chosen, hidden_ref[...], preferred_element_type=jnp.float32).astype(jnp.bfloat16)
    out_ref[...] = rows.reshape(out_ref.shape)


def dispatch(first, flat, hidden, groups, slots):
    shape = jax.ShapeDtypeStruct((groups, slots, hidden.shape[1]), hidden.dtype)
    return pl.pallas_call(
        functools.partial(dispatch_kernel, groups),
        out_shape=shape, in_specs=[SMEM, VMEM, VMEM], out_specs=VMEM,
        compiler_params=PARAMS, cost_estimate=cost(2 * groups * slots * hidden.size, hidden, shape),
    )(jnp.full((1,), first, jnp.int32), flat, hidden)


def experts_kernel(steps, counts, pos_ref, *refs):
    half = sum(counts)
    x_refs, w_refs = (refs[:half], refs[half:2 * half]), refs[2 * half:2 * half + 5]
    gate_ref, row_ref, mine_ref, other_ref, x_ref, p_ref = refs[2 * half + 5:]
    turn, k = pl.program_id(0), pl.program_id(1)
    capacity, hidden_width = x_refs[0][0].shape[-2:]
    experts = pl.num_programs(1)
    slots = capacity * experts
    depth, width = w_refs[0].shape[1:]
    planes, _, rows, _ = mine_ref.shape
    c, x = pos_ref[1], pos_ref[3]
    first = 0
    for number, count in enumerate(counts):
        for part in range(2):
            @pl.when((turn == number) & (k // 2 == part))
            def _(first=first, count=count, part=part):
                for d in range(4):
                    start = pl.multiple_of(lax.rem(x + 4 - d, 4) * depth, 128)
                    block = [r[:, :, pl.ds(start, depth)].reshape(-1, depth) for r in x_refs[part][first:first + count]]
                    x_ref[:, d * depth:(d + 1) * depth] = jnp.concatenate(block, 0)
        first += count
    opposite = jnp.where(k < 2, w_refs[2][0], w_refs[3][0])
    weights = jnp.concatenate([w_refs[0][0], w_refs[1][0], opposite, w_refs[4][0]], 0)
    total = jnp.dot(x_ref[...], weights, preferred_element_type=jnp.float32)
    high = total.astype(jnp.bfloat16)
    low = (total - high.astype(jnp.float32)).astype(jnp.bfloat16)
    high, low = (v.reshape(-1, capacity, width) for v in (high, low))
    for part, value in enumerate((high, high, low)):
        start = pl.multiple_of(part * slots + k * capacity, capacity)
        p_ref[:, pl.ds(start, capacity), :] = value

    @pl.when(k == experts - 1)
    def _():
        number = lax.broadcasted_iota(jnp.int32, (rows, 3 * slots), 0).astype(jnp.float32)
        column = lax.broadcasted_iota(jnp.int32, (rows, 3 * slots), 1)
        middle = (column >= slots) & (column < 2 * slots)
        step = steps[0] + turn * (steps[-1] - steps[0])
        for plane in range(planes):
            for core, out_ref in enumerate((mine_ref, other_ref)):
                source = plane * 2 + lax.rem(c + core, 2)
                index = source * 4 + step
                gate = gate_ref[pl.ds(index, 1), :]
                gate_high = gate.astype(jnp.bfloat16).astype(jnp.float32)
                value = jnp.where(middle, gate - gate_high, gate_high)
                combine = jnp.where(number == row_ref[pl.ds(index, 1), :], value, 0.0).astype(jnp.bfloat16)
                mixed = jnp.dot(combine, p_ref[source], preferred_element_type=jnp.float32)
                out_ref[plane, 0] = mixed.astype(out_ref.dtype)


def experts_call(steps, pos, xs, ws, gate, row, rows):
    experts, depth, width = ws[0].shape
    half = experts // 2
    hidden_width = xs[0][0][0].shape[2]
    capacity = xs[0][0][0].shape[1] // half
    groups = sum(v.shape[0] for v in xs[0][0])
    turns = len(steps)
    mine = jax.ShapeDtypeStruct((groups // 2, turns, rows, width), jnp.float32)
    other = jax.ShapeDtypeStruct((groups // 2, turns, rows, width), jnp.bfloat16)
    arrays, specs = [], []
    for part in range(2):
        for turn in range(turns):
            for v in xs[turn][part]:
                def index(t, k, part=part, turn=turn):
                    now = jnp.clip(k - part * half, 0, half - 1)
                    return 0, jnp.where(t == turn, now, jnp.where(t < turn, 0, half - 1)), 0

                arrays.append(v)
                specs.append(pl.BlockSpec((v.shape[0], capacity, hidden_width), index))
    kinds = [lambda k: k, lambda k: k, lambda k: jnp.minimum(k, half - 1), lambda k: jnp.maximum(k - half, 0), lambda k: k]
    w_specs = [pl.BlockSpec((1, depth, width), lambda t, k, f=f: (f(k), 0, 0)) for f in kinds]
    whole = pl.BlockSpec((groups // 2, 1, rows, width), lambda t, k: (0, t, 0, 0))
    info = pl.BlockSpec(gate.shape, lambda t, k: (0, 0))
    flops = 2 * turns * groups * capacity * experts * hidden_width * width
    return pl.pallas_call(
        functools.partial(experts_kernel, steps, [len(v[0]) for v in xs]),
        grid=(turns, experts),
        out_shape=[mine, other],
        in_specs=[SMEM] + specs + w_specs + [info] * 2,
        out_specs=[whole] * 2,
        scratch_shapes=[
            pltpu.VMEM((groups * capacity, hidden_width), jnp.bfloat16),
            pltpu.VMEM((groups, 3 * experts * capacity, width), jnp.bfloat16),
        ],
        compiler_params=PARAMS,
        cost_estimate=cost(flops, *arrays, *ws, *ws, mine, other),
    )(pos, *arrays, *ws, gate, row)


def place_kernel(pos_ref, *refs):
    in_refs, out_ref = refs[:-1], refs[-1]
    width = in_refs[0].shape[1]
    for d, in_ref in enumerate(in_refs):
        start = pl.multiple_of(lax.rem(pos_ref[2] + d, len(in_refs)) * width, 128)
        out_ref[:, pl.ds(start, width)] = in_ref[...]


def place_blocks(pos, blocks):
    rows, width = blocks[0].shape
    shape = jax.ShapeDtypeStruct((rows, width * len(blocks)), blocks[0].dtype)
    return pl.pallas_call(
        place_kernel, out_shape=shape, in_specs=[SMEM] + [VMEM] * len(blocks), out_specs=VMEM,
        compiler_params=PARAMS, cost_estimate=cost(0, shape, shape),
    )(pos, *blocks)


def per_device(trainer_weight, owner, expert_ids, gates, hidden):
    experts = owner.shape[0]
    rows, fanout = expert_ids.shape
    hidden_width = hidden.shape[2]
    capacity = min(rows, 2 * rows * fanout // experts)
    own = trainer_weight[0, 0]
    exp_train, slice_rows, width = own.shape
    ny = lax.axis_size("y")
    groups = experts // exp_train
    slots = exp_train * capacity
    block_width = width // ny
    low = lax.axis_size("zl")
    z, c, y = lax.axis_index("zh") * low + lax.axis_index("zl"), lax.axis_index("c"), lax.axis_index("y")
    pos = jnp.stack([z, c, y, lax.axis_index("x")]).astype(jnp.int32)

    zl, cs, zh = (lax.axis_size(a) for a in ("zl", "c", "zh"))
    slot_of = owner.reshape(zl, cs, zh, exp_train).transpose(2, 0, 1, 3).reshape(experts)
    match = expert_ids[:, :, None] == slot_of[None, None, :]
    named = jnp.any(match, axis=1)
    position = jnp.cumsum(named.astype(jnp.int32), axis=0) - 1
    place = jnp.arange(experts, dtype=jnp.int32)[None, :] * capacity + position
    flat = jnp.sum(jnp.where(match, place[:, None, :], 0), axis=2).reshape(1, -1)
    pairs = hidden.reshape(-1, hidden_width)
    group_axes = Z + ("c",)

    blocks = split_blocks(pos, own, ny)
    blocks = [blocks[0]] + [shifted(blocks[d], "y", d) for d in range(1, ny)]

    outbound = dispatch(0, flat, pairs, groups, slots // 2)
    blocks[1] = after(blocks[1], outbound)
    first = lax.all_to_all(outbound, group_axes, 0, 0, tiled=True)

    chosen = jnp.arange(experts * capacity, dtype=jnp.int32)[:, None] == flat
    pair_row = jnp.arange(rows * fanout, dtype=jnp.int32) // fanout
    slot_gate = jnp.sum(jnp.where(chosen, gates.reshape(-1)[None, :], 0.0), axis=1).reshape(groups, slots)
    slot_row = jnp.sum(jnp.where(chosen, pair_row[None, :] + 1, 0), axis=1).reshape(groups, slots) - 1
    info = jnp.concatenate([slot_gate, slot_row.astype(jnp.float32)], 1)
    info = jnp.stack([info] + [shifted(info, "y", d) for d in range(1, ny)], 1)

    weight = join_blocks(pos, blocks)
    weight_up, weight_down = shifted(weight, "x", 1), shifted(weight, "x", -1)

    first_up, first_down = shifted(first, "y", 1), shifted(first, "y", -1)
    outbound = dispatch(slots // 2, flat, pairs, groups, slots // 2)
    second = lax.all_to_all(after(outbound, first, weight, info), group_axes, 0, 0, tiled=True)
    middle = groups // 2
    first_up, first_down, weight_up, weight_down = lax.optimization_barrier(
        (first_up, first_down, weight_up, weight_down)
    )
    first_opposite = [shifted(first_up[:middle], "y", 1), shifted(first_down[middle:], "y", -1)]
    half = exp_train // 2
    weight_opposite = [shifted(weight_up[:half], "x", 1), shifted(weight_down[half:], "x", -1)]
    weights = [weight, weight_up, *weight_opposite, weight_down]
    second_late = after(second, first_up, first_down, weight_up, weight_down)
    second_up, second_down = shifted(second_late, "y", 1), shifted(second_late, "y", -1)
    info = lax.all_to_all(after(info, second), group_axes, 0, 0, tiled=True).reshape(groups * ny, 2 * slots)
    gate = jnp.tile(info[:, :slots], (1, 3))
    row = jnp.tile(info[:, slots:], (1, 3))
    second_opposite = [shifted(second_up[:middle], "y", 1), shifted(second_down[middle:], "y", -1)]

    partials = []
    own_rows, up_rows = ([first], [second]), ([first_up], [second_up])
    down_rows, opposite_rows = ([first_down], [second_down]), (first_opposite, second_opposite)
    for steps, xs in (((0, 1), (own_rows, up_rows)), ((ny - 1, 2), (down_rows, opposite_rows))):
        mine, other = experts_call(steps, pos, xs, weights, gate, row, rows)
        other = shifted(other, "c", 1)
        partials.append((mine + other.astype(jnp.float32)).astype(jnp.bfloat16))
    partial = jnp.concatenate(partials, 1).reshape(-1, block_width)
    summed = lax.psum_scatter(partial, Z, scatter_dimension=0, tiled=True).reshape(ny, rows, block_width)
    final = [summed[0], shifted(summed[1], "y", -1), shifted(summed[3], "y", 2), shifted(summed[2], "y", 1)]
    return place_blocks(pos, final)


def solution(mesh):
    devices = mesh.devices.reshape(2, 2, 4, 4, 4)
    inner = Mesh(devices, AXES)
    rep, exp = ("zl", "c"), ("zh", "x", "y")
    return jax.shard_map(
        per_device,
        mesh=inner,
        in_specs=(
            P(rep, exp, None, None, None),
            P(),
            P(rep + exp, None),
            P(rep + exp, None),
            P(rep + exp, None, None),
        ),
        out_specs=P(rep + exp, None),
        check_vma=False,
    )
```

```python
import functools
import jax
import jax.numpy as jnp
from jax import lax
from jax.experimental import pallas as pl
from jax.experimental.pallas import tpu as pltpu
from jax.sharding import Mesh, PartitionSpec as P

AXES = ("zl", "c", "zh", "x", "y")
Z = ("zh", "zl")
VMEM = pl.BlockSpec(memory_space=pltpu.VMEM)
SMEM = pl.BlockSpec(memory_space=pltpu.SMEM)
PARAMS = pltpu.CompilerParams(vmem_limit_bytes=48 << 20)


def shifted(value, axis, steps):
    count = lax.axis_size(axis)
    return lax.ppermute(value, axis, [(i, (i + steps) % count) for i in range(count)])


def after(value, *others):
    return lax.optimization_barrier((value, *others))[0]


def cost(flops, *arrays):
    size = sum(a.size * a.dtype.itemsize for a in arrays)
    return pl.CostEstimate(flops=flops, bytes_accessed=size, transcendentals=0)


def split_kernel(pos_ref, w_ref, *out_refs):
    count = len(out_refs)
    width = out_refs[0].shape[2]
    for d, out_ref in enumerate(out_refs):
        start = pl.multiple_of(lax.rem(pos_ref[2] + d, count) * width, 128)
        out_ref[...] = w_ref[:, :, pl.ds(start, width)]


def split_blocks(pos, own, count):
    exp_train, depth, width = own.shape
    shape = jax.ShapeDtypeStruct((exp_train, depth, width // count), own.dtype)
    return pl.pallas_call(
        split_kernel, out_shape=[shape] * count, in_specs=[SMEM, VMEM], out_specs=[VMEM] * count,
        compiler_params=PARAMS, cost_estimate=cost(0, own, own),
    )(pos, own)


def join_kernel(pos_ref, *refs):
    in_refs, out_ref = refs[:-1], refs[-1]
    count, depth = len(in_refs), in_refs[0].shape[1]
    for d, in_ref in enumerate(in_refs):
        start = pl.multiple_of(lax.rem(pos_ref[2] + count - d, count) * depth, depth)
        out_ref[:, pl.ds(start, depth), :] = in_ref[...]


def join_blocks(pos, blocks):
    exp_train, depth, width = blocks[0].shape
    shape = jax.ShapeDtypeStruct((exp_train, depth * len(blocks), width), blocks[0].dtype)
    return pl.pallas_call(
        join_kernel, out_shape=shape, in_specs=[SMEM] + [VMEM] * len(blocks), out_specs=VMEM,
        compiler_params=PARAMS, cost_estimate=cost(0, shape, shape),
    )(pos, *blocks)


def dispatch_kernel(groups, first_ref, flat_ref, hidden_ref, out_ref):
    slots, pairs = out_ref.shape[1], flat_ref.shape[1]
    whole = 2 * slots
    number = lax.broadcasted_iota(jnp.int32, (groups * slots, pairs), 0)
    number = number // slots * whole + lax.rem(number, slots) + first_ref[0]
    chosen = jnp.where(number == flat_ref[...], 1.0, 0.0).astype(jnp.bfloat16)
    rows = jnp.dot(chosen, hidden_ref[...], preferred_element_type=jnp.float32).astype(jnp.bfloat16)
    out_ref[...] = rows.reshape(out_ref.shape)


def dispatch(first, flat, hidden, groups, slots):
    shape = jax.ShapeDtypeStruct((groups, slots, hidden.shape[1]), hidden.dtype)
    return pl.pallas_call(
        functools.partial(dispatch_kernel, groups),
        out_shape=shape, in_specs=[SMEM, VMEM, VMEM], out_specs=VMEM,
        compiler_params=PARAMS, cost_estimate=cost(2 * groups * slots * hidden.size, hidden, shape),
    )(jnp.full((1,), first, jnp.int32), flat, hidden)


def experts_kernel(steps, pos_ref, *refs):
    turns = len(steps)
    x_refs = refs[:turns], refs[turns:2 * turns]
    w_ref, gate_ref, row_ref, mine_ref, other_ref, p_ref = refs[2 * turns:]
    k, turn = pl.program_id(0), pl.program_id(1)
    groups, capacity, hidden_width = x_refs[0][0].shape
    experts = pl.num_programs(0)
    slots = capacity * experts
    width = w_ref.shape[3]
    planes, _, rows, _ = mine_ref.shape
    c = pos_ref[1]
    for number in range(turns):
        for part in range(2):
            @pl.when((turn == number) & (k // 2 == part))
            def _(number=number, part=part):
                total = jnp.dot(
                    x_refs[part][number][...].reshape(groups * capacity, hidden_width),
                    w_ref[...].reshape(hidden_width, width),
                    preferred_element_type=jnp.float32,
                )
                high = total.astype(jnp.bfloat16)
                low = (total - high.astype(jnp.float32)).astype(jnp.bfloat16)
                high, low = (v.reshape(groups, capacity, width) for v in (high, low))
                for block, value in enumerate((high, high, low)):
                    start = pl.multiple_of(block * slots + k * capacity, capacity)
                    p_ref[number, :, pl.ds(start, capacity), :] = value

    @pl.when(k == experts - 1)
    def _():
        number = lax.broadcasted_iota(jnp.int32, (rows, 3 * slots), 0).astype(jnp.float32)
        column = lax.broadcasted_iota(jnp.int32, (rows, 3 * slots), 1)
        middle = (column >= slots) & (column < 2 * slots)
        step = steps[0] + turn * (steps[-1] - steps[0])
        for plane in range(planes):
            for core, out_ref in enumerate((mine_ref, other_ref)):
                source = plane * 2 + lax.rem(c + core, 2)
                index = source * 4 + step
                gate = gate_ref[pl.ds(index, 1), :]
                gate_high = gate.astype(jnp.bfloat16).astype(jnp.float32)
                value = jnp.where(middle, gate - gate_high, gate_high)
                combine = jnp.where(number == row_ref[pl.ds(index, 1), :], value, 0.0).astype(jnp.bfloat16)
                mixed = jnp.dot(combine, p_ref[turn, source], preferred_element_type=jnp.float32)
                out_ref[plane, 0] = mixed.astype(out_ref.dtype)


def experts_call(steps, pos, xs, weight, gate, row, rows):
    blocks, experts, depth, width = weight.shape
    half = experts // 2
    groups, slots, hidden_width = xs[0][0].shape
    capacity = slots // half
    turns = len(steps)
    mine = jax.ShapeDtypeStruct((groups // 2, turns, rows, width), jnp.float32)
    other = jax.ShapeDtypeStruct((groups // 2, turns, rows, width), jnp.bfloat16)
    arrays, specs = [], []
    for part in range(2):
        for turn in range(turns):
            def index(k, t, part=part, turn=turn):
                now = jnp.where(t > turn, k + 1, k) if turn < turns - 1 else k
                return 0, jnp.clip(now - part * half, 0, half - 1), 0

            arrays.append(xs[turn][part])
            specs.append(pl.BlockSpec((groups, capacity, hidden_width), index))
    whole = pl.BlockSpec((groups // 2, 1, rows, width), lambda k, t: (0, jnp.where(k == experts - 1, t, 0), 0, 0))
    info = pl.BlockSpec(gate.shape, lambda k, t: (0, 0))
    flops = 2 * turns * groups * capacity * experts * hidden_width * width
    return pl.pallas_call(
        functools.partial(experts_kernel, steps),
        grid=(experts, turns),
        out_shape=[mine, other],
        in_specs=[SMEM] + specs + [pl.BlockSpec((blocks, 1, depth, width), lambda k, t: (0, k, 0, 0))] + [info] * 2,
        out_specs=[whole] * 2,
        scratch_shapes=[pltpu.VMEM((turns, groups, 3 * experts * capacity, width), jnp.bfloat16)],
        compiler_params=PARAMS,
        cost_estimate=cost(flops, *arrays, weight, mine, other),
    )(pos, *arrays, weight, gate, row)


def place_kernel(pos_ref, *refs):
    in_refs, out_ref = refs[:-1], refs[-1]
    width = in_refs[0].shape[1]
    for d, in_ref in enumerate(in_refs):
        start = pl.multiple_of(lax.rem(pos_ref[2] + d, len(in_refs)) * width, 128)
        out_ref[:, pl.ds(start, width)] = in_ref[...]


def place_blocks(pos, blocks):
    rows, width = blocks[0].shape
    shape = jax.ShapeDtypeStruct((rows, width * len(blocks)), blocks[0].dtype)
    return pl.pallas_call(
        place_kernel, out_shape=shape, in_specs=[SMEM] + [VMEM] * len(blocks), out_specs=VMEM,
        compiler_params=PARAMS, cost_estimate=cost(0, shape, shape),
    )(pos, *blocks)


def per_device(trainer_weight, owner, expert_ids, gates, hidden):
    experts = owner.shape[0]
    rows, fanout = expert_ids.shape
    hidden_width = hidden.shape[2]
    capacity = min(rows, 2 * rows * fanout // experts)
    own = trainer_weight[0, 0]
    exp_train, slice_rows, width = own.shape
    ny = lax.axis_size("y")
    groups = experts // exp_train
    slots = exp_train * capacity
    block_width = width // ny
    low = lax.axis_size("zl")
    z, c, y = lax.axis_index("zh") * low + lax.axis_index("zl"), lax.axis_index("c"), lax.axis_index("y")
    pos = jnp.stack([z, c, y, lax.axis_index("x")]).astype(jnp.int32)

    zl, cs, zh = (lax.axis_size(a) for a in ("zl", "c", "zh"))
    slot_of = owner.reshape(zl, cs, zh, exp_train).transpose(2, 0, 1, 3).reshape(experts)
    match = expert_ids[:, :, None] == slot_of[None, None, :]
    named = jnp.any(match, axis=1)
    position = jnp.cumsum(named.astype(jnp.int32), axis=0) - 1
    place = jnp.arange(experts, dtype=jnp.int32)[None, :] * capacity + position
    flat = jnp.sum(jnp.where(match, place[:, None, :], 0), axis=2).reshape(1, -1)
    pairs = hidden.reshape(-1, hidden_width)
    group_axes = Z + ("c",)

    blocks = split_blocks(pos, own, ny)
    flat = after(flat, blocks[1])
    blocks = [blocks[0]] + [shifted(blocks[d], "y", d) for d in range(1, ny)]

    outbound = dispatch(0, flat, pairs, groups, slots // 2)
    blocks[1] = after(blocks[1], outbound)
    first = lax.all_to_all(outbound, group_axes, 0, 0, tiled=True)

    chosen = jnp.arange(experts * capacity, dtype=jnp.int32)[:, None] == flat
    pair_row = jnp.arange(rows * fanout, dtype=jnp.int32) // fanout
    slot_gate = jnp.sum(jnp.where(chosen, gates.reshape(-1)[None, :], 0.0), axis=1).reshape(groups, slots)
    slot_row = jnp.sum(jnp.where(chosen, pair_row[None, :] + 1, 0), axis=1).reshape(groups, slots) - 1
    info = jnp.concatenate([slot_gate, slot_row.astype(jnp.float32)], 1)
    info = [info] + [shifted(info, "y", d) for d in range(1, ny)]

    joined = join_blocks(pos, blocks)
    weight = lax.all_gather(joined, "x")

    first_up, first_down = shifted(first, "y", 1), shifted(first, "y", -1)
    outbound = dispatch(slots // 2, flat, pairs, groups, slots // 2)
    second = lax.all_to_all(after(outbound, first, joined, *info[1:]), group_axes, 0, 0, tiled=True)
    first_opposite = shifted(first_up, "y", 1)
    second_late = after(second, first_up, first_down)
    second_up, second_down = shifted(second_late, "y", 1), shifted(second_late, "y", -1)
    second_opposite = shifted(second_down, "y", -1)
    info = after(jnp.stack(info, 1), second)
    info = lax.all_to_all(info, group_axes, 0, 0, tiled=True).reshape(groups * ny, 2 * slots)
    gate = jnp.tile(info[:, :slots], (1, 3))
    row = jnp.tile(info[:, slots:], (1, 3))

    partials = []
    own_rows, up_rows = (first, second), (first_up, second_up)
    down_rows, opposite_rows = (first_down, second_down), (first_opposite, second_opposite)
    for steps, xs in (((0, ny - 1), (own_rows, down_rows)), ((1, 2), (up_rows, opposite_rows))):
        mine, other = experts_call(steps, pos, xs, weight, gate, row, rows)
        other = shifted(other, "c", 1)
        partials.append((mine + other.astype(jnp.float32)).astype(jnp.bfloat16))
    partial = jnp.concatenate(partials, 1).reshape(-1, block_width)
    summed = lax.psum_scatter(partial, Z, scatter_dimension=0, tiled=True).reshape(ny, rows, block_width)
    final = [summed[0], shifted(summed[2], "y", -1), shifted(summed[3], "y", 2), shifted(summed[1], "y", 1)]
    return place_blocks(pos, final)


def solution(mesh):
    devices = mesh.devices.reshape(2, 2, 4, 4, 4)
    inner = Mesh(devices, AXES)
    rep, exp = ("zl", "c"), ("zh", "x", "y")
    return jax.shard_map(
        per_device,
        mesh=inner,
        in_specs=(
            P(rep, exp, None, None, None),
            P(),
            P(rep + exp, None),
            P(rep + exp, None),
            P(rep + exp, None, None),
        ),
        out_specs=P(rep + exp, None),
        check_vma=False,
    )
```

```python
import functools
import jax
import jax.numpy as jnp
from jax import lax
from jax.experimental import pallas as pl
from jax.experimental.pallas import tpu as pltpu
from jax.sharding import Mesh, PartitionSpec as P

AXES = ("zl", "c", "zh", "x", "y")
Z = ("zh", "zl")
VMEM = pl.BlockSpec(memory_space=pltpu.VMEM)
SMEM = pl.BlockSpec(memory_space=pltpu.SMEM)
PARAMS = pltpu.CompilerParams(vmem_limit_bytes=48 << 20)


def shifted(value, axis, steps):
    count = lax.axis_size(axis)
    return lax.ppermute(value, axis, [(i, (i + steps) % count) for i in range(count)])


def after(value, *others):
    return lax.optimization_barrier((value, *others))[0]


def cost(flops, *arrays):
    size = sum(a.size * a.dtype.itemsize for a in arrays)
    return pl.CostEstimate(flops=flops, bytes_accessed=size, transcendentals=0)


def split_kernel(pos_ref, w_ref, gate_ref, row_ref, *out_refs):
    count = len(out_refs)
    exp_train, depth, _ = w_ref.shape
    groups, slots = gate_ref.shape
    size, width = exp_train * depth, out_refs[0].shape[1]
    gate = gate_ref[...]
    high = gate.astype(jnp.bfloat16)
    low = (gate - high.astype(jnp.float32)).astype(jnp.bfloat16)
    for d, out_ref in enumerate(out_refs):
        start = pl.multiple_of(lax.rem(pos_ref[2] + d, count) * width, 128)
        out_ref[:size] = w_ref[:, :, pl.ds(start, width)].reshape(size, width)
        out_ref[size:] = jnp.zeros((groups, width), jnp.bfloat16)
        for part, value in enumerate((high, low, row_ref[...].astype(jnp.bfloat16))):
            out_ref[size:, part * slots:(part + 1) * slots] = value


def split_blocks(pos, own, gate, row, count):
    exp_train, depth, width = own.shape
    shape = jax.ShapeDtypeStruct((exp_train * depth + gate.shape[0], width // count), own.dtype)
    return pl.pallas_call(
        split_kernel, out_shape=[shape] * count, in_specs=[SMEM] + [VMEM] * 3, out_specs=[VMEM] * count,
        compiler_params=PARAMS, cost_estimate=cost(0, own, own),
    )(pos, own, gate, row)


def join_kernel(pos_ref, *refs):
    *in_refs, out_ref, info_ref = refs
    count = len(in_refs)
    exp_train, hidden, width = out_ref.shape
    depth = hidden // count
    size, lanes = exp_train * depth, info_ref.shape[2]
    for d, in_ref in enumerate(in_refs):
        start = pl.multiple_of(lax.rem(pos_ref[2] + count - d, count) * depth, depth)
        out_ref[:, pl.ds(start, depth), :] = in_ref[:size].reshape(exp_train, depth, width)
        info_ref[d] = in_ref[size:, :lanes]


def join_blocks(pos, blocks, exp_train, depth, lanes):
    total, width = blocks[0].shape
    count = len(blocks)
    shape = jax.ShapeDtypeStruct((exp_train, depth * count, width), blocks[0].dtype)
    info = jax.ShapeDtypeStruct((count, total - exp_train * depth, lanes), blocks[0].dtype)
    return pl.pallas_call(
        join_kernel, out_shape=[shape, info], in_specs=[SMEM] + [VMEM] * count, out_specs=[VMEM] * 2,
        compiler_params=PARAMS, cost_estimate=cost(0, shape, shape),
    )(pos, *blocks)


def dispatch_kernel(groups, whole, first_ref, flat_ref, hidden_ref, out_ref):
    slots, pairs = out_ref.shape[1], flat_ref.shape[1]
    number = lax.broadcasted_iota(jnp.int32, (groups * slots, pairs), 0)
    number = number // slots * whole + lax.rem(number, slots) + first_ref[0]
    chosen = jnp.where(number == flat_ref[...], 1.0, 0.0).astype(jnp.bfloat16)
    rows = jnp.dot(chosen, hidden_ref[...], preferred_element_type=jnp.float32).astype(jnp.bfloat16)
    out_ref[...] = rows.reshape(out_ref.shape)


def dispatch(first, slots, whole, flat, hidden, groups):
    shape = jax.ShapeDtypeStruct((groups, slots, hidden.shape[1]), hidden.dtype)
    return pl.pallas_call(
        functools.partial(dispatch_kernel, groups, whole),
        out_shape=shape, in_specs=[SMEM, VMEM, VMEM], out_specs=VMEM,
        compiler_params=PARAMS, cost_estimate=cost(2 * groups * slots * hidden.size, hidden, shape),
    )(jnp.full((1,), first, jnp.int32), flat, hidden)


def experts_kernel(counts, pos_ref, *refs):
    *x_refs, w_ref, gate_ref, row_ref, mine_ref, other_ref, p_ref = refs
    k, turn = pl.program_id(0), pl.program_id(1)
    capacity, hidden_width = x_refs[0].shape[1:]
    experts, turns = pl.num_programs(0), pl.num_programs(1)
    slots = capacity * experts
    width = w_ref.shape[3]
    planes, _, rows, _ = mine_ref.shape
    c = pos_ref[1]
    first = 0
    for part, part_counts in enumerate(counts):
        for number, count in enumerate(part_counts):
            @pl.when((turn == number) & (jnp.maximum(k, 1) - 1 == part))
            def _(number=number, sources=x_refs[first:first + count]):
                block = jnp.concatenate([ref[...].reshape(-1, hidden_width) for ref in sources], 0)
                total = jnp.dot(
                    block, w_ref[...].reshape(hidden_width, width), preferred_element_type=jnp.float32
                )
                high = total.astype(jnp.bfloat16)
                low = (total - high.astype(jnp.float32)).astype(jnp.bfloat16)
                high, low = (v.reshape(-1, capacity, width) for v in (high, low))
                for segment, value in enumerate((high, high, low)):
                    start = pl.multiple_of(segment * slots + k * capacity, capacity)
                    p_ref[number, :, pl.ds(start, capacity), :] = value
            first += count

    @pl.when(k == experts - 1)
    def _():
        number = lax.broadcasted_iota(jnp.int32, (rows, 3 * slots), 0).astype(jnp.float32)
        for plane in range(planes):
            for core, out_ref in enumerate((mine_ref, other_ref)):
                source = plane * 2 + lax.rem(c + core, 2)
                index = turn * planes * 2 + source
                mine = number == row_ref[pl.ds(index, 1), :]
                combine = jnp.where(mine, gate_ref[pl.ds(index, 1), :], 0.0).astype(jnp.bfloat16)
                mixed = jnp.dot(combine, p_ref[turn, source], preferred_element_type=jnp.float32)
                out_ref[plane, 0] = mixed.astype(out_ref.dtype)


def experts_call(pos, xs, weight, gate, row, rows):
    blocks, experts, depth, width = weight.shape
    turns = len(xs[0])
    groups, capacity, hidden_width = xs[1][0][0].shape
    mine = jax.ShapeDtypeStruct((groups // 2, turns, rows, width), jnp.float32)
    other = jax.ShapeDtypeStruct((groups // 2, turns, rows, width), jnp.bfloat16)
    arrays, specs = [], []
    for part, part_arrays in enumerate(xs):
        for turn, values in enumerate(part_arrays):
            for v in values:
                def index(k, t, part=part, turn=turn):
                    now = jnp.where(t > turn, k + 1, k) if turn < turns - 1 else k
                    return 0, jnp.clip(now, 0, 1) if part == 0 else 0, 0

                arrays.append(v)
                specs.append(pl.BlockSpec((v.shape[0], capacity, hidden_width), index))
    whole = pl.BlockSpec((groups // 2, 1, rows, width), lambda k, t: (0, jnp.where(k == experts - 1, t, 0), 0, 0))
    info = pl.BlockSpec(gate.shape, lambda k, t: (0, 0))
    flops = 2 * turns * groups * capacity * experts * hidden_width * width
    return pl.pallas_call(
        functools.partial(experts_kernel, [[len(v) for v in part_arrays] for part_arrays in xs]),
        grid=(experts, turns),
        out_shape=[mine, other],
        in_specs=[SMEM] + specs + [pl.BlockSpec((blocks, 1, depth, width), lambda k, t: (0, k, 0, 0))] + [info] * 2,
        out_specs=[whole] * 2,
        scratch_shapes=[pltpu.VMEM((turns, groups, 3 * experts * capacity, width), jnp.bfloat16)],
        compiler_params=PARAMS,
        cost_estimate=cost(flops, *arrays, weight, mine, other),
    )(pos, *arrays, weight, gate, row)


def place_kernel(pos_ref, *refs):
    in_refs, out_ref = refs[:-1], refs[-1]
    width = in_refs[0].shape[1]
    for d, in_ref in enumerate(in_refs):
        start = pl.multiple_of(lax.rem(pos_ref[2] + d, len(in_refs)) * width, 128)
        out_ref[:, pl.ds(start, width)] = in_ref[...]


def place_blocks(pos, blocks):
    rows, width = blocks[0].shape
    shape = jax.ShapeDtypeStruct((rows, width * len(blocks)), blocks[0].dtype)
    return pl.pallas_call(
        place_kernel, out_shape=shape, in_specs=[SMEM] + [VMEM] * len(blocks), out_specs=VMEM,
        compiler_params=PARAMS, cost_estimate=cost(0, shape, shape),
    )(pos, *blocks)


def per_device(trainer_weight, owner, expert_ids, gates, hidden):
    experts = owner.shape[0]
    rows, fanout = expert_ids.shape
    hidden_width = hidden.shape[2]
    capacity = min(rows, 2 * rows * fanout // experts)
    own = trainer_weight[0, 0]
    exp_train, slice_rows, width = own.shape
    ny = lax.axis_size("y")
    groups = experts // exp_train
    slots = exp_train * capacity
    block_width = width // ny
    low = lax.axis_size("zl")
    z, c, y = lax.axis_index("zh") * low + lax.axis_index("zl"), lax.axis_index("c"), lax.axis_index("y")
    pos = jnp.stack([z, c, y, lax.axis_index("x")]).astype(jnp.int32)

    zl, cs, zh = (lax.axis_size(a) for a in ("zl", "c", "zh"))
    slot_of = owner.reshape(zl, cs, zh, exp_train).transpose(2, 0, 1, 3).reshape(experts)
    match = expert_ids[:, :, None] == slot_of[None, None, :]
    named = jnp.any(match, axis=1)
    position = jnp.cumsum(named.astype(jnp.int32), axis=0) - 1
    place = jnp.arange(experts, dtype=jnp.int32)[None, :] * capacity + position
    flat = jnp.sum(jnp.where(match, place[:, None, :], 0), axis=2).reshape(1, -1)
    pairs = hidden.reshape(-1, hidden_width)
    group_axes = Z + ("c",)

    send = lambda first, count: dispatch(first * capacity, count * capacity, slots, flat, pairs, groups)
    exchange = lambda value: lax.all_to_all(value, group_axes, 0, 0, tiled=True)
    first = exchange(send(0, 2))

    chosen = jnp.arange(experts * capacity, dtype=jnp.int32)[:, None] == flat
    pair_row = jnp.arange(rows * fanout, dtype=jnp.int32) // fanout
    slot_gate = jnp.sum(jnp.where(chosen, gates.reshape(-1)[None, :], 0.0), axis=1).reshape(groups, slots)
    slot_row = jnp.sum(jnp.where(chosen, pair_row[None, :] + 1, 0), axis=1).reshape(groups, slots) - 1

    blocks = split_blocks(pos, own, slot_gate, slot_row.astype(jnp.float32), ny)
    blocks = [blocks[0]] + [shifted(blocks[d], "y", d) for d in range(1, ny)]
    blocks[1] = after(blocks[1], first)
    joined, info = join_blocks(pos, blocks, exp_train, slice_rows, 4 * slots)
    weight = lax.all_gather(joined, "x")

    first_up, first_down = shifted(first, "y", 1), shifted(first, "y", -1)
    second = exchange(after(send(2, 1), first))
    third = exchange(after(send(3, 1), first))
    middle = groups // 2
    first_opposite = [shifted(first_up[:middle], "y", 1), shifted(first_down[middle:], "y", -1)]
    second_late = after(second, first_up, first_down)
    second_up, second_down = shifted(second_late, "y", 1), shifted(second_late, "y", -1)
    third_up, third_down = shifted(third, "y", 1), shifted(third, "y", -1)
    info = lax.all_to_all(after(info, third), group_axes, 1, 1, tiled=True).astype(jnp.float32)
    high, low, row = (info[:, :, i * slots:(i + 1) * slots].reshape(ny * groups, slots) for i in range(3))
    gate = jnp.concatenate([high, low, high], 1)
    row = jnp.tile(row, (1, 3))
    second_opposite = shifted(second_up, "y", 1)
    third_opposite = shifted(after(third_down, info), "y", -1)

    xs = [
        [[first], [first_up], first_opposite, [first_down]],
        [[second], [second_up], [second_opposite], [second_down]],
        [[third], [third_up], [third_opposite], [third_down]],
    ]
    mine, other = experts_call(pos, xs, weight, gate, row, rows)
    partial = (mine + shifted(other, "c", 1).astype(jnp.float32)).astype(jnp.bfloat16)
    partial = partial.reshape(-1, block_width)
    summed = lax.psum_scatter(partial, Z, scatter_dimension=0, tiled=True).reshape(ny, rows, block_width)
    final = [summed[0]] + [shifted(summed[d], "y", -d) for d in range(1, ny)]
    return place_blocks(pos, final)


def solution(mesh):
    devices = mesh.devices.reshape(2, 2, 4, 4, 4)
    inner = Mesh(devices, AXES)
    rep, exp = ("zl", "c"), ("zh", "x", "y")
    return jax.shard_map(
        per_device,
        mesh=inner,
        in_specs=(
            P(rep, exp, None, None, None),
            P(),
            P(rep + exp, None),
            P(rep + exp, None),
            P(rep + exp, None, None),
        ),
        out_specs=P(rep + exp, None),
        check_vma=False,
    )
```

```python
import functools
import jax
import jax.numpy as jnp
from jax import lax
from jax.experimental import pallas as pl
from jax.experimental.pallas import tpu as pltpu
from jax.sharding import Mesh, PartitionSpec as P

AXES = ("zl", "c", "zh", "x", "y")
Z = ("zh", "zl")
VMEM = pl.BlockSpec(memory_space=pltpu.VMEM)
SMEM = pl.BlockSpec(memory_space=pltpu.SMEM)
PARAMS = pltpu.CompilerParams(vmem_limit_bytes=48 << 20)


def shifted(value, axis, steps):
    count = lax.axis_size(axis)
    return lax.ppermute(value, axis, [(i, (i + steps) % count) for i in range(count)])


def mirrored(value, axis, steps):
    cores, count = lax.axis_size("c"), lax.axis_size(axis)
    pairs = [(c * count + i, c * count + (i + (1 - 2 * c) * steps) % count) for c in range(cores) for i in range(count)]
    return lax.ppermute(value, ("c", axis), pairs)


def after(value, *others):
    return lax.optimization_barrier((value, *others))[0]


def cost(flops, *arrays):
    size = sum(a.size * a.dtype.itemsize for a in arrays)
    return pl.CostEstimate(flops=flops, bytes_accessed=size, transcendentals=0)


def split_kernel(pos_ref, w_ref, gate_ref, row_ref, *out_refs):
    count = len(out_refs)
    exp_train, depth, _ = w_ref.shape
    groups, slots = gate_ref.shape
    size, width = exp_train * depth, out_refs[0].shape[1]
    gate = gate_ref[...]
    high = gate.astype(jnp.bfloat16)
    low = (gate - high.astype(jnp.float32)).astype(jnp.bfloat16)
    for d, out_ref in enumerate(out_refs):
        start = pl.multiple_of(lax.rem(pos_ref[2] + d, count) * width, 128)
        out_ref[:size] = w_ref[:, :, pl.ds(start, width)].reshape(size, width)
        out_ref[size:] = jnp.zeros((groups, width), jnp.bfloat16)
        for part, value in enumerate((high, low, row_ref[...].astype(jnp.bfloat16))):
            out_ref[size:, part * slots:(part + 1) * slots] = value


def split_blocks(pos, own, gate, row, count):
    exp_train, depth, width = own.shape
    shape = jax.ShapeDtypeStruct((exp_train * depth + gate.shape[0], width // count), own.dtype)
    return pl.pallas_call(
        split_kernel, out_shape=[shape] * count, in_specs=[SMEM] + [VMEM] * 3, out_specs=[VMEM] * count,
        compiler_params=PARAMS, cost_estimate=cost(0, own, own),
    )(pos, own, gate, row)


def join_kernel(pos_ref, *refs):
    *in_refs, out_ref, info_ref = refs
    count = len(in_refs)
    exp_train, hidden, width = out_ref.shape
    depth = hidden // count
    size, lanes = exp_train * depth, info_ref.shape[2]
    for d, in_ref in enumerate(in_refs):
        start = pl.multiple_of(lax.rem(pos_ref[2] + count - d, count) * depth, depth)
        out_ref[:, pl.ds(start, depth), :] = in_ref[:size].reshape(exp_train, depth, width)
        info_ref[d] = in_ref[size:, :lanes]


def join_blocks(pos, blocks, exp_train, depth, lanes):
    total, width = blocks[0].shape
    count = len(blocks)
    shape = jax.ShapeDtypeStruct((exp_train, depth * count, width), blocks[0].dtype)
    info = jax.ShapeDtypeStruct((count, total - exp_train * depth, lanes), blocks[0].dtype)
    return pl.pallas_call(
        join_kernel, out_shape=[shape, info], in_specs=[SMEM] + [VMEM] * count, out_specs=[VMEM] * 2,
        compiler_params=PARAMS, cost_estimate=cost(0, shape, shape),
    )(pos, *blocks)


def dispatch_kernel(groups, whole, first_ref, flat_ref, hidden_ref, out_ref):
    slots, pairs = out_ref.shape[1], flat_ref.shape[1]
    number = lax.broadcasted_iota(jnp.int32, (groups * slots, pairs), 0)
    number = number // slots * whole + lax.rem(number, slots) + first_ref[0]
    chosen = jnp.where(number == flat_ref[...], 1.0, 0.0).astype(jnp.bfloat16)
    rows = jnp.dot(chosen, hidden_ref[...], preferred_element_type=jnp.float32).astype(jnp.bfloat16)
    out_ref[...] = rows.reshape(out_ref.shape)


def dispatch(first, slots, whole, flat, hidden, groups):
    shape = jax.ShapeDtypeStruct((groups, slots, hidden.shape[1]), hidden.dtype)
    return pl.pallas_call(
        functools.partial(dispatch_kernel, groups, whole),
        out_shape=shape, in_specs=[SMEM, VMEM, VMEM], out_specs=VMEM,
        compiler_params=PARAMS, cost_estimate=cost(2 * groups * slots * hidden.size, hidden, shape),
    )(jnp.full((1,), first, jnp.int32), flat, hidden)


def experts_kernel(turns, pos_ref, *refs):
    x_refs = refs[:turns], refs[turns:2 * turns]
    w_refs = refs[2 * turns:3 * turns], refs[3 * turns:4 * turns]
    gate_ref, row_ref, out_ref, x_all, w_all, p_all, sums, out_all, x_sem, w_sem, out_sem = refs[4 * turns:]
    _, _, planes, part_slots, hidden_width = x_all.shape
    rows, width = sums.shape[1:]
    experts, depth, _ = w_refs[0][0].shape
    capacity = part_slots // experts
    slots = experts * capacity
    c, x = pos_ref[1], pos_ref[3]

    def x_copy(part, turn):
        return pltpu.make_async_copy(x_refs[part][turn], x_all.at[part, turn], x_sem.at[part, turn])

    def w_copy(core, k, d):
        number = lax.rem(c + core, 2)
        start = pl.multiple_of(lax.rem(x + d * (3 - 2 * number), turns) * depth, depth)
        return pltpu.make_async_copy(
            w_refs[core][d].at[k], w_all.at[core * experts + k, pl.ds(start, depth), :], w_sem.at[core * experts + k, d]
        )

    for turn in range(turns):
        x_copy(0, turn).start()
    for core in range(2):
        for k in range(experts):
            for d in range(turns):
                w_copy(core, k, d).start()
            if (core, k) == (0, 1):
                for turn in range(turns):
                    x_copy(1, turn).start()

    number = lax.broadcasted_iota(jnp.int32, (rows, 3 * slots), 0).astype(jnp.float32)
    for core in range(2):
        group = lax.rem(c + core, 2)

        def multiply(k, _, core=core, group=group):
            if core == 0:
                for part in range(2):
                    @pl.when(k == 2 * part)
                    def _(part=part):
                        for turn in range(turns):
                            x_copy(part, turn).wait()
            for d in range(turns):
                w_copy(core, k, d).wait()
            start = pl.multiple_of(group * (part_slots // 2) + lax.rem(k, 2) * capacity, capacity)
            block = x_all[k // 2, :, :, pl.ds(start, capacity), :].reshape(turns * planes * capacity, hidden_width)
            total = jnp.dot(block, w_all[core * experts + k], preferred_element_type=jnp.float32)
            high = total.astype(jnp.bfloat16)
            low = (total - high.astype(jnp.float32)).astype(jnp.bfloat16)
            for segment, value in enumerate((high, high, low)):
                place = pl.multiple_of(segment * slots + k * capacity, capacity)
                p_all[:, pl.ds(place, capacity), :] = value.reshape(turns * planes, capacity, width)
            return 0

        lax.fori_loop(0, experts, multiply, 0)

        def combine(turn, _, core=core, group=group):
            shift = lax.rem(turn * (1 + 2 * c), turns)

            def one(plane, _):
                index = (shift * planes + plane) * 2 + group
                mine = number == row_ref[pl.ds(index, 1), :]
                weights = jnp.where(mine, gate_ref[pl.ds(index, 1), :], 0.0).astype(jnp.bfloat16)
                source = turn * planes + plane
                mixed = jnp.dot(weights, p_all[source], preferred_element_type=jnp.float32)
                if core == 0:
                    sums[source] = mixed
                else:
                    out_all[turn, plane] = (sums[source] + mixed).astype(out_all.dtype)
                return 0

            lax.fori_loop(0, planes, one, 0, unroll=2)
            if core == 1:
                pltpu.make_async_copy(out_all.at[turn], out_ref.at[:, turn], out_sem.at[turn]).start()
            return 0

        lax.fori_loop(0, turns, combine, 0)
    for turn in range(turns):
        pltpu.make_async_copy(out_all.at[turn], out_ref.at[:, turn], out_sem.at[turn]).wait()


def experts_call(pos, xs, ws, gate, row, rows):
    turns = len(ws[0])
    experts, depth, width = ws[0][0].shape
    planes, part_slots, hidden_width = xs[0][0].shape
    slots = part_slots
    out = jax.ShapeDtypeStruct((planes, turns, rows, width), jnp.bfloat16)
    hbm = pl.BlockSpec(memory_space=pl.ANY)
    arrays = [*xs[0], *xs[1], *ws[0], *ws[1]]
    flops = 2 * turns * planes * 2 * part_slots * hidden_width * width
    bf16 = lambda *shape: pltpu.VMEM(shape, jnp.bfloat16)
    return pl.pallas_call(
        functools.partial(experts_kernel, turns),
        out_shape=out,
        in_specs=[SMEM] + [hbm] * len(arrays) + [VMEM] * 2,
        out_specs=hbm,
        scratch_shapes=[
            bf16(2, turns, planes, part_slots, hidden_width),
            bf16(2 * experts, hidden_width, width),
            bf16(turns * planes, 3 * slots, width),
            pltpu.VMEM((turns * planes, rows, width), jnp.float32),
            bf16(turns, planes, rows, width),
            pltpu.SemaphoreType.DMA((2, turns)),
            pltpu.SemaphoreType.DMA((2 * experts, turns)),
            pltpu.SemaphoreType.DMA((turns,)),
        ],
        compiler_params=pltpu.CompilerParams(vmem_limit_bytes=56 << 20),
        cost_estimate=cost(flops, *arrays, out),
    )(pos, *arrays, gate, row)


def place_kernel(pos_ref, *refs):
    in_refs, out_ref = refs[:-1], refs[-1]
    width = in_refs[0].shape[1]
    for d, in_ref in enumerate(in_refs):
        turned = lax.rem(pos_ref[2] + d * (1 + 2 * pos_ref[1]), len(in_refs))
        start = pl.multiple_of(turned * width, 128)
        out_ref[:, pl.ds(start, width)] = in_ref[...]


def place_blocks(pos, blocks):
    rows, width = blocks[0].shape
    shape = jax.ShapeDtypeStruct((rows, width * len(blocks)), blocks[0].dtype)
    return pl.pallas_call(
        place_kernel, out_shape=shape, in_specs=[SMEM] + [VMEM] * len(blocks), out_specs=VMEM,
        compiler_params=PARAMS, cost_estimate=cost(0, shape, shape),
    )(pos, *blocks)


def per_device(trainer_weight, owner, expert_ids, gates, hidden):
    experts = owner.shape[0]
    rows, fanout = expert_ids.shape
    hidden_width = hidden.shape[2]
    capacity = min(rows, 2 * rows * fanout // experts)
    own = trainer_weight[0, 0]
    exp_train, slice_rows, width = own.shape
    ny = lax.axis_size("y")
    groups = experts // exp_train
    slots = exp_train * capacity
    block_width = width // ny
    low = lax.axis_size("zl")
    z, c, y = lax.axis_index("zh") * low + lax.axis_index("zl"), lax.axis_index("c"), lax.axis_index("y")
    pos = jnp.stack([z, c, y, lax.axis_index("x")]).astype(jnp.int32)

    zl, cs, zh = (lax.axis_size(a) for a in ("zl", "c", "zh"))
    slot_of = owner.reshape(zl, cs, zh, exp_train).transpose(2, 0, 1, 3).reshape(experts)
    match = expert_ids[:, :, None] == slot_of[None, None, :]
    named = jnp.any(match, axis=1)
    position = jnp.cumsum(named.astype(jnp.int32), axis=0) - 1
    place = jnp.arange(experts, dtype=jnp.int32)[None, :] * capacity + position
    flat = jnp.sum(jnp.where(match, place[:, None, :], 0), axis=2).reshape(1, -1)
    pairs = hidden.reshape(-1, hidden_width)

    planes = groups // 2
    half = exp_train // 2
    send = lambda first: dispatch(first * capacity, half * capacity, slots, flat, pairs, groups).reshape(planes, -1, hidden_width)
    first = lax.all_to_all(send(0), Z, 0, 0, tiled=True)

    chosen = jnp.arange(experts * capacity, dtype=jnp.int32)[:, None] == flat
    pair_row = jnp.arange(rows * fanout, dtype=jnp.int32) // fanout
    slot_gate = jnp.sum(jnp.where(chosen, gates.reshape(-1)[None, :], 0.0), axis=1).reshape(groups, slots)
    slot_row = jnp.sum(jnp.where(chosen, pair_row[None, :] + 1, 0), axis=1).reshape(groups, slots) - 1

    blocks = split_blocks(pos, own, slot_gate, slot_row.astype(jnp.float32), ny)
    blocks = [blocks[0]] + [shifted(blocks[d], "y", d) for d in range(1, ny)]
    blocks[1] = after(blocks[1], first)
    joined, info = join_blocks(pos, blocks, exp_train, slice_rows, 4 * slots)
    second = lax.all_to_all(after(send(half), first), Z, 0, 0, tiled=True)
    weight_up, weight_down = mirrored(joined, "x", 1), mirrored(joined, "x", -1)
    first_up, first_down = mirrored(first, "y", 1), mirrored(first, "y", -1)
    first_opposite = mirrored(first_up, "y", 1)
    weight_opposite = mirrored(weight_up, "x", 1)
    weights = [joined, weight_up, weight_opposite, weight_down]
    other_weights = [shifted(v, "c", 1) for v in weights]
    second_late = after(second, first_up, first_down)
    second_up, second_down = mirrored(second_late, "y", 1), mirrored(second_late, "y", -1)
    info = after(info, second).reshape(ny, planes, 2, 4 * slots)
    info = lax.all_to_all(info, Z, 1, 1, tiled=True).astype(jnp.float32)
    high, low, row = (info[..., i * slots:(i + 1) * slots].reshape(ny * groups, slots) for i in range(3))
    gate = jnp.concatenate([high, low, high], 1)
    row = jnp.tile(row, (1, 3))
    second_opposite = mirrored(after(second_up, info), "y", 1)

    xs = [first, first_up, first_opposite, first_down], [second, second_up, second_opposite, second_down]
    partial = experts_call(pos, xs, (weights, other_weights), gate, row, rows).reshape(-1, block_width)
    summed = lax.psum_scatter(partial, Z, scatter_dimension=0, tiled=True).reshape(ny, rows, block_width)
    final = [summed[0]] + [mirrored(summed[d], "y", -d) for d in range(1, ny)]
    return place_blocks(pos, final)


def solution(mesh):
    devices = mesh.devices.reshape(2, 2, 4, 4, 4)
    inner = Mesh(devices, AXES)
    rep, exp = ("zl", "c"), ("zh", "x", "y")
    return jax.shard_map(
        per_device,
        mesh=inner,
        in_specs=(
            P(rep, exp, None, None, None),
            P(),
            P(rep + exp, None),
            P(rep + exp, None),
            P(rep + exp, None, None),
        ),
        out_specs=P(rep + exp, None),
        check_vma=False,
    )
```

```python
import functools
import jax
import jax.numpy as jnp
from jax import lax
from jax.experimental import pallas as pl
from jax.experimental.pallas import tpu as pltpu
from jax.sharding import Mesh, PartitionSpec as P

AXES = ("zl", "c", "zh", "x", "y")
Z = ("zh", "zl")
VMEM = pl.BlockSpec(memory_space=pltpu.VMEM)
SMEM = pl.BlockSpec(memory_space=pltpu.SMEM)
BESIDE = 60_000_000_000
PARAMS = pltpu.CompilerParams(vmem_limit_bytes=48 << 20)


def shifted(value, axis, steps):
    count = lax.axis_size(axis)
    return lax.ppermute(value, axis, [(i, (i + steps) % count) for i in range(count)])


def mirrored(value, axis, steps):
    cores, count = lax.axis_size("c"), lax.axis_size(axis)
    pairs = [(c * count + i, c * count + (i + (1 - 2 * c) * steps) % count) for c in range(cores) for i in range(count)]
    return lax.ppermute(value, ("c", axis), pairs)


def after(value, *others):
    return lax.optimization_barrier((value, *others))[0]


def cost(flops, *arrays):
    size = sum(a.size * a.dtype.itemsize for a in arrays)
    return pl.CostEstimate(flops=flops, bytes_accessed=size, transcendentals=0)


def split_kernel(pos_ref, w_ref, gate_ref, row_ref, *out_refs):
    count = len(out_refs)
    exp_train, depth, _ = w_ref.shape
    groups, slots = gate_ref.shape
    size, width = exp_train * depth, out_refs[0].shape[1]
    gate = gate_ref[...]
    high = gate.astype(jnp.bfloat16)
    low = (gate - high.astype(jnp.float32)).astype(jnp.bfloat16)
    for d, out_ref in enumerate(out_refs):
        start = pl.multiple_of(lax.rem(pos_ref[2] + d, count) * width, 128)
        out_ref[:size] = w_ref[:, :, pl.ds(start, width)].reshape(size, width)
        out_ref[size:] = jnp.zeros((groups, width), jnp.bfloat16)
        for part, value in enumerate((high, low, row_ref[...].astype(jnp.bfloat16))):
            out_ref[size:, part * slots:(part + 1) * slots] = value


def split_blocks(pos, own, gate, row, count):
    exp_train, depth, width = own.shape
    shape = jax.ShapeDtypeStruct((exp_train * depth + gate.shape[0], width // count), own.dtype)
    return pl.pallas_call(
        split_kernel, out_shape=[shape] * count, in_specs=[SMEM] + [VMEM] * 3, out_specs=[VMEM] * count,
        compiler_params=PARAMS, cost_estimate=cost(0, own, own),
    )(pos, own, gate, row)


def join_kernel(pos_ref, *refs):
    *in_refs, out_ref, info_ref = refs
    count = len(in_refs)
    exp_train, hidden, width = out_ref.shape
    depth = hidden // count
    size, lanes = exp_train * depth, info_ref.shape[2]
    for d, in_ref in enumerate(in_refs):
        start = pl.multiple_of(lax.rem(pos_ref[2] + count - d, count) * depth, depth)
        out_ref[:, pl.ds(start, depth), :] = in_ref[:size].reshape(exp_train, depth, width)
        info_ref[d] = in_ref[size:, :lanes]


def join_blocks(pos, blocks, exp_train, depth, lanes):
    total, width = blocks[0].shape
    count = len(blocks)
    shape = jax.ShapeDtypeStruct((exp_train, depth * count, width), blocks[0].dtype)
    info = jax.ShapeDtypeStruct((count, total - exp_train * depth, lanes), blocks[0].dtype)
    return pl.pallas_call(
        join_kernel, out_shape=[shape, info], in_specs=[SMEM] + [VMEM] * count, out_specs=[VMEM] * 2,
        compiler_params=PARAMS, cost_estimate=cost(0, shape, shape),
    )(pos, *blocks)


def dispatch_kernel(groups, whole, first_ref, flat_ref, hidden_ref, out_ref):
    slots, pairs = out_ref.shape[1], flat_ref.shape[1]
    number = lax.broadcasted_iota(jnp.int32, (groups * slots, pairs), 0)
    number = number // slots * whole + lax.rem(number, slots) + first_ref[0]
    chosen = jnp.where(number == flat_ref[...], 1.0, 0.0).astype(jnp.bfloat16)
    rows = jnp.dot(chosen, hidden_ref[...], preferred_element_type=jnp.float32).astype(jnp.bfloat16)
    out_ref[...] = rows.reshape(out_ref.shape)


def dispatch(first, slots, whole, flat, hidden, groups, beside=0):
    shape = jax.ShapeDtypeStruct((groups, slots, hidden.shape[1]), hidden.dtype)
    return pl.pallas_call(
        functools.partial(dispatch_kernel, groups, whole),
        out_shape=shape, in_specs=[SMEM, VMEM, VMEM], out_specs=VMEM,
        compiler_params=PARAMS, cost_estimate=cost(2 * groups * slots * hidden.size + beside, hidden, shape),
    )(jnp.full((1,), first, jnp.int32), flat, hidden)


def gates_kernel(info_ref, out_ref):
    shifts, cores, planes, _ = info_ref.shape
    slots = out_ref.shape[3] // 2
    out_ref[...] = jnp.zeros_like(out_ref)
    for d in range(shifts):
        for core in range(cores):
            info = info_ref[d, core].astype(jnp.float32)
            high, low, row = (info[:, i * slots:(i + 1) * slots] for i in range(3))
            for part, place, value in ((0, 0, high), (0, 1, high), (1, 0, low), (2, 0, row), (2, 1, row)):
                out_ref[core, part, d * planes:(d + 1) * planes, place * slots:(place + 1) * slots] = value


def gates_call(info, slots):
    shifts, cores, planes, _ = info.shape
    shape = jax.ShapeDtypeStruct((cores, 3, shifts * planes, 2 * slots), jnp.float32)
    return pl.pallas_call(
        gates_kernel, out_shape=shape, in_specs=[VMEM], out_specs=VMEM,
        compiler_params=PARAMS, cost_estimate=cost(BESIDE, info, shape),
    )(info)


def experts_kernel(core, turns, pos_ref, *refs):
    x_refs = refs[:turns], refs[turns:2 * turns]
    w_ref, gate_ref, *refs = refs[2 * turns:]
    last = core == 1
    sums_ref, out_ref = refs[:2] if last else (None, refs[0])
    x_all, w_all, p_all, sums, out_all, x_sem, w_sem, sum_sem, out_sem = refs[1 + last:]
    _, _, planes, part_slots, hidden_width = x_all.shape
    blocks, experts, depth, width = w_ref.shape
    rows = sums.shape[2]
    slots = p_all.shape[1] // 2
    capacity = slots // experts
    c = pos_ref[1]
    group = lax.rem(c + core, 2)

    def x_copy(part, turn):
        source = x_refs[part][turn].at[:, pl.ds(pl.multiple_of(group * part_slots, part_slots), part_slots), :]
        return pltpu.make_async_copy(source, x_all.at[part, turn], x_sem.at[part, turn])

    def w_copy(k, d):
        return pltpu.make_async_copy(w_ref.at[d, k], w_all.at[k, pl.ds(d * depth, depth), :], w_sem.at[k, d])

    def sum_copy(turn):
        return pltpu.make_async_copy(sums_ref.at[turn], sums.at[turn], sum_sem.at[turn])

    def out_copy(turn):
        if last:
            return pltpu.make_async_copy(out_all.at[turn], out_ref.at[:, turn], out_sem.at[turn])
        return pltpu.make_async_copy(sums.at[turn], out_ref.at[turn], out_sem.at[turn])

    for k in range(experts):
        if k % 2 == 0:
            for turn in range(turns):
                x_copy(k // 2, turn).start()
        for d in range(blocks):
            w_copy(k, d).start()
    if last:
        for turn in range(turns):
            sum_copy(turn).start()

    def multiply(k, _):
        for part in range(2):
            @pl.when(k == 2 * part)
            def _(part=part):
                for turn in range(turns):
                    x_copy(part, turn).wait()
        for d in range(blocks):
            w_copy(k, d).wait()
        start = pl.multiple_of(lax.rem(k, 2) * capacity, capacity)
        block = x_all[k // 2, :, :, pl.ds(start, capacity), :].reshape(turns * planes * capacity, hidden_width)
        total = jnp.dot(block, w_all[k], preferred_element_type=jnp.float32)
        high = total.astype(jnp.bfloat16)
        low = (total - high.astype(jnp.float32)).astype(jnp.bfloat16)
        for segment, value in enumerate((high, low)):
            place = pl.multiple_of(segment * slots + k * capacity, capacity)
            p_all[:, pl.ds(place, capacity), :] = value.reshape(turns * planes, capacity, width)
        return 0

    lax.fori_loop(0, experts, multiply, 0)
    number = lax.broadcasted_iota(jnp.int32, (rows, 2 * slots), 0).astype(jnp.float32)

    def combine(turn, _):
        shift = lax.rem(turn * (1 + 2 * c), turns)
        if last:
            sum_copy(turn).wait()

        def one(plane, _):
            index = pl.ds(shift * planes + plane, 1)
            mine = number == gate_ref[group, 2, index, :]
            high, low = (jnp.where(mine, gate_ref[group, part, index, :], 0.0) for part in range(2))
            weights = jnp.concatenate([high, low], 0).astype(jnp.bfloat16)
            mixed = jnp.dot(weights, p_all[turn * planes + plane], preferred_element_type=jnp.float32)
            mixed = mixed[:rows] + mixed[rows:]
            if last:
                out_all[turn, plane] = (sums[turn, plane] + mixed).astype(out_all.dtype)
            else:
                sums[turn, plane] = mixed
            return 0

        lax.fori_loop(0, planes, one, 0, unroll=2)
        out_copy(turn).start()
        return 0

    lax.fori_loop(0, turns, combine, 0)
    for turn in range(turns):
        out_copy(turn).wait()


def experts_call(core, pos, xs, weight, gate, rows, sums=None):
    turns = len(xs[0])
    blocks, experts, depth, width = weight.shape
    planes, part_slots, hidden_width = xs[0][0].shape
    part_slots = part_slots // 2
    slots = 2 * part_slots
    total = jax.ShapeDtypeStruct((turns, planes, rows, width), jnp.float32)
    out = jax.ShapeDtypeStruct((planes, turns, rows, width), jnp.bfloat16) if core else total
    hbm = pl.BlockSpec(memory_space=pl.ANY)
    arrays = [*xs[0], *xs[1], weight]
    flops = 2 * turns * planes * slots * hidden_width * width
    bf16 = lambda *shape: pltpu.VMEM(shape, jnp.bfloat16)
    given = [] if sums is None else [sums]
    return pl.pallas_call(
        functools.partial(experts_kernel, core, turns),
        out_shape=out,
        in_specs=[SMEM] + [hbm] * len(arrays) + [VMEM] + [hbm] * len(given),
        out_specs=hbm,
        scratch_shapes=[
            bf16(2, turns, planes, part_slots, hidden_width),
            bf16(experts, blocks * depth, width),
            bf16(turns * planes, 2 * slots, width),
            pltpu.VMEM(total.shape, jnp.float32),
            bf16(turns, planes, rows, width),
            pltpu.SemaphoreType.DMA((2, turns)),
            pltpu.SemaphoreType.DMA((experts, blocks)),
            pltpu.SemaphoreType.DMA((turns,)),
            pltpu.SemaphoreType.DMA((turns,)),
        ],
        compiler_params=PARAMS,
        cost_estimate=cost(flops, *arrays, total, out),
    )(pos, *arrays, gate, *given)


def place_kernel(pos_ref, *refs):
    in_refs, out_ref = refs[:-1], refs[-1]
    width = in_refs[0].shape[1]
    for d, in_ref in enumerate(in_refs):
        turned = lax.rem(pos_ref[2] + d * (1 + 2 * pos_ref[1]), len(in_refs))
        start = pl.multiple_of(turned * width, 128)
        out_ref[:, pl.ds(start, width)] = in_ref[...]


def place_blocks(pos, blocks):
    rows, width = blocks[0].shape
    shape = jax.ShapeDtypeStruct((rows, width * len(blocks)), blocks[0].dtype)
    return pl.pallas_call(
        place_kernel, out_shape=shape, in_specs=[SMEM] + [VMEM] * len(blocks), out_specs=VMEM,
        compiler_params=PARAMS, cost_estimate=cost(0, shape, shape),
    )(pos, *blocks)


def per_device(trainer_weight, owner, expert_ids, gates, hidden):
    experts = owner.shape[0]
    rows, fanout = expert_ids.shape
    hidden_width = hidden.shape[2]
    capacity = min(rows, 2 * rows * fanout // experts)
    own = trainer_weight[0, 0]
    exp_train, slice_rows, width = own.shape
    ny = lax.axis_size("y")
    groups = experts // exp_train
    slots = exp_train * capacity
    block_width = width // ny
    low = lax.axis_size("zl")
    z, c, y = lax.axis_index("zh") * low + lax.axis_index("zl"), lax.axis_index("c"), lax.axis_index("y")
    pos = jnp.stack([z, c, y, lax.axis_index("x")]).astype(jnp.int32)

    zl, cs, zh = (lax.axis_size(a) for a in ("zl", "c", "zh"))
    slot_of = owner.reshape(zl, cs, zh, exp_train).transpose(2, 0, 1, 3).reshape(experts)
    match = expert_ids[:, :, None] == slot_of[None, None, :]
    named = jnp.any(match, axis=1)
    position = jnp.cumsum(named.astype(jnp.int32), axis=0) - 1
    place = jnp.arange(experts, dtype=jnp.int32)[None, :] * capacity + position
    flat = jnp.sum(jnp.where(match, place[:, None, :], 0), axis=2).reshape(1, -1)
    pairs = hidden.reshape(-1, hidden_width)

    planes = groups // 2
    half = exp_train // 2
    send = lambda first, flat, beside=0: dispatch(
        first * capacity, half * capacity, slots, flat, pairs, groups, beside
    ).reshape(planes, -1, hidden_width)
    first = lax.all_to_all(send(0, flat), Z, 0, 0, tiled=True)

    chosen = jnp.arange(experts * capacity, dtype=jnp.int32)[:, None] == flat
    pair_row = jnp.arange(rows * fanout, dtype=jnp.int32) // fanout
    slot_gate = jnp.sum(jnp.where(chosen, gates.reshape(-1)[None, :], 0.0), axis=1).reshape(groups, slots)
    slot_row = jnp.sum(jnp.where(chosen, pair_row[None, :] + 1, 0), axis=1).reshape(groups, slots) - 1

    by_core = lambda v: v.astype(jnp.float32).reshape(planes, 2, slots).transpose(1, 0, 2).reshape(groups, slots)
    blocks = split_blocks(pos, own, by_core(slot_gate), by_core(slot_row), ny)
    blocks = [blocks[0]] + [shifted(blocks[d], "y", d) for d in range(1, ny)]
    blocks[1] = after(blocks[1], first)
    joined, info = join_blocks(pos, blocks, exp_train, slice_rows, 4 * slots)
    weight = lax.all_gather(joined, "x")

    first_up, first_down = mirrored(first, "y", 1), mirrored(first, "y", -1)
    second = lax.all_to_all(send(half, after(flat, first, joined), BESIDE), Z, 0, 0, tiled=True)
    first_opposite = mirrored(after(first_up, first_down), "y", 1)
    second_late = after(second, first_opposite)
    second_up, second_down = mirrored(second_late, "y", 1), mirrored(second_late, "y", -1)
    info = lax.all_to_all(after(info, second).reshape(ny, 2, planes, 4 * slots), Z, 2, 2, tiled=True)
    gate = gates_call(info, slots)
    second_opposite = mirrored(after(second_up, second_down), "y", 1)
    other_weight = shifted(after(weight, second_opposite, gate), "c", 1)

    xs = [first, first_up, first_opposite, first_down], [second, second_up, second_opposite, second_down]
    sums = experts_call(0, pos, xs, weight, gate, rows)
    partial = experts_call(1, pos, xs, other_weight, gate, rows, sums).reshape(-1, block_width)
    summed = lax.psum_scatter(partial, Z, scatter_dimension=0, tiled=True).reshape(ny, rows, block_width)
    final = [summed[0]] + [mirrored(summed[d], "y", -d) for d in range(1, ny)]
    return place_blocks(pos, final)


def solution(mesh):
    devices = mesh.devices.reshape(2, 2, 4, 4, 4)
    inner = Mesh(devices, AXES)
    rep, exp = ("zl", "c"), ("zh", "x", "y")
    return jax.shard_map(
        per_device,
        mesh=inner,
        in_specs=(
            P(rep, exp, None, None, None),
            P(),
            P(rep + exp, None),
            P(rep + exp, None),
            P(rep + exp, None, None),
        ),
        out_specs=P(rep + exp, None),
        check_vma=False,
    )
```

```python
import functools
import jax
import jax.numpy as jnp
from jax import lax
from jax.experimental import pallas as pl
from jax.experimental.pallas import tpu as pltpu
from jax.sharding import Mesh, PartitionSpec as P

AXES = ("zl", "c", "zh", "x", "y")
Z = ("zh", "zl")
VMEM = pl.BlockSpec(memory_space=pltpu.VMEM)
SMEM = pl.BlockSpec(memory_space=pltpu.SMEM)
BESIDE = 60_000_000_000
PARAMS = pltpu.CompilerParams(vmem_limit_bytes=48 << 20)


def shifted(value, axis, steps):
    count = lax.axis_size(axis)
    return lax.ppermute(value, axis, [(i, (i + steps) % count) for i in range(count)])


def mirrored(value, axis, steps):
    cores, count = lax.axis_size("c"), lax.axis_size(axis)
    pairs = [(c * count + i, c * count + (i + (1 - 2 * c) * steps) % count) for c in range(cores) for i in range(count)]
    return lax.ppermute(value, ("c", axis), pairs)


def after(value, *others):
    return lax.optimization_barrier((value, *others))[0]


def cost(flops, *arrays):
    size = sum(a.size * a.dtype.itemsize for a in arrays)
    return pl.CostEstimate(flops=flops, bytes_accessed=size, transcendentals=0)


def split_kernel(pos_ref, w_ref, gate_ref, row_ref, *out_refs):
    count = len(out_refs)
    exp_train, depth, _ = w_ref.shape
    groups, slots = gate_ref.shape
    size, width = exp_train * depth, out_refs[0].shape[1]
    gate = gate_ref[...]
    high = gate.astype(jnp.bfloat16)
    low = (gate - high.astype(jnp.float32)).astype(jnp.bfloat16)
    for d, out_ref in enumerate(out_refs):
        start = pl.multiple_of(lax.rem(pos_ref[2] + d, count) * width, 128)
        out_ref[:size] = w_ref[:, :, pl.ds(start, width)].reshape(size, width)
        out_ref[size:] = jnp.zeros((groups, width), jnp.bfloat16)
        for part, value in enumerate((high, low, row_ref[...].astype(jnp.bfloat16))):
            out_ref[size:, part * slots:(part + 1) * slots] = value


def split_blocks(pos, own, gate, row, count):
    exp_train, depth, width = own.shape
    shape = jax.ShapeDtypeStruct((exp_train * depth + gate.shape[0], width // count), own.dtype)
    return pl.pallas_call(
        split_kernel, out_shape=[shape] * count, in_specs=[SMEM] + [VMEM] * 3, out_specs=[VMEM] * count,
        compiler_params=PARAMS, cost_estimate=cost(0, own, own),
    )(pos, own, gate, row)


def join_kernel(pos_ref, *refs):
    *in_refs, out_ref, info_ref = refs
    count = len(in_refs)
    exp_train, hidden, width = out_ref.shape
    depth = hidden // count
    size, lanes = exp_train * depth, info_ref.shape[2]
    for d, in_ref in enumerate(in_refs):
        start = pl.multiple_of(lax.rem(pos_ref[2] + count - d, count) * depth, depth)
        out_ref[:, pl.ds(start, depth), :] = in_ref[:size].reshape(exp_train, depth, width)
        info_ref[d] = in_ref[size:, :lanes]


def join_blocks(pos, blocks, exp_train, depth, lanes):
    total, width = blocks[0].shape
    count = len(blocks)
    shape = jax.ShapeDtypeStruct((exp_train, depth * count, width), blocks[0].dtype)
    info = jax.ShapeDtypeStruct((count, total - exp_train * depth, lanes), blocks[0].dtype)
    return pl.pallas_call(
        join_kernel, out_shape=[shape, info], in_specs=[SMEM] + [VMEM] * count, out_specs=[VMEM] * 2,
        compiler_params=PARAMS, cost_estimate=cost(BESIDE // 8, shape, shape),
    )(pos, *blocks)


def dispatch_kernel(groups, whole, first_ref, flat_ref, hidden_ref, out_ref):
    slots, pairs = out_ref.shape[1], flat_ref.shape[1]
    number = lax.broadcasted_iota(jnp.int32, (groups * slots, pairs), 0)
    number = number // slots * whole + lax.rem(number, slots) + first_ref[0]
    chosen = jnp.where(number == flat_ref[...], 1.0, 0.0).astype(jnp.bfloat16)
    rows = jnp.dot(chosen, hidden_ref[...], preferred_element_type=jnp.float32).astype(jnp.bfloat16)
    out_ref[...] = rows.reshape(out_ref.shape)


def dispatch(first, slots, whole, flat, hidden, groups, beside=0):
    shape = jax.ShapeDtypeStruct((groups, slots, hidden.shape[1]), hidden.dtype)
    return pl.pallas_call(
        functools.partial(dispatch_kernel, groups, whole),
        out_shape=shape, in_specs=[SMEM, VMEM, VMEM], out_specs=VMEM,
        compiler_params=PARAMS, cost_estimate=cost(2 * groups * slots * hidden.size + beside, hidden, shape),
    )(jnp.full((1,), first, jnp.int32), flat, hidden)


def gates_kernel(info_ref, out_ref):
    shifts, cores, planes, _ = info_ref.shape
    slots = out_ref.shape[3] // 2
    out_ref[...] = jnp.zeros_like(out_ref)
    for d in range(shifts):
        for core in range(cores):
            info = info_ref[d, core].astype(jnp.float32)
            high, low, row = (info[:, i * slots:(i + 1) * slots] for i in range(3))
            for part, place, value in ((0, 0, high), (0, 1, high), (1, 0, low), (2, 0, row), (2, 1, row)):
                out_ref[core, part, d * planes:(d + 1) * planes, place * slots:(place + 1) * slots] = value


def gates_call(info, slots):
    shifts, cores, planes, _ = info.shape
    shape = jax.ShapeDtypeStruct((cores, 3, shifts * planes, 2 * slots), jnp.float32)
    return pl.pallas_call(
        gates_kernel, out_shape=shape, in_specs=[VMEM], out_specs=VMEM,
        compiler_params=PARAMS, cost_estimate=cost(BESIDE, info, shape),
    )(info)


def experts_kernel(core, turns, pos_ref, *refs):
    x_refs = refs[:turns], refs[turns:2 * turns]
    w_ref, gate_ref, *refs = refs[2 * turns:]
    last = core == 1
    sums_ref, out_ref = refs[:2] if last else (None, refs[0])
    x_all, w_all, p_all, sums, out_all, x_sem, w_sem, sum_sem, out_sem = refs[1 + last:]
    _, _, planes, part_slots, hidden_width = x_all.shape
    blocks, experts, depth, width = w_ref.shape
    rows = sums.shape[2]
    slots = p_all.shape[1] // 2
    capacity = slots // experts
    c = pos_ref[1]
    group = lax.rem(c + core, 2)

    def x_copy(part, turn):
        source = x_refs[part][turn].at[:, pl.ds(pl.multiple_of(group * part_slots, part_slots), part_slots), :]
        return pltpu.make_async_copy(source, x_all.at[part, turn], x_sem.at[part, turn])

    def w_copy(k, d):
        return pltpu.make_async_copy(w_ref.at[d, k], w_all.at[k, pl.ds(d * depth, depth), :], w_sem.at[k, d])

    def sum_copy(turn):
        return pltpu.make_async_copy(sums_ref.at[turn], sums.at[turn], sum_sem.at[turn])

    def out_copy(turn):
        if last:
            return pltpu.make_async_copy(out_all.at[turn], out_ref.at[:, turn], out_sem.at[turn])
        return pltpu.make_async_copy(sums.at[turn], out_ref.at[turn], out_sem.at[turn])

    for k in range(experts):
        if k % 2 == 0:
            for turn in range(turns):
                x_copy(k // 2, turn).start()
        for d in range(blocks):
            w_copy(k, d).start()
    if last:
        for turn in range(turns):
            sum_copy(turn).start()

    def multiply(k, _):
        for part in range(2):
            @pl.when(k == 2 * part)
            def _(part=part):
                for turn in range(turns):
                    x_copy(part, turn).wait()
        for d in range(blocks):
            w_copy(k, d).wait()
        start = pl.multiple_of(lax.rem(k, 2) * capacity, capacity)
        block = x_all[k // 2, :, :, pl.ds(start, capacity), :].reshape(turns * planes * capacity, hidden_width)
        total = jnp.dot(block, w_all[k], preferred_element_type=jnp.float32)
        high = total.astype(jnp.bfloat16)
        low = (total - high.astype(jnp.float32)).astype(jnp.bfloat16)
        for segment, value in enumerate((high, low)):
            place = pl.multiple_of(segment * slots + k * capacity, capacity)
            p_all[:, pl.ds(place, capacity), :] = value.reshape(turns * planes, capacity, width)
        return 0

    lax.fori_loop(0, experts, multiply, 0)
    number = lax.broadcasted_iota(jnp.int32, (rows, 2 * slots), 0).astype(jnp.float32)

    def combine(turn, _):
        shift = lax.rem(turn * (1 + 2 * c), turns)
        if last:
            sum_copy(turn).wait()

        def one(plane, _):
            index = pl.ds(shift * planes + plane, 1)
            mine = number == gate_ref[group, 2, index, :]
            high, low = (jnp.where(mine, gate_ref[group, part, index, :], 0.0) for part in range(2))
            weights = jnp.concatenate([high, low], 0).astype(jnp.bfloat16)
            mixed = jnp.dot(weights, p_all[turn * planes + plane], preferred_element_type=jnp.float32)
            mixed = mixed[:rows] + mixed[rows:]
            if last:
                out_all[turn, plane] = (sums[turn, plane] + mixed).astype(out_all.dtype)
            else:
                sums[turn, plane] = mixed
            return 0

        lax.fori_loop(0, planes, one, 0, unroll=2)
        out_copy(turn).start()
        return 0

    lax.fori_loop(0, turns, combine, 0)
    for turn in range(turns):
        out_copy(turn).wait()


def experts_call(core, pos, xs, weight, gate, rows, sums=None):
    turns = len(xs[0])
    blocks, experts, depth, width = weight.shape
    planes, part_slots, hidden_width = xs[0][0].shape
    part_slots = part_slots // 2
    slots = 2 * part_slots
    total = jax.ShapeDtypeStruct((turns, planes, rows, width), jnp.float32)
    out = jax.ShapeDtypeStruct((planes, turns, rows, width), jnp.bfloat16) if core else total
    hbm = pl.BlockSpec(memory_space=pl.ANY)
    arrays = [*xs[0], *xs[1], weight]
    flops = 2 * turns * planes * slots * hidden_width * width
    bf16 = lambda *shape: pltpu.VMEM(shape, jnp.bfloat16)
    given = [] if sums is None else [sums]
    return pl.pallas_call(
        functools.partial(experts_kernel, core, turns),
        out_shape=out,
        in_specs=[SMEM] + [hbm] * len(arrays) + [VMEM] + [hbm] * len(given),
        out_specs=hbm,
        scratch_shapes=[
            bf16(2, turns, planes, part_slots, hidden_width),
            bf16(experts, blocks * depth, width),
            bf16(turns * planes, 2 * slots, width),
            pltpu.VMEM(total.shape, jnp.float32),
            bf16(turns, planes, rows, width),
            pltpu.SemaphoreType.DMA((2, turns)),
            pltpu.SemaphoreType.DMA((experts, blocks)),
            pltpu.SemaphoreType.DMA((turns,)),
            pltpu.SemaphoreType.DMA((turns,)),
        ],
        compiler_params=pltpu.CompilerParams(vmem_limit_bytes=60 << 20),
        cost_estimate=cost(flops, *arrays, total, out),
    )(pos, *arrays, gate, *given)


def place_kernel(pos_ref, *refs):
    in_refs, out_ref = refs[:-1], refs[-1]
    width = in_refs[0].shape[1]
    for d, in_ref in enumerate(in_refs):
        turned = lax.rem(pos_ref[2] + d * (1 + 2 * pos_ref[1]), len(in_refs))
        start = pl.multiple_of(turned * width, 128)
        out_ref[:, pl.ds(start, width)] = in_ref[...]


def place_blocks(pos, blocks):
    rows, width = blocks[0].shape
    shape = jax.ShapeDtypeStruct((rows, width * len(blocks)), blocks[0].dtype)
    return pl.pallas_call(
        place_kernel, out_shape=shape, in_specs=[SMEM] + [VMEM] * len(blocks), out_specs=VMEM,
        compiler_params=PARAMS, cost_estimate=cost(0, shape, shape),
    )(pos, *blocks)


def per_device(trainer_weight, owner, expert_ids, gates, hidden):
    experts = owner.shape[0]
    rows, fanout = expert_ids.shape
    hidden_width = hidden.shape[2]
    capacity = min(rows, 2 * rows * fanout // experts)
    own = trainer_weight[0, 0]
    exp_train, slice_rows, width = own.shape
    ny = lax.axis_size("y")
    groups = experts // exp_train
    slots = exp_train * capacity
    block_width = width // ny
    low = lax.axis_size("zl")
    z, c, y = lax.axis_index("zh") * low + lax.axis_index("zl"), lax.axis_index("c"), lax.axis_index("y")
    pos = jnp.stack([z, c, y, lax.axis_index("x")]).astype(jnp.int32)

    zl, cs, zh = (lax.axis_size(a) for a in ("zl", "c", "zh"))
    slot_of = owner.reshape(zl, cs, zh, exp_train).transpose(2, 0, 1, 3).reshape(experts)
    match = expert_ids[:, :, None] == slot_of[None, None, :]
    named = jnp.any(match, axis=1)
    position = jnp.cumsum(named.astype(jnp.int32), axis=0) - 1
    place = jnp.arange(experts, dtype=jnp.int32)[None, :] * capacity + position
    flat = jnp.sum(jnp.where(match, place[:, None, :], 0), axis=2).reshape(1, -1)
    pairs = hidden.reshape(-1, hidden_width)

    planes = groups // 2
    half = exp_train // 2
    send = lambda first, flat, beside=0: dispatch(
        first * capacity, half * capacity, slots, flat, pairs, groups, beside
    ).reshape(planes, -1, hidden_width)
    outbound = send(0, flat)
    first = lax.all_to_all(outbound, Z, 0, 0, tiled=True)

    chosen = jnp.arange(experts * capacity, dtype=jnp.int32)[:, None] == flat
    pair_row = jnp.arange(rows * fanout, dtype=jnp.int32) // fanout
    slot_gate = jnp.sum(jnp.where(chosen, gates.reshape(-1)[None, :], 0.0), axis=1).reshape(groups, slots)
    slot_row = jnp.sum(jnp.where(chosen, pair_row[None, :] + 1, 0), axis=1).reshape(groups, slots) - 1

    by_core = lambda v: v.astype(jnp.float32).reshape(planes, 2, slots).transpose(1, 0, 2).reshape(groups, slots)
    blocks = split_blocks(pos, own, after(by_core(slot_gate), outbound), by_core(slot_row), ny)
    blocks = [blocks[0]] + [shifted(blocks[d], "y", d) for d in range(1, ny)]
    joined, info = join_blocks(pos, blocks, exp_train, slice_rows, 4 * slots)
    weight = lax.all_gather(joined, "x")

    first_up, first_down = mirrored(first, "y", 1), mirrored(first, "y", -1)
    second = lax.all_to_all(send(half, after(flat, first, joined), BESIDE), Z, 0, 0, tiled=True)
    first_opposite = mirrored(after(first_up, first_down), "y", 1)
    second_late = after(second, first_opposite)
    second_up, second_down = mirrored(second_late, "y", 1), mirrored(second_late, "y", -1)
    info = lax.all_to_all(after(info, second).reshape(ny, 2, planes, 4 * slots), Z, 2, 2, tiled=True)
    gate = gates_call(info, slots)
    second_opposite = mirrored(after(second_up, second_down), "y", 1)
    other_weight = shifted(after(weight, second_opposite, gate), "c", 1)

    xs = [first, first_up, first_opposite, first_down], [second, second_up, second_opposite, second_down]
    sums = experts_call(0, pos, xs, weight, gate, rows)
    partial = experts_call(1, pos, xs, other_weight, gate, rows, sums).reshape(-1, block_width)
    summed = lax.psum_scatter(partial, Z, scatter_dimension=0, tiled=True).reshape(ny, rows, block_width)
    final = [summed[0]] + [mirrored(summed[d], "y", -d) for d in range(1, ny)]
    return place_blocks(pos, final)


def solution(mesh):
    devices = mesh.devices.reshape(2, 2, 4, 4, 4)
    inner = Mesh(devices, AXES)
    rep, exp = ("zl", "c"), ("zh", "x", "y")
    return jax.shard_map(
        per_device,
        mesh=inner,
        in_specs=(
            P(rep, exp, None, None, None),
            P(),
            P(rep + exp, None),
            P(rep + exp, None),
            P(rep + exp, None, None),
        ),
        out_specs=P(rep + exp, None),
        check_vma=False,
    )
```

```python
import functools
import jax
import jax.numpy as jnp
from jax import lax
from jax.experimental import pallas as pl
from jax.experimental.pallas import tpu as pltpu
from jax.sharding import Mesh, PartitionSpec as P

AXES = ("zl", "c", "zh", "x", "y")
Z = ("zh", "zl")
VMEM = pl.BlockSpec(memory_space=pltpu.VMEM)
SMEM = pl.BlockSpec(memory_space=pltpu.SMEM)
BESIDE = 60_000_000_000
PARAMS = pltpu.CompilerParams(vmem_limit_bytes=48 << 20)


def shifted(value, axis, steps):
    count = lax.axis_size(axis)
    return lax.ppermute(value, axis, [(i, (i + steps) % count) for i in range(count)])


def mirrored(value, axis, steps):
    cores, count = lax.axis_size("c"), lax.axis_size(axis)
    pairs = [(c * count + i, c * count + (i + (1 - 2 * c) * steps) % count) for c in range(cores) for i in range(count)]
    return lax.ppermute(value, ("c", axis), pairs)


def after(value, *others):
    return lax.optimization_barrier((value, *others))[0]


def cost(flops, *arrays):
    size = sum(a.size * a.dtype.itemsize for a in arrays)
    return pl.CostEstimate(flops=flops, bytes_accessed=size, transcendentals=0)


def split_kernel(pos_ref, w_ref, gate_ref, row_ref, *out_refs):
    count = len(out_refs)
    exp_train, depth, _ = w_ref.shape
    groups, slots = gate_ref.shape
    size, width = exp_train * depth, out_refs[0].shape[1]
    gate = gate_ref[...]
    high = gate.astype(jnp.bfloat16)
    low = (gate - high.astype(jnp.float32)).astype(jnp.bfloat16)
    for d, out_ref in enumerate(out_refs):
        start = pl.multiple_of(lax.rem(pos_ref[2] + d, count) * width, 128)
        out_ref[:size] = w_ref[:, :, pl.ds(start, width)].reshape(size, width)
        out_ref[size:] = jnp.zeros((groups, width), jnp.bfloat16)
        for part, value in enumerate((high, low, row_ref[...].astype(jnp.bfloat16))):
            out_ref[size:, part * slots:(part + 1) * slots] = value


def split_blocks(pos, own, gate, row, count):
    exp_train, depth, width = own.shape
    shape = jax.ShapeDtypeStruct((exp_train * depth + gate.shape[0], width // count), own.dtype)
    return pl.pallas_call(
        split_kernel, out_shape=[shape] * count, in_specs=[SMEM] + [VMEM] * 3, out_specs=[VMEM] * count,
        compiler_params=PARAMS, cost_estimate=cost(0, own, own),
    )(pos, own, gate, row)


def join_kernel(pos_ref, *refs):
    *in_refs, out_ref, info_ref = refs
    count = len(in_refs)
    exp_train, hidden, width = out_ref.shape
    depth = hidden // count
    size, lanes = exp_train * depth, info_ref.shape[2]
    for d, in_ref in enumerate(in_refs):
        start = pl.multiple_of(lax.rem(pos_ref[2] + count - d, count) * depth, depth)
        out_ref[:, pl.ds(start, depth), :] = in_ref[:size].reshape(exp_train, depth, width)
        info_ref[d] = in_ref[size:, :lanes]


def join_blocks(pos, blocks, exp_train, depth, lanes):
    total, width = blocks[0].shape
    count = len(blocks)
    shape = jax.ShapeDtypeStruct((exp_train, depth * count, width), blocks[0].dtype)
    info = jax.ShapeDtypeStruct((count, total - exp_train * depth, lanes), blocks[0].dtype)
    return pl.pallas_call(
        join_kernel, out_shape=[shape, info], in_specs=[SMEM] + [VMEM] * count, out_specs=[VMEM] * 2,
        compiler_params=PARAMS, cost_estimate=cost(BESIDE // 8, shape, shape),
    )(pos, *blocks)


def dispatch_kernel(groups, whole, first_ref, flat_ref, hidden_ref, out_ref):
    slots, pairs = out_ref.shape[1], flat_ref.shape[1]
    number = lax.broadcasted_iota(jnp.int32, (groups * slots, pairs), 0)
    number = number // slots * whole + lax.rem(number, slots) + first_ref[0]
    chosen = jnp.where(number == flat_ref[...], 1.0, 0.0).astype(jnp.bfloat16)
    rows = jnp.dot(chosen, hidden_ref[...], preferred_element_type=jnp.float32).astype(jnp.bfloat16)
    out_ref[...] = rows.reshape(out_ref.shape)


def dispatch(first, slots, whole, flat, hidden, groups, beside=0):
    shape = jax.ShapeDtypeStruct((groups, slots, hidden.shape[1]), hidden.dtype)
    return pl.pallas_call(
        functools.partial(dispatch_kernel, groups, whole),
        out_shape=shape, in_specs=[SMEM, VMEM, VMEM], out_specs=VMEM,
        compiler_params=PARAMS, cost_estimate=cost(2 * groups * slots * hidden.size + beside, hidden, shape),
    )(jnp.full((1,), first, jnp.int32), flat, hidden)


def gates_kernel(info_ref, out_ref):
    shifts, cores, planes, _ = info_ref.shape
    slots = out_ref.shape[3] // 2
    out_ref[...] = jnp.zeros_like(out_ref)
    for d in range(shifts):
        for core in range(cores):
            info = info_ref[d, core].astype(jnp.float32)
            high, low, row = (info[:, i * slots:(i + 1) * slots] for i in range(3))
            for part, place, value in ((0, 0, high), (0, 1, high), (1, 0, low), (2, 0, row), (2, 1, row)):
                out_ref[core, part, d * planes:(d + 1) * planes, place * slots:(place + 1) * slots] = value


def gates_call(info, slots):
    shifts, cores, planes, _ = info.shape
    shape = jax.ShapeDtypeStruct((cores, 3, shifts * planes, 2 * slots), jnp.float32)
    return pl.pallas_call(
        gates_kernel, out_shape=shape, in_specs=[VMEM], out_specs=VMEM,
        compiler_params=PARAMS, cost_estimate=cost(BESIDE, info, shape),
    )(info)


def experts_kernel(core, turns, pos_ref, *refs):
    x_refs = refs[:turns], refs[turns:2 * turns]
    w_ref, gate_ref, *refs = refs[2 * turns:]
    last = core == 1
    sums_ref, out_ref = refs[:2] if last else (None, refs[0])
    x_all, w_all, p_all, sums, out_all, x_sem, w_sem, sum_sem, out_sem = refs[1 + last:]
    _, _, planes, part_slots, hidden_width = x_all.shape
    blocks, experts, depth, width = w_ref.shape
    rows = sums.shape[2]
    slots = p_all.shape[1] // 2
    capacity = slots // experts
    c = pos_ref[1]
    group = lax.rem(c + core, 2)

    def x_copy(part, turn):
        source = x_refs[part][turn].at[:, pl.ds(pl.multiple_of(group * part_slots, part_slots), part_slots), :]
        return pltpu.make_async_copy(source, x_all.at[part, turn], x_sem.at[part, turn])

    def w_copy(k, d):
        return pltpu.make_async_copy(w_ref.at[d, k], w_all.at[k, pl.ds(d * depth, depth), :], w_sem.at[k, d])

    def sum_copy(turn):
        return pltpu.make_async_copy(sums_ref.at[turn], sums.at[turn], sum_sem.at[turn])

    def out_copy(turn):
        if last:
            return pltpu.make_async_copy(out_all.at[turn], out_ref.at[:, turn], out_sem.at[turn])
        return pltpu.make_async_copy(sums.at[turn], out_ref.at[turn], out_sem.at[turn])

    for k in range(experts):
        if k % 2 == 0:
            for turn in range(turns):
                x_copy(k // 2, turn).start()
        for d in range(blocks):
            w_copy(k, d).start()
    if last:
        for turn in range(turns):
            sum_copy(turn).start()

    def multiply(k, _):
        for part in range(2):
            @pl.when(k == 2 * part)
            def _(part=part):
                for turn in range(turns):
                    x_copy(part, turn).wait()
        for d in range(blocks):
            w_copy(k, d).wait()
        start = pl.multiple_of(lax.rem(k, 2) * capacity, capacity)
        block = x_all[k // 2, :, :, pl.ds(start, capacity), :].reshape(turns * planes * capacity, hidden_width)
        total = jnp.dot(block, w_all[k], preferred_element_type=jnp.float32)
        high = total.astype(jnp.bfloat16)
        low = (total - high.astype(jnp.float32)).astype(jnp.bfloat16)
        for segment, value in enumerate((high, low)):
            place = pl.multiple_of(segment * slots + k * capacity, capacity)
            p_all[:, pl.ds(place, capacity), :] = value.reshape(turns * planes, capacity, width)
        return 0

    lax.fori_loop(0, experts, multiply, 0, unroll=True)
    number = lax.broadcasted_iota(jnp.int32, (rows, 2 * slots), 0).astype(jnp.float32)

    def combine(turn, _):
        shift = lax.rem(turn * (1 + 2 * c), turns)
        if last:
            sum_copy(turn).wait()

        def one(plane, _):
            index = pl.ds(shift * planes + plane, 1)
            mine = number == gate_ref[group, 2, index, :]
            high, low = (jnp.where(mine, gate_ref[group, part, index, :], 0.0) for part in range(2))
            weights = jnp.concatenate([high, low], 0).astype(jnp.bfloat16)
            mixed = jnp.dot(weights, p_all[turn * planes + plane], preferred_element_type=jnp.float32)
            mixed = mixed[:rows] + mixed[rows:]
            if last:
                out_all[turn, plane] = (sums[turn, plane] + mixed).astype(out_all.dtype)
            else:
                sums[turn, plane] = mixed
            return 0

        lax.fori_loop(0, planes, one, 0, unroll=8)
        out_copy(turn).start()
        return 0

    lax.fori_loop(0, turns, combine, 0)
    for turn in range(turns):
        out_copy(turn).wait()


def experts_call(core, pos, xs, weight, gate, rows, sums=None):
    turns = len(xs[0])
    blocks, experts, depth, width = weight.shape
    planes, part_slots, hidden_width = xs[0][0].shape
    part_slots = part_slots // 2
    slots = 2 * part_slots
    total = jax.ShapeDtypeStruct((turns, planes, rows, width), jnp.float32)
    out = jax.ShapeDtypeStruct((planes, turns, rows, width), jnp.bfloat16) if core else total
    hbm = pl.BlockSpec(memory_space=pl.ANY)
    arrays = [*xs[0], *xs[1], weight]
    flops = 2 * turns * planes * slots * hidden_width * width
    bf16 = lambda *shape: pltpu.VMEM(shape, jnp.bfloat16)
    given = [] if sums is None else [sums]
    return pl.pallas_call(
        functools.partial(experts_kernel, core, turns),
        out_shape=out,
        in_specs=[SMEM] + [hbm] * len(arrays) + [VMEM] + [hbm] * len(given),
        out_specs=hbm,
        scratch_shapes=[
            bf16(2, turns, planes, part_slots, hidden_width),
            bf16(experts, blocks * depth, width),
            bf16(turns * planes, 2 * slots, width),
            pltpu.VMEM(total.shape, jnp.float32),
            bf16(turns, planes, rows, width),
            pltpu.SemaphoreType.DMA((2, turns)),
            pltpu.SemaphoreType.DMA((experts, blocks)),
            pltpu.SemaphoreType.DMA((turns,)),
            pltpu.SemaphoreType.DMA((turns,)),
        ],
        compiler_params=pltpu.CompilerParams(vmem_limit_bytes=60 << 20),
        cost_estimate=cost(flops, *arrays, total, out),
    )(pos, *arrays, gate, *given)


def place_kernel(pos_ref, *refs):
    in_refs, out_ref = refs[:-1], refs[-1]
    width = in_refs[0].shape[1]
    for d, in_ref in enumerate(in_refs):
        turned = lax.rem(pos_ref[2] + d * (1 + 2 * pos_ref[1]), len(in_refs))
        start = pl.multiple_of(turned * width, 128)
        out_ref[:, pl.ds(start, width)] = in_ref[...]


def place_blocks(pos, blocks):
    rows, width = blocks[0].shape
    shape = jax.ShapeDtypeStruct((rows, width * len(blocks)), blocks[0].dtype)
    return pl.pallas_call(
        place_kernel, out_shape=shape, in_specs=[SMEM] + [VMEM] * len(blocks), out_specs=VMEM,
        compiler_params=PARAMS, cost_estimate=cost(0, shape, shape),
    )(pos, *blocks)


def per_device(trainer_weight, owner, expert_ids, gates, hidden):
    experts = owner.shape[0]
    rows, fanout = expert_ids.shape
    hidden_width = hidden.shape[2]
    capacity = min(rows, 2 * rows * fanout // experts)
    own = trainer_weight[0, 0]
    exp_train, slice_rows, width = own.shape
    ny = lax.axis_size("y")
    groups = experts // exp_train
    slots = exp_train * capacity
    block_width = width // ny
    low = lax.axis_size("zl")
    z, c, y = lax.axis_index("zh") * low + lax.axis_index("zl"), lax.axis_index("c"), lax.axis_index("y")
    pos = jnp.stack([z, c, y, lax.axis_index("x")]).astype(jnp.int32)

    zl, cs, zh = (lax.axis_size(a) for a in ("zl", "c", "zh"))
    slot_of = owner.reshape(zl, cs, zh, exp_train).transpose(2, 0, 1, 3).reshape(experts)
    match = expert_ids[:, :, None] == slot_of[None, None, :]
    named = jnp.any(match, axis=1)
    position = jnp.cumsum(named.astype(jnp.int32), axis=0) - 1
    place = jnp.arange(experts, dtype=jnp.int32)[None, :] * capacity + position
    flat = jnp.sum(jnp.where(match, place[:, None, :], 0), axis=2).reshape(1, -1)
    pairs = hidden.reshape(-1, hidden_width)

    planes = groups // 2
    half = exp_train // 2
    send = lambda first, flat, beside=0: dispatch(
        first * capacity, half * capacity, slots, flat, pairs, groups, beside
    ).reshape(planes, -1, hidden_width)
    outbound = send(0, flat)
    first = lax.all_to_all(outbound, Z, 0, 0, tiled=True)

    chosen = jnp.arange(experts * capacity, dtype=jnp.int32)[:, None] == flat
    pair_row = jnp.arange(rows * fanout, dtype=jnp.int32) // fanout
    slot_gate = jnp.sum(jnp.where(chosen, gates.reshape(-1)[None, :], 0.0), axis=1).reshape(groups, slots)
    slot_row = jnp.sum(jnp.where(chosen, pair_row[None, :] + 1, 0), axis=1).reshape(groups, slots) - 1

    by_core = lambda v: v.astype(jnp.float32).reshape(planes, 2, slots).transpose(1, 0, 2).reshape(groups, slots)
    blocks = split_blocks(pos, own, after(by_core(slot_gate), outbound), by_core(slot_row), ny)
    blocks = [blocks[0]] + [shifted(blocks[d], "y", d) for d in range(1, ny)]
    joined, info = join_blocks(pos, blocks, exp_train, slice_rows, 4 * slots)
    weight = lax.all_gather(joined, "x")

    first_up, first_down = mirrored(first, "y", 1), mirrored(first, "y", -1)
    second = lax.all_to_all(send(half, after(flat, first, joined), BESIDE), Z, 0, 0, tiled=True)
    first_opposite = mirrored(after(first_up, first_down), "y", 1)
    second_late = after(second, first_opposite)
    second_up, second_down = mirrored(second_late, "y", 1), mirrored(second_late, "y", -1)
    info = lax.all_to_all(after(info, second).reshape(ny, 2, planes, 4 * slots), Z, 2, 2, tiled=True)
    gate = gates_call(info, slots)
    second_opposite = mirrored(after(second_up, second_down), "y", 1)
    other_weight = shifted(after(weight, second_opposite, gate), "c", 1)

    xs = [first, first_up, first_opposite, first_down], [second, second_up, second_opposite, second_down]
    sums = experts_call(0, pos, xs, weight, gate, rows)
    partial = experts_call(1, pos, xs, other_weight, gate, rows, sums).reshape(-1, block_width)
    summed = lax.psum_scatter(partial, Z, scatter_dimension=0, tiled=True).reshape(ny, rows, block_width)
    final = [summed[0]] + [mirrored(summed[d], "y", -d) for d in range(1, ny)]
    return place_blocks(pos, final)


def solution(mesh):
    devices = mesh.devices.reshape(2, 2, 4, 4, 4)
    inner = Mesh(devices, AXES)
    rep, exp = ("zl", "c"), ("zh", "x", "y")
    return jax.shard_map(
        per_device,
        mesh=inner,
        in_specs=(
            P(rep, exp, None, None, None),
            P(),
            P(rep + exp, None),
            P(rep + exp, None),
            P(rep + exp, None, None),
        ),
        out_specs=P(rep + exp, None),
        check_vma=False,
    )
```

```python
import functools
import jax
import jax.numpy as jnp
from jax import lax
from jax.experimental import pallas as pl
from jax.experimental.pallas import tpu as pltpu
from jax.sharding import Mesh, PartitionSpec as P

AXES = ("zl", "c", "zh", "x", "y")
Z = ("zh", "zl")
VMEM = pl.BlockSpec(memory_space=pltpu.VMEM)
SMEM = pl.BlockSpec(memory_space=pltpu.SMEM)
BESIDE = 60_000_000_000
PARAMS = pltpu.CompilerParams(vmem_limit_bytes=48 << 20)


def shifted(value, axis, steps):
    count = lax.axis_size(axis)
    return lax.ppermute(value, axis, [(i, (i + steps) % count) for i in range(count)])


def mirrored(value, axis, steps):
    cores, count = lax.axis_size("c"), lax.axis_size(axis)
    pairs = [(c * count + i, c * count + (i + (1 - 2 * c) * steps) % count) for c in range(cores) for i in range(count)]
    return lax.ppermute(value, ("c", axis), pairs)


def after(value, *others):
    return lax.optimization_barrier((value, *others))[0]


def cost(flops, *arrays):
    size = sum(a.size * a.dtype.itemsize for a in arrays)
    return pl.CostEstimate(flops=flops, bytes_accessed=size, transcendentals=0)


def split_kernel(pos_ref, w_ref, gate_ref, row_ref, *out_refs):
    count = len(out_refs)
    exp_train, depth, _ = w_ref.shape
    groups, slots = gate_ref.shape
    size, width = exp_train * depth, out_refs[0].shape[1]
    gate = gate_ref[...]
    high = gate.astype(jnp.bfloat16)
    low = (gate - high.astype(jnp.float32)).astype(jnp.bfloat16)
    for d, out_ref in enumerate(out_refs):
        start = pl.multiple_of(lax.rem(pos_ref[2] + d, count) * width, 128)
        out_ref[:size] = w_ref[:, :, pl.ds(start, width)].reshape(size, width)
        out_ref[size:] = jnp.zeros((groups, width), jnp.bfloat16)
        for part, value in enumerate((high, low, row_ref[...].astype(jnp.bfloat16))):
            out_ref[size:, part * slots:(part + 1) * slots] = value


def split_blocks(pos, own, gate, row, count):
    exp_train, depth, width = own.shape
    shape = jax.ShapeDtypeStruct((exp_train * depth + gate.shape[0], width // count), own.dtype)
    return pl.pallas_call(
        split_kernel, out_shape=[shape] * count, in_specs=[SMEM] + [VMEM] * 3, out_specs=[VMEM] * count,
        compiler_params=PARAMS, cost_estimate=cost(0, own, own),
    )(pos, own, gate, row)


def join_kernel(pos_ref, *refs):
    *in_refs, out_ref, info_ref = refs
    count = len(in_refs)
    exp_train, hidden, width = out_ref.shape
    depth = hidden // count
    size, lanes = exp_train * depth, info_ref.shape[2]
    for d, in_ref in enumerate(in_refs):
        start = pl.multiple_of(lax.rem(pos_ref[2] + count - d, count) * depth, depth)
        out_ref[:, pl.ds(start, depth), :] = in_ref[:size].reshape(exp_train, depth, width)
        info_ref[d] = in_ref[size:, :lanes]


def join_blocks(pos, blocks, exp_train, depth, lanes):
    total, width = blocks[0].shape
    count = len(blocks)
    shape = jax.ShapeDtypeStruct((exp_train, depth * count, width), blocks[0].dtype)
    info = jax.ShapeDtypeStruct((count, total - exp_train * depth, lanes), blocks[0].dtype)
    return pl.pallas_call(
        join_kernel, out_shape=[shape, info], in_specs=[SMEM] + [VMEM] * count, out_specs=[VMEM] * 2,
        compiler_params=PARAMS, cost_estimate=cost(BESIDE // 8, shape, shape),
    )(pos, *blocks)


def dispatch_kernel(groups, whole, first_ref, flat_ref, hidden_ref, out_ref):
    slots, pairs = out_ref.shape[1], flat_ref.shape[1]
    number = lax.broadcasted_iota(jnp.int32, (groups * slots, pairs), 0)
    number = number // slots * whole + lax.rem(number, slots) + first_ref[0]
    chosen = jnp.where(number == flat_ref[...], 1.0, 0.0).astype(jnp.bfloat16)
    rows = jnp.dot(chosen, hidden_ref[...], preferred_element_type=jnp.float32).astype(jnp.bfloat16)
    out_ref[...] = rows.reshape(out_ref.shape)


def dispatch(first, slots, whole, flat, hidden, groups, beside=0):
    shape = jax.ShapeDtypeStruct((groups, slots, hidden.shape[1]), hidden.dtype)
    return pl.pallas_call(
        functools.partial(dispatch_kernel, groups, whole),
        out_shape=shape, in_specs=[SMEM, VMEM, VMEM], out_specs=VMEM,
        compiler_params=PARAMS, cost_estimate=cost(2 * groups * slots * hidden.size + beside, hidden, shape),
    )(jnp.full((1,), first, jnp.int32), flat, hidden)


def gates_kernel(info_ref, out_ref):
    shifts, cores, planes, _ = info_ref.shape
    slots = out_ref.shape[3] // 2
    out_ref[...] = jnp.zeros_like(out_ref)
    for d in range(shifts):
        for core in range(cores):
            info = info_ref[d, core].astype(jnp.float32)
            high, low, row = (info[:, i * slots:(i + 1) * slots] for i in range(3))
            for part, place, value in ((0, 0, high), (0, 1, high), (1, 0, low), (2, 0, row), (2, 1, row)):
                out_ref[core, part, d * planes:(d + 1) * planes, place * slots:(place + 1) * slots] = value


def gates_call(info, slots):
    shifts, cores, planes, _ = info.shape
    shape = jax.ShapeDtypeStruct((cores, 3, shifts * planes, 2 * slots), jnp.float32)
    return pl.pallas_call(
        gates_kernel, out_shape=shape, in_specs=[VMEM], out_specs=VMEM,
        compiler_params=PARAMS, cost_estimate=cost(BESIDE, info, shape),
    )(info)


def experts_kernel(core, shifts, given, early, pos_ref, *refs):
    turns = len(shifts)
    last = core == 1
    operands = []
    for count in (turns, len(early)):
        if count:
            operands.append((refs[:count], refs[count:2 * count], refs[2 * count]))
            refs = refs[2 * count + 1:]
    gate_ref, *refs = refs
    given_refs, out_ref = refs[:len(given)], refs[2 * len(given)]
    x_all, w_all, p_all, sums, out_all, x_sem, w_sem, sum_sem, out_sem = refs[1 + 2 * len(given):]
    _, _, planes, part_slots, hidden_width = x_all.shape
    blocks, experts, depth, width = operands[0][2].shape
    rows = sums.shape[2]
    slots = p_all.shape[1] // 2
    capacity = slots // experts
    c = pos_ref[1]
    number = lax.broadcasted_iota(jnp.int32, (rows, 2 * slots), 0).astype(jnp.float32)

    def stage(place, group, count):
        *x_refs, w_ref = operands[place]
        first, base = place * turns, place * experts

        def x_copy(part, turn):
            source = x_refs[part][turn].at[:, pl.ds(pl.multiple_of(group * part_slots, part_slots), part_slots), :]
            return pltpu.make_async_copy(source, x_all.at[part, first + turn], x_sem.at[part, first + turn])

        def w_copy(k, d):
            target = w_all.at[base + k, pl.ds(d * depth, depth), :]
            return pltpu.make_async_copy(w_ref.at[d, k], target, w_sem.at[base + k, d])

        def start():
            for k in range(experts):
                if k % 2 == 0:
                    for turn in range(count):
                        x_copy(k // 2, turn).start()
                for d in range(blocks):
                    w_copy(k, d).start()

        def multiply():
            for k in range(experts):
                if k % 2 == 0:
                    for turn in range(count):
                        x_copy(k // 2, turn).wait()
                for d in range(blocks):
                    w_copy(k, d).wait()
                held = k % 2 * capacity
                block = x_all[k // 2, first:first + count, :, held:held + capacity, :].reshape(-1, hidden_width)
                total = jnp.dot(block, w_all[base + k], preferred_element_type=jnp.float32)
                high = total.astype(jnp.bfloat16)
                low = (total - high.astype(jnp.float32)).astype(jnp.bfloat16)
                for segment, value in enumerate((high, low)):
                    start = segment * slots + k * capacity
                    p_all[:count * planes, start:start + capacity, :] = value.reshape(-1, capacity, width)

        def mixed(shift, source, plane):
            index = pl.ds(lax.rem(shift * (1 + 2 * c), 4) * planes + plane, 1)
            mine = number == gate_ref[group, 2, index, :]
            high, low = (jnp.where(mine, gate_ref[group, part, index, :], 0.0) for part in range(2))
            weights = jnp.concatenate([high, low], 0).astype(jnp.bfloat16)
            value = jnp.dot(weights, p_all[source], preferred_element_type=jnp.float32)
            return value[:rows] + value[rows:]

        return start, multiply, mixed

    def sum_copy(turn):
        source = given_refs[0].at[given[0].index(shifts[turn])]
        return pltpu.make_async_copy(source, sums.at[turn], sum_sem.at[turn])

    def out_copy(turn):
        if last:
            return pltpu.make_async_copy(out_all.at[turn], out_ref.at[:, turn], out_sem.at[turn])
        return pltpu.make_async_copy(sums.at[turn], out_ref.at[turn], out_sem.at[turn])

    start, multiply, mixed = stage(0, lax.rem(c + core, 2), turns)
    added = [turn for turn in range(turns) if given and shifts[turn] in given[0]]
    if early:
        start_early, multiply_early, mixed_early = stage(1, c, len(early))
        start_early()
    start()
    for turn in added:
        sum_copy(turn).start()
    if early:
        multiply_early()
        for place, shift in enumerate(early):
            turn = shifts.index(shift)

            def one(plane, _, place=place, shift=shift, turn=turn):
                sums[turn, plane] = mixed_early(shift, place * planes + plane, plane)
                return 0

            lax.fori_loop(0, planes, one, 0, unroll=8)
    multiply()
    for turn in added:
        sum_copy(turn).wait()

    def combine(turn, _):
        shift = shifts[0] + turn + turn // 2 * (shifts[-1] - shifts[0] + 1 - turns)

        def one(plane, _):
            value = mixed(shift, turn * planes + plane, plane)
            if last:
                out_all[turn, plane] = (sums[turn, plane] + value).astype(out_all.dtype)
            else:
                sums[turn, plane] = value
            return 0

        lax.fori_loop(0, planes, one, 0, unroll=8)
        out_copy(turn).start()
        return 0

    lax.fori_loop(0, turns, combine, 0)
    for turn in range(turns):
        out_copy(turn).wait()


def wait_for_kernel(in_ref, sums_ref, out_ref):
    out_ref[...] = in_ref[0]


def wait_for(value, sums):
    lanes = value.shape[2] // 8
    return pl.pallas_call(
        wait_for_kernel, grid=(1,), out_shape=jax.ShapeDtypeStruct((16, lanes), value.dtype),
        in_specs=[pl.BlockSpec((1, 16, lanes), lambda i: (0, 0, 0)), pl.BlockSpec(memory_space=pl.ANY)], out_specs=pl.BlockSpec((16, lanes), lambda i: (0, 0)),
        cost_estimate=pl.CostEstimate(flops=BESIDE, bytes_accessed=8192, transcendentals=0),
    )(value, sums)


def experts_call(core, shifts, pos, xs, weight, gate, rows, given=(), early=(), early_weight=None):
    turns = len(shifts)
    blocks, experts, depth, width = weight.shape
    planes, part_slots, hidden_width = xs[0][0].shape
    part_slots = part_slots // 2
    slots = 2 * part_slots
    total = jax.ShapeDtypeStruct((turns, planes, rows, width), jnp.float32)
    out = jax.ShapeDtypeStruct((planes, turns, rows, width), jnp.bfloat16) if core else total
    hbm = pl.BlockSpec(memory_space=pl.ANY)
    arrays = [xs[part][shift] for part in range(2) for shift in shifts] + [weight]
    if early:
        arrays += [xs[part][shift] for part in range(2) for shift in early] + [early_weight]
    stages = 1 + bool(early)
    flops = 2 * turns * planes * slots * hidden_width * width
    bf16 = lambda *shape: pltpu.VMEM(shape, jnp.bfloat16)
    return pl.pallas_call(
        functools.partial(experts_kernel, core, shifts, [v[0] for v in given], early),
        out_shape=out,
        in_specs=[SMEM] + [hbm] * len(arrays) + [VMEM] + [hbm] * (2 * len(given)),
        out_specs=hbm,
        scratch_shapes=[
            bf16(2, turns + len(early), planes, part_slots, hidden_width),
            bf16(stages * experts, blocks * depth, width),
            bf16(turns * planes, 2 * slots, width),
            pltpu.VMEM(total.shape, jnp.float32),
            bf16(turns, planes, rows, width),
            pltpu.SemaphoreType.DMA((2, turns + len(early))),
            pltpu.SemaphoreType.DMA((stages * experts, blocks)),
            pltpu.SemaphoreType.DMA((turns,)),
            pltpu.SemaphoreType.DMA((turns,)),
        ],
        compiler_params=pltpu.CompilerParams(vmem_limit_bytes=60 << 20),
        cost_estimate=cost(flops, *arrays, total, out) if core else cost(BESIDE, gate),
    )(pos, *arrays, gate, *[v[1] for v in given], *[v[2] for v in given])


def place_kernel(pos_ref, *refs):
    in_refs, out_ref = refs[:-1], refs[-1]
    width = in_refs[0].shape[1]
    for d, in_ref in enumerate(in_refs):
        turned = lax.rem(pos_ref[2] + d * (1 + 2 * pos_ref[1]), len(in_refs))
        start = pl.multiple_of(turned * width, 128)
        out_ref[:, pl.ds(start, width)] = in_ref[...]


def place_blocks(pos, blocks):
    rows, width = blocks[0].shape
    shape = jax.ShapeDtypeStruct((rows, width * len(blocks)), blocks[0].dtype)
    return pl.pallas_call(
        place_kernel, out_shape=shape, in_specs=[SMEM] + [VMEM] * len(blocks), out_specs=VMEM,
        compiler_params=PARAMS, cost_estimate=cost(0, shape, shape),
    )(pos, *blocks)


def per_device(trainer_weight, owner, expert_ids, gates, hidden):
    experts = owner.shape[0]
    rows, fanout = expert_ids.shape
    hidden_width = hidden.shape[2]
    capacity = min(rows, 2 * rows * fanout // experts)
    own = trainer_weight[0, 0]
    exp_train, slice_rows, width = own.shape
    ny = lax.axis_size("y")
    groups = experts // exp_train
    slots = exp_train * capacity
    block_width = width // ny
    low = lax.axis_size("zl")
    z, c, y = lax.axis_index("zh") * low + lax.axis_index("zl"), lax.axis_index("c"), lax.axis_index("y")
    pos = jnp.stack([z, c, y, lax.axis_index("x")]).astype(jnp.int32)

    zl, cs, zh = (lax.axis_size(a) for a in ("zl", "c", "zh"))
    slot_of = owner.reshape(zl, cs, zh, exp_train).transpose(2, 0, 1, 3).reshape(experts)
    match = expert_ids[:, :, None] == slot_of[None, None, :]
    named = jnp.any(match, axis=1)
    position = jnp.cumsum(named.astype(jnp.int32), axis=0) - 1
    place = jnp.arange(experts, dtype=jnp.int32)[None, :] * capacity + position
    flat = jnp.sum(jnp.where(match, place[:, None, :], 0), axis=2).reshape(1, -1)
    pairs = hidden.reshape(-1, hidden_width)

    planes = groups // 2
    half = exp_train // 2
    send = lambda first, flat, beside=0: dispatch(
        first * capacity, half * capacity, slots, flat, pairs, groups, beside
    ).reshape(planes, -1, hidden_width)
    outbound = send(0, flat)
    first = lax.all_to_all(outbound, Z, 0, 0, tiled=True)

    chosen = jnp.arange(experts * capacity, dtype=jnp.int32)[:, None] == flat
    pair_row = jnp.arange(rows * fanout, dtype=jnp.int32) // fanout
    slot_gate = jnp.sum(jnp.where(chosen, gates.reshape(-1)[None, :], 0.0), axis=1).reshape(groups, slots)
    slot_row = jnp.sum(jnp.where(chosen, pair_row[None, :] + 1, 0), axis=1).reshape(groups, slots) - 1

    by_core = lambda v: v.astype(jnp.float32).reshape(planes, 2, slots).transpose(1, 0, 2).reshape(groups, slots)
    blocks = split_blocks(pos, own, after(by_core(slot_gate), outbound), by_core(slot_row), ny)
    blocks = [blocks[0]] + [shifted(blocks[d], "y", d) for d in range(1, ny)]
    joined, info = join_blocks(pos, blocks, exp_train, slice_rows, 4 * slots)
    weight = lax.all_gather(joined, "x")

    first_up, first_down = mirrored(first, "y", 1), mirrored(first, "y", -1)
    second = lax.all_to_all(send(half, after(flat, first, joined), BESIDE), Z, 0, 0, tiled=True)
    first_opposite = mirrored(after(first_up, first_down), "y", 1)
    second_late = after(second, first_opposite)
    second_up, second_down = mirrored(second_late, "y", 1), mirrored(second_late, "y", -1)
    info = lax.all_to_all(after(info, second).reshape(ny, 2, planes, 4 * slots), Z, 2, 2, tiled=True)
    gate = gates_call(after(info, second_up, second_down), slots)
    second_opposite = mirrored(after(second_up, second_down), "y", 1)
    other_weight = shifted(after(weight, gate), "c", 1)

    xs = [first, first_up, first_opposite, first_down], [second, second_up, second_opposite, second_down]
    near, every = (0, 1, 3), (0, 1, 2, 3)
    sums = (near, experts_call(0, near, pos, xs, weight, gate, rows))
    sums = (near, sums[1], wait_for(second_opposite, sums[1]))
    partial = experts_call(1, every, pos, xs, other_weight, gate, rows, (sums,), (2,), weight)
    partial = partial.reshape(-1, block_width)
    summed = lax.psum_scatter(partial, Z, scatter_dimension=0, tiled=True).reshape(ny, rows, block_width)
    final = [summed[0]] + [mirrored(summed[d], "y", -d) for d in range(1, ny)]
    return place_blocks(pos, final)


def solution(mesh):
    devices = mesh.devices.reshape(2, 2, 4, 4, 4)
    inner = Mesh(devices, AXES)
    rep, exp = ("zl", "c"), ("zh", "x", "y")
    return jax.shard_map(
        per_device,
        mesh=inner,
        in_specs=(
            P(rep, exp, None, None, None),
            P(),
            P(rep + exp, None),
            P(rep + exp, None),
            P(rep + exp, None, None),
        ),
        out_specs=P(rep + exp, None),
        check_vma=False,
    )
```

```python
import functools
import jax
import jax.numpy as jnp
from jax import lax
from jax.experimental import pallas as pl
from jax.experimental.pallas import tpu as pltpu
from jax.sharding import Mesh, PartitionSpec as P

AXES = ("zl", "c", "zh", "x", "y")
Z = ("zh", "zl")
VMEM = pl.BlockSpec(memory_space=pltpu.VMEM)
SMEM = pl.BlockSpec(memory_space=pltpu.SMEM)
BESIDE = 60_000_000_000
PARAMS = pltpu.CompilerParams(vmem_limit_bytes=48 << 20)


def shifted(value, axis, steps):
    count = lax.axis_size(axis)
    return lax.ppermute(value, axis, [(i, (i + steps) % count) for i in range(count)])


def mirrored(value, axis, steps):
    cores, count = lax.axis_size("c"), lax.axis_size(axis)
    pairs = [(c * count + i, c * count + (i + (1 - 2 * c) * steps) % count) for c in range(cores) for i in range(count)]
    return lax.ppermute(value, ("c", axis), pairs)


def after(value, *others):
    return lax.optimization_barrier((value, *others))[0]


def cost(flops, *arrays):
    size = sum(a.size * a.dtype.itemsize for a in arrays)
    return pl.CostEstimate(flops=flops, bytes_accessed=size, transcendentals=0)


def split_kernel(pos_ref, w_ref, gate_ref, row_ref, *out_refs):
    count = len(out_refs)
    exp_train, depth, _ = w_ref.shape
    groups, slots = gate_ref.shape
    size, width = exp_train * depth, out_refs[0].shape[1]
    gate = gate_ref[...]
    high = gate.astype(jnp.bfloat16)
    low = (gate - high.astype(jnp.float32)).astype(jnp.bfloat16)
    for d, out_ref in enumerate(out_refs):
        start = pl.multiple_of(lax.rem(pos_ref[2] + d, count) * width, 128)
        out_ref[:size] = w_ref[:, :, pl.ds(start, width)].reshape(size, width)
        out_ref[size:] = jnp.zeros((groups, width), jnp.bfloat16)
        for part, value in enumerate((high, low, row_ref[...].astype(jnp.bfloat16))):
            out_ref[size:, part * slots:(part + 1) * slots] = value


def split_blocks(pos, own, gate, row, count):
    exp_train, depth, width = own.shape
    shape = jax.ShapeDtypeStruct((exp_train * depth + gate.shape[0], width // count), own.dtype)
    return pl.pallas_call(
        split_kernel, out_shape=[shape] * count, in_specs=[SMEM] + [VMEM] * 3, out_specs=[VMEM] * count,
        compiler_params=PARAMS, cost_estimate=cost(0, own, own),
    )(pos, own, gate, row)


def join_kernel(pos_ref, *refs):
    *in_refs, out_ref, info_ref = refs
    count = len(in_refs)
    exp_train, hidden, width = out_ref.shape
    depth = hidden // count
    size, lanes = exp_train * depth, info_ref.shape[2]
    for d, in_ref in enumerate(in_refs):
        start = pl.multiple_of(lax.rem(pos_ref[2] + count - d, count) * depth, depth)
        out_ref[:, pl.ds(start, depth), :] = in_ref[:size].reshape(exp_train, depth, width)
        info_ref[d] = in_ref[size:, :lanes]


def join_blocks(pos, blocks, exp_train, depth, lanes):
    total, width = blocks[0].shape
    count = len(blocks)
    shape = jax.ShapeDtypeStruct((exp_train, depth * count, width), blocks[0].dtype)
    info = jax.ShapeDtypeStruct((count, total - exp_train * depth, lanes), blocks[0].dtype)
    return pl.pallas_call(
        join_kernel, out_shape=[shape, info], in_specs=[SMEM] + [VMEM] * count, out_specs=[VMEM] * 2,
        compiler_params=PARAMS, cost_estimate=cost(BESIDE // 8, shape, shape),
    )(pos, *blocks)


def dispatch_kernel(groups, whole, first_ref, flat_ref, hidden_ref, out_ref):
    slots, pairs = out_ref.shape[1], flat_ref.shape[1]
    number = lax.broadcasted_iota(jnp.int32, (groups * slots, pairs), 0)
    number = number // slots * whole + lax.rem(number, slots) + first_ref[0]
    chosen = jnp.where(number == flat_ref[...], 1.0, 0.0).astype(jnp.bfloat16)
    rows = jnp.dot(chosen, hidden_ref[...], preferred_element_type=jnp.float32).astype(jnp.bfloat16)
    out_ref[...] = rows.reshape(out_ref.shape)


def dispatch(first, slots, whole, flat, hidden, groups, beside=0):
    shape = jax.ShapeDtypeStruct((groups, slots, hidden.shape[1]), hidden.dtype)
    return pl.pallas_call(
        functools.partial(dispatch_kernel, groups, whole),
        out_shape=shape, in_specs=[SMEM, VMEM, VMEM], out_specs=VMEM,
        compiler_params=PARAMS, cost_estimate=cost(2 * groups * slots * hidden.size + beside, hidden, shape),
    )(jnp.full((1,), first, jnp.int32), flat, hidden)


def gates_kernel(info_ref, out_ref):
    shifts, cores, planes, _ = info_ref.shape
    slots = out_ref.shape[3] // 2
    out_ref[...] = jnp.zeros_like(out_ref)
    for d in range(shifts):
        for core in range(cores):
            info = info_ref[d, core].astype(jnp.float32)
            high, low, row = (info[:, i * slots:(i + 1) * slots] for i in range(3))
            for part, place, value in ((0, 0, high), (0, 1, high), (1, 0, low), (2, 0, row), (2, 1, row)):
                out_ref[core, part, d * planes:(d + 1) * planes, place * slots:(place + 1) * slots] = value


def gates_call(info, slots):
    shifts, cores, planes, _ = info.shape
    shape = jax.ShapeDtypeStruct((cores, 3, shifts * planes, 2 * slots), jnp.float32)
    return pl.pallas_call(
        gates_kernel, out_shape=shape, in_specs=[VMEM], out_specs=VMEM,
        compiler_params=PARAMS, cost_estimate=cost(BESIDE, info, shape),
    )(info)


def experts_kernel(core, shifts, given, early, pos_ref, *refs):
    turns = len(shifts)
    last = core == 1
    operands = []
    for count in (turns, len(early)):
        if count:
            operands.append((refs[:count], refs[count:2 * count], refs[2 * count]))
            refs = refs[2 * count + 1:]
    gate_ref, *refs = refs
    given_refs, out_ref = refs[:len(given)], refs[2 * len(given)]
    x_all, w_all, p_all, sums, out_all, x_sem, w_sem, sum_sem, out_sem = refs[1 + 2 * len(given):]
    _, _, planes, part_slots, hidden_width = x_all.shape
    blocks, experts, depth, width = operands[0][2].shape
    rows = sums.shape[2]
    slots = p_all.shape[1] // 2
    capacity = slots // experts
    c = pos_ref[1]
    number = lax.broadcasted_iota(jnp.int32, (rows, 2 * slots), 0).astype(jnp.float32)

    def stage(place, group, count):
        *x_refs, w_ref = operands[place]
        first, base = place * turns, place * experts

        def x_copy(part, turn):
            source = x_refs[part][turn].at[:, pl.ds(pl.multiple_of(group * part_slots, part_slots), part_slots), :]
            return pltpu.make_async_copy(source, x_all.at[part, first + turn], x_sem.at[part, first + turn])

        def w_copy(k, d):
            target = w_all.at[base + k, pl.ds(d * depth, depth), :]
            return pltpu.make_async_copy(w_ref.at[d, k], target, w_sem.at[base + k, d])

        def start():
            for k in range(experts):
                if k % 2 == 0:
                    for turn in range(count):
                        x_copy(k // 2, turn).start()
                for d in range(blocks):
                    w_copy(k, d).start()

        def multiply():
            for k in range(experts):
                if k % 2 == 0:
                    for turn in range(count):
                        x_copy(k // 2, turn).wait()
                for d in range(blocks):
                    w_copy(k, d).wait()
                held = k % 2 * capacity
                block = x_all[k // 2, first:first + count, :, held:held + capacity, :].reshape(-1, hidden_width)
                total = jnp.dot(block, w_all[base + k], preferred_element_type=jnp.float32)
                high = total.astype(jnp.bfloat16)
                low = (total - high.astype(jnp.float32)).astype(jnp.bfloat16)
                for segment, value in enumerate((high, low)):
                    start = segment * slots + k * capacity
                    p_all[:count * planes, start:start + capacity, :] = value.reshape(-1, capacity, width)

        def mixed(shift, source, plane):
            index = pl.ds(lax.rem(shift * (1 + 2 * c), 4) * planes + plane, 1)
            mine = number == gate_ref[group, 2, index, :]
            high, low = (jnp.where(mine, gate_ref[group, part, index, :], 0.0) for part in range(2))
            weights = jnp.concatenate([high, low], 0).astype(jnp.bfloat16)
            value = jnp.dot(weights, p_all[source], preferred_element_type=jnp.float32)
            return value[:rows] + value[rows:]

        return start, multiply, mixed

    def sum_copy(turn):
        source = given_refs[0].at[given[0].index(shifts[turn])]
        return pltpu.make_async_copy(source, sums.at[turn], sum_sem.at[turn])

    def out_copy(turn):
        if last:
            return pltpu.make_async_copy(out_all.at[turn], out_ref.at[:, turn], out_sem.at[turn])
        return pltpu.make_async_copy(sums.at[turn], out_ref.at[turn], out_sem.at[turn])

    start, multiply, mixed = stage(0, lax.rem(c + core, 2), turns)
    added = [turn for turn in range(turns) if given and shifts[turn] in given[0]]
    if early:
        start_early, multiply_early, mixed_early = stage(1, c, len(early))
        start_early()
    start()
    for turn in added:
        sum_copy(turn).start()
    if early:
        multiply_early()
        for place, shift in enumerate(early):
            turn = shifts.index(shift)

            def one(plane, _, place=place, shift=shift, turn=turn):
                sums[turn, plane] = mixed_early(shift, place * planes + plane, plane)
                return 0

            lax.fori_loop(0, planes, one, 0, unroll=8)
    multiply()
    for turn in added:
        sum_copy(turn).wait()

    def combine(turn, _):
        shift = shifts[0] + turn + turn // 2 * (shifts[-1] - shifts[0] + 1 - turns)

        def one(plane, _):
            value = mixed(shift, turn * planes + plane, plane)
            if last:
                out_all[turn, plane] = (sums[turn, plane] + value).astype(out_all.dtype)
            else:
                sums[turn, plane] = value
            return 0

        lax.fori_loop(0, planes, one, 0, unroll=8)
        out_copy(turn).start()
        return 0

    lax.fori_loop(0, turns, combine, 0)
    for turn in range(turns):
        out_copy(turn).wait()


def wait_for_kernel(in_ref, sums_ref, out_ref):
    out_ref[...] = in_ref[0]


def wait_for(value, sums):
    lanes = value.shape[2] // 8
    return pl.pallas_call(
        wait_for_kernel, grid=(1,), out_shape=jax.ShapeDtypeStruct((16, lanes), value.dtype),
        in_specs=[pl.BlockSpec((1, 16, lanes), lambda i: (0, 0, 0)), pl.BlockSpec(memory_space=pl.ANY)], out_specs=pl.BlockSpec((16, lanes), lambda i: (0, 0)),
        cost_estimate=pl.CostEstimate(flops=BESIDE, bytes_accessed=8192, transcendentals=0),
    )(value, sums)


def experts_call(core, shifts, pos, xs, weight, gate, rows, given=(), early=(), early_weight=None):
    turns = len(shifts)
    blocks, experts, depth, width = weight.shape
    planes, part_slots, hidden_width = xs[0][0].shape
    part_slots = part_slots // 2
    slots = 2 * part_slots
    total = jax.ShapeDtypeStruct((turns, planes, rows, width), jnp.float32)
    out = jax.ShapeDtypeStruct((planes, turns, rows, width), jnp.bfloat16) if core else total
    hbm = pl.BlockSpec(memory_space=pl.ANY)
    arrays = [xs[part][shift] for part in range(2) for shift in shifts] + [weight]
    if early:
        arrays += [xs[part][shift] for part in range(2) for shift in early] + [early_weight]
    stages = 1 + bool(early)
    flops = 2 * turns * planes * slots * hidden_width * width
    bf16 = lambda *shape: pltpu.VMEM(shape, jnp.bfloat16)
    return pl.pallas_call(
        functools.partial(experts_kernel, core, shifts, [v[0] for v in given], early),
        out_shape=out,
        in_specs=[SMEM] + [hbm] * len(arrays) + [VMEM] + [hbm] * (2 * len(given)),
        out_specs=hbm,
        scratch_shapes=[
            bf16(2, turns + len(early), planes, part_slots, hidden_width),
            bf16(stages * experts, blocks * depth, width),
            bf16(turns * planes, 2 * slots, width),
            pltpu.VMEM(total.shape, jnp.float32),
            bf16(turns, planes, rows, width),
            pltpu.SemaphoreType.DMA((2, turns + len(early))),
            pltpu.SemaphoreType.DMA((stages * experts, blocks)),
            pltpu.SemaphoreType.DMA((turns,)),
            pltpu.SemaphoreType.DMA((turns,)),
        ],
        compiler_params=pltpu.CompilerParams(vmem_limit_bytes=(46 if core else 60) << 20),
        cost_estimate=cost(flops, *arrays, total, out) if core else cost(BESIDE, gate),
    )(pos, *arrays, gate, *[v[1] for v in given], *[v[2] for v in given])


def place_kernel(pos_ref, *refs):
    in_refs, out_ref = refs[:-1], refs[-1]
    width = in_refs[0].shape[1]
    for d, in_ref in enumerate(in_refs):
        turned = lax.rem(pos_ref[2] + d * (1 + 2 * pos_ref[1]), len(in_refs))
        start = pl.multiple_of(turned * width, 128)
        out_ref[:, pl.ds(start, width)] = in_ref[...]


def place_blocks(pos, blocks):
    rows, width = blocks[0].shape
    shape = jax.ShapeDtypeStruct((rows, width * len(blocks)), blocks[0].dtype)
    return pl.pallas_call(
        place_kernel, out_shape=shape, in_specs=[SMEM] + [VMEM] * len(blocks), out_specs=VMEM,
        compiler_params=PARAMS, cost_estimate=cost(0, shape, shape),
    )(pos, *blocks)


def per_device(trainer_weight, owner, expert_ids, gates, hidden):
    experts = owner.shape[0]
    rows, fanout = expert_ids.shape
    hidden_width = hidden.shape[2]
    capacity = min(rows, 2 * rows * fanout // experts)
    own = trainer_weight[0, 0]
    exp_train, slice_rows, width = own.shape
    ny = lax.axis_size("y")
    groups = experts // exp_train
    slots = exp_train * capacity
    block_width = width // ny
    low = lax.axis_size("zl")
    z, c, y = lax.axis_index("zh") * low + lax.axis_index("zl"), lax.axis_index("c"), lax.axis_index("y")
    pos = jnp.stack([z, c, y, lax.axis_index("x")]).astype(jnp.int32)

    zl, cs, zh = (lax.axis_size(a) for a in ("zl", "c", "zh"))
    slot_of = owner.reshape(zl, cs, zh, exp_train).transpose(2, 0, 1, 3).reshape(experts)
    match = expert_ids[:, :, None] == slot_of[None, None, :]
    named = jnp.any(match, axis=1)
    position = jnp.cumsum(named.astype(jnp.int32), axis=0) - 1
    place = jnp.arange(experts, dtype=jnp.int32)[None, :] * capacity + position
    flat = jnp.sum(jnp.where(match, place[:, None, :], 0), axis=2).reshape(1, -1)
    pairs = hidden.reshape(-1, hidden_width)

    planes = groups // 2
    half = exp_train // 2
    send = lambda first, flat, beside=0: dispatch(
        first * capacity, half * capacity, slots, flat, pairs, groups, beside
    ).reshape(planes, -1, hidden_width)
    outbound = send(0, flat)
    first = lax.all_to_all(outbound, Z, 0, 0, tiled=True)

    chosen = jnp.arange(experts * capacity, dtype=jnp.int32)[:, None] == flat
    pair_row = jnp.arange(rows * fanout, dtype=jnp.int32) // fanout
    slot_gate = jnp.sum(jnp.where(chosen, gates.reshape(-1)[None, :], 0.0), axis=1).reshape(groups, slots)
    slot_row = jnp.sum(jnp.where(chosen, pair_row[None, :] + 1, 0), axis=1).reshape(groups, slots) - 1

    by_core = lambda v: v.astype(jnp.float32).reshape(planes, 2, slots).transpose(1, 0, 2).reshape(groups, slots)
    blocks = split_blocks(pos, own, after(by_core(slot_gate), outbound), by_core(slot_row), ny)
    blocks = [blocks[0]] + [shifted(blocks[d], "y", d) for d in range(1, ny)]
    joined, info = join_blocks(pos, blocks, exp_train, slice_rows, 4 * slots)
    weight = lax.all_gather(joined, "x")

    first_up, first_down = mirrored(first, "y", 1), mirrored(first, "y", -1)
    second = lax.all_to_all(send(half, after(flat, first, joined), BESIDE), Z, 0, 0, tiled=True)
    first_opposite = mirrored(after(first_up, first_down), "y", 1)
    second_late = after(second, first_opposite)
    second_up, second_down = mirrored(second_late, "y", 1), mirrored(second_late, "y", -1)
    info = lax.all_to_all(after(info, second).reshape(ny, 2, planes, 4 * slots), Z, 2, 2, tiled=True)
    gate = gates_call(after(info, second_up, second_down), slots)
    second_opposite = mirrored(after(second_up, second_down), "y", 1)
    other_weight = shifted(after(weight, gate), "c", 1)

    xs = [first, first_up, first_opposite, first_down], [second, second_up, second_opposite, second_down]
    near, every = (0, 1, 3), (0, 1, 2, 3)
    sums = (near, experts_call(0, near, pos, xs, weight, gate, rows))
    sums = (near, sums[1], wait_for(second_opposite, sums[1]))
    partial = experts_call(1, every, pos, xs, other_weight, gate, rows, (sums,), (2,), weight)
    partial = partial.reshape(-1, block_width)
    summed = lax.psum_scatter(partial, Z, scatter_dimension=0, tiled=True).reshape(ny, rows, block_width)
    final = [summed[0]] + [mirrored(summed[d], "y", -d) for d in range(1, ny)]
    return place_blocks(pos, final)


def solution(mesh):
    devices = mesh.devices.reshape(2, 2, 4, 4, 4)
    inner = Mesh(devices, AXES)
    rep, exp = ("zl", "c"), ("zh", "x", "y")
    return jax.shard_map(
        per_device,
        mesh=inner,
        in_specs=(
            P(rep, exp, None, None, None),
            P(),
            P(rep + exp, None),
            P(rep + exp, None),
            P(rep + exp, None, None),
        ),
        out_specs=P(rep + exp, None),
        check_vma=False,
    )
```

```python
import functools
import jax
import jax.numpy as jnp
from jax import lax
from jax.experimental import pallas as pl
from jax.experimental.pallas import tpu as pltpu
from jax.sharding import Mesh, PartitionSpec as P

AXES = ("zl", "c", "zh", "x", "y")
Z = ("zh", "zl")
VMEM = pl.BlockSpec(memory_space=pltpu.VMEM)
SMEM = pl.BlockSpec(memory_space=pltpu.SMEM)
BESIDE = 60_000_000_000
PARAMS = pltpu.CompilerParams(vmem_limit_bytes=48 << 20)


def shifted(value, axis, steps):
    count = lax.axis_size(axis)
    return lax.ppermute(value, axis, [(i, (i + steps) % count) for i in range(count)])


def mirrored(value, axis, steps):
    cores, count = lax.axis_size("c"), lax.axis_size(axis)
    pairs = [(c * count + i, c * count + (i + (1 - 2 * c) * steps) % count) for c in range(cores) for i in range(count)]
    return lax.ppermute(value, ("c", axis), pairs)


def after(value, *others):
    return lax.optimization_barrier((value, *others))[0]


def cost(flops, *arrays):
    size = sum(a.size * a.dtype.itemsize for a in arrays)
    return pl.CostEstimate(flops=flops, bytes_accessed=size, transcendentals=0)


def split_kernel(pos_ref, w_ref, gate_ref, row_ref, *out_refs):
    count = len(out_refs)
    exp_train, depth, _ = w_ref.shape
    groups, slots = gate_ref.shape
    size, width = exp_train * depth, out_refs[0].shape[1]
    gate = gate_ref[...]
    high = gate.astype(jnp.bfloat16)
    low = (gate - high.astype(jnp.float32)).astype(jnp.bfloat16)
    for d, out_ref in enumerate(out_refs):
        start = pl.multiple_of(lax.rem(pos_ref[2] + d, count) * width, 128)
        out_ref[:size] = w_ref[:, :, pl.ds(start, width)].reshape(size, width)
        out_ref[size:] = jnp.zeros((groups, width), jnp.bfloat16)
        for part, value in enumerate((high, low, row_ref[...].astype(jnp.bfloat16))):
            out_ref[size:, part * slots:(part + 1) * slots] = value


def split_blocks(pos, own, gate, row, count):
    exp_train, depth, width = own.shape
    shape = jax.ShapeDtypeStruct((exp_train * depth + gate.shape[0], width // count), own.dtype)
    return pl.pallas_call(
        split_kernel, out_shape=[shape] * count, in_specs=[SMEM] + [VMEM] * 3, out_specs=[VMEM] * count,
        compiler_params=PARAMS, cost_estimate=cost(0, own, own),
    )(pos, own, gate, row)


def join_kernel(pos_ref, *refs):
    *in_refs, out_ref, info_ref = refs
    count = len(in_refs)
    exp_train, hidden, width = out_ref.shape
    depth = hidden // count
    size, lanes = exp_train * depth, info_ref.shape[2]
    for d, in_ref in enumerate(in_refs):
        start = pl.multiple_of(lax.rem(pos_ref[2] + count - d, count) * depth, depth)
        out_ref[:, pl.ds(start, depth), :] = in_ref[:size].reshape(exp_train, depth, width)
        info_ref[d] = in_ref[size:, :lanes]


def join_blocks(pos, blocks, exp_train, depth, lanes):
    total, width = blocks[0].shape
    count = len(blocks)
    shape = jax.ShapeDtypeStruct((exp_train, depth * count, width), blocks[0].dtype)
    info = jax.ShapeDtypeStruct((count, total - exp_train * depth, lanes), blocks[0].dtype)
    return pl.pallas_call(
        join_kernel, out_shape=[shape, info], in_specs=[SMEM] + [VMEM] * count, out_specs=[VMEM] * 2,
        compiler_params=PARAMS, cost_estimate=cost(BESIDE // 8, shape, shape),
    )(pos, *blocks)


def dispatch_kernel(groups, whole, first_ref, flat_ref, hidden_ref, out_ref):
    slots, pairs = out_ref.shape[1], flat_ref.shape[1]
    number = lax.broadcasted_iota(jnp.int32, (groups * slots, pairs), 0)
    number = number // slots * whole + lax.rem(number, slots) + first_ref[0]
    chosen = jnp.where(number == flat_ref[...], 1.0, 0.0).astype(jnp.bfloat16)
    rows = jnp.dot(chosen, hidden_ref[...], preferred_element_type=jnp.float32).astype(jnp.bfloat16)
    out_ref[...] = rows.reshape(out_ref.shape)


def dispatch(first, slots, whole, flat, hidden, groups, beside=0):
    shape = jax.ShapeDtypeStruct((groups, slots, hidden.shape[1]), hidden.dtype)
    return pl.pallas_call(
        functools.partial(dispatch_kernel, groups, whole),
        out_shape=shape, in_specs=[SMEM, VMEM, VMEM], out_specs=VMEM,
        compiler_params=PARAMS, cost_estimate=cost(2 * groups * slots * hidden.size + beside, hidden, shape),
    )(jnp.full((1,), first, jnp.int32), flat, hidden)


def gates_kernel(info_ref, out_ref):
    shifts, cores, planes, _ = info_ref.shape
    slots = out_ref.shape[3] // 2
    out_ref[...] = jnp.zeros_like(out_ref)
    for d in range(shifts):
        for core in range(cores):
            info = info_ref[d, core].astype(jnp.float32)
            high, low, row = (info[:, i * slots:(i + 1) * slots] for i in range(3))
            for part, place, value in ((0, 0, high), (0, 1, high), (1, 0, low), (2, 0, row), (2, 1, row)):
                out_ref[core, part, d * planes:(d + 1) * planes, place * slots:(place + 1) * slots] = value


def gates_call(info, slots):
    shifts, cores, planes, _ = info.shape
    shape = jax.ShapeDtypeStruct((cores, 3, shifts * planes, 2 * slots), jnp.float32)
    return pl.pallas_call(
        gates_kernel, out_shape=shape, in_specs=[VMEM], out_specs=VMEM,
        compiler_params=PARAMS, cost_estimate=cost(BESIDE, info, shape),
    )(info)


def experts_kernel(core, shifts, given, early, pos_ref, *refs):
    turns = len(shifts)
    last = core == 1
    operands = []
    for count in (turns, len(early)):
        if count:
            operands.append((refs[:count], refs[count:2 * count], refs[2 * count]))
            refs = refs[2 * count + 1:]
    gate_ref, *refs = refs
    given_refs, out_ref = refs[:len(given)], refs[2 * len(given)]
    x_all, w_all, p_all, sums, out_all, x_sem, w_sem, sum_sem, out_sem = refs[1 + 2 * len(given):]
    _, _, planes, part_slots, hidden_width = x_all.shape
    blocks, experts, depth, width = operands[0][2].shape
    rows = sums.shape[2]
    slots = p_all.shape[1] // 2
    capacity = slots // experts
    c = pos_ref[1]
    number = lax.broadcasted_iota(jnp.int32, (rows, 2 * slots), 0).astype(jnp.float32)

    def stage(place, group, count):
        *x_refs, w_ref = operands[place]
        first, base = place * turns, place * experts

        def x_copy(part, turn):
            source = x_refs[part][turn].at[:, pl.ds(pl.multiple_of(group * part_slots, part_slots), part_slots), :]
            return pltpu.make_async_copy(source, x_all.at[part, first + turn], x_sem.at[part, first + turn])

        def w_copy(k, d):
            target = w_all.at[base + k, pl.ds(d * depth, depth), :]
            return pltpu.make_async_copy(w_ref.at[d, k], target, w_sem.at[base + k, d])

        def start():
            for k in range(experts):
                if k % 2 == 0:
                    for turn in range(count):
                        x_copy(k // 2, turn).start()
                for d in range(blocks):
                    w_copy(k, d).start()

        def multiply():
            for k in range(experts):
                if k % 2 == 0:
                    for turn in range(count):
                        x_copy(k // 2, turn).wait()
                for d in range(blocks):
                    w_copy(k, d).wait()
                held = k % 2 * capacity
                block = x_all[k // 2, first:first + count, :, held:held + capacity, :].reshape(-1, hidden_width)
                total = jnp.dot(block, w_all[base + k], preferred_element_type=jnp.float32)
                high = total.astype(jnp.bfloat16)
                low = (total - high.astype(jnp.float32)).astype(jnp.bfloat16)
                for segment, value in enumerate((high, low)):
                    start = segment * slots + k * capacity
                    p_all[:count * planes, start:start + capacity, :] = value.reshape(-1, capacity, width)

        def mixed(shift, source, plane):
            index = pl.ds(lax.rem(shift * (1 + 2 * c), 4) * planes + plane, 1)
            mine = number == gate_ref[group, 2, index, :]
            high, low = (jnp.where(mine, gate_ref[group, part, index, :], 0.0) for part in range(2))
            weights = jnp.concatenate([high, low], 0).astype(jnp.bfloat16)
            value = jnp.dot(weights, p_all[source], preferred_element_type=jnp.float32)
            return value[:rows] + value[rows:]

        return start, multiply, mixed

    def sum_copy(turn):
        source = given_refs[0].at[given[0].index(shifts[turn])]
        return pltpu.make_async_copy(source, sums.at[turn], sum_sem.at[turn])

    def out_copy(turn):
        if last:
            return pltpu.make_async_copy(out_all.at[turn], out_ref.at[:, turn], out_sem.at[turn])
        return pltpu.make_async_copy(sums.at[turn], out_ref.at[turn], out_sem.at[turn])

    start, multiply, mixed = stage(0, lax.rem(c + core, 2), turns)
    added = [turn for turn in range(turns) if given and shifts[turn] in given[0]]
    if early:
        start_early, multiply_early, mixed_early = stage(1, c, len(early))
        start_early()
    start()
    for turn in added:
        sum_copy(turn).start()
    if early:
        multiply_early()
        for place, shift in enumerate(early):
            turn = shifts.index(shift)

            def one(plane, _, place=place, shift=shift, turn=turn):
                sums[turn, plane] = mixed_early(shift, place * planes + plane, plane)
                return 0

            lax.fori_loop(0, planes, one, 0, unroll=8)
    multiply()
    for turn in added:
        sum_copy(turn).wait()

    def combine(turn, _):
        shift = shifts[0] + turn + turn // 2 * (shifts[-1] - shifts[0] + 1 - turns)

        def one(plane, _):
            value = mixed(shift, turn * planes + plane, plane)
            if last:
                out_all[turn, plane] = (sums[turn, plane] + value).astype(out_all.dtype)
            else:
                sums[turn, plane] = value
            return 0

        lax.fori_loop(0, planes, one, 0, unroll=8)
        out_copy(turn).start()
        return 0

    lax.fori_loop(0, turns, combine, 0, unroll=True)
    for turn in range(turns):
        out_copy(turn).wait()


def wait_for_kernel(in_ref, sums_ref, out_ref):
    out_ref[...] = in_ref[0]


def wait_for(value, sums):
    lanes = value.shape[2] // 8
    return pl.pallas_call(
        wait_for_kernel, grid=(1,), out_shape=jax.ShapeDtypeStruct((16, lanes), value.dtype),
        in_specs=[pl.BlockSpec((1, 16, lanes), lambda i: (0, 0, 0)), pl.BlockSpec(memory_space=pl.ANY)], out_specs=pl.BlockSpec((16, lanes), lambda i: (0, 0)),
        cost_estimate=pl.CostEstimate(flops=BESIDE, bytes_accessed=8192, transcendentals=0),
    )(value, sums)


def experts_call(core, shifts, pos, xs, weight, gate, rows, given=(), early=(), early_weight=None):
    turns = len(shifts)
    blocks, experts, depth, width = weight.shape
    planes, part_slots, hidden_width = xs[0][0].shape
    part_slots = part_slots // 2
    slots = 2 * part_slots
    total = jax.ShapeDtypeStruct((turns, planes, rows, width), jnp.float32)
    out = jax.ShapeDtypeStruct((planes, turns, rows, width), jnp.bfloat16) if core else total
    hbm = pl.BlockSpec(memory_space=pl.ANY)
    arrays = [xs[part][shift] for part in range(2) for shift in shifts] + [weight]
    if early:
        arrays += [xs[part][shift] for part in range(2) for shift in early] + [early_weight]
    stages = 1 + bool(early)
    flops = 2 * turns * planes * slots * hidden_width * width
    bf16 = lambda *shape: pltpu.VMEM(shape, jnp.bfloat16)
    return pl.pallas_call(
        functools.partial(experts_kernel, core, shifts, [v[0] for v in given], early),
        out_shape=out,
        in_specs=[SMEM] + [hbm] * len(arrays) + [VMEM] + [hbm] * (2 * len(given)),
        out_specs=hbm,
        scratch_shapes=[
            bf16(2, turns + len(early), planes, part_slots, hidden_width),
            bf16(stages * experts, blocks * depth, width),
            bf16(turns * planes, 2 * slots, width),
            pltpu.VMEM(total.shape, jnp.float32),
            bf16(turns, planes, rows, width),
            pltpu.SemaphoreType.DMA((2, turns + len(early))),
            pltpu.SemaphoreType.DMA((stages * experts, blocks)),
            pltpu.SemaphoreType.DMA((turns,)),
            pltpu.SemaphoreType.DMA((turns,)),
        ],
        compiler_params=pltpu.CompilerParams(vmem_limit_bytes=60 << 20),
        cost_estimate=cost(flops, *arrays, total, out) if core else cost(BESIDE, gate),
    )(pos, *arrays, gate, *[v[1] for v in given], *[v[2] for v in given])


def place_kernel(pos_ref, *refs):
    in_refs, out_ref = refs[:-1], refs[-1]
    width = in_refs[0].shape[1]
    for d, in_ref in enumerate(in_refs):
        turned = lax.rem(pos_ref[2] + d * (1 + 2 * pos_ref[1]), len(in_refs))
        start = pl.multiple_of(turned * width, 128)
        out_ref[:, pl.ds(start, width)] = in_ref[...]


def place_blocks(pos, blocks):
    rows, width = blocks[0].shape
    shape = jax.ShapeDtypeStruct((rows, width * len(blocks)), blocks[0].dtype)
    return pl.pallas_call(
        place_kernel, out_shape=shape, in_specs=[SMEM] + [VMEM] * len(blocks), out_specs=VMEM,
        compiler_params=PARAMS, cost_estimate=cost(0, shape, shape),
    )(pos, *blocks)


def per_device(trainer_weight, owner, expert_ids, gates, hidden):
    experts = owner.shape[0]
    rows, fanout = expert_ids.shape
    hidden_width = hidden.shape[2]
    capacity = min(rows, 2 * rows * fanout // experts)
    own = trainer_weight[0, 0]
    exp_train, slice_rows, width = own.shape
    ny = lax.axis_size("y")
    groups = experts // exp_train
    slots = exp_train * capacity
    block_width = width // ny
    low = lax.axis_size("zl")
    z, c, y = lax.axis_index("zh") * low + lax.axis_index("zl"), lax.axis_index("c"), lax.axis_index("y")
    pos = jnp.stack([z, c, y, lax.axis_index("x")]).astype(jnp.int32)

    zl, cs, zh = (lax.axis_size(a) for a in ("zl", "c", "zh"))
    slot_of = owner.reshape(zl, cs, zh, exp_train).transpose(2, 0, 1, 3).reshape(experts)
    match = expert_ids[:, :, None] == slot_of[None, None, :]
    named = jnp.any(match, axis=1)
    position = jnp.cumsum(named.astype(jnp.int32), axis=0) - 1
    place = jnp.arange(experts, dtype=jnp.int32)[None, :] * capacity + position
    flat = jnp.sum(jnp.where(match, place[:, None, :], 0), axis=2).reshape(1, -1)
    pairs = hidden.reshape(-1, hidden_width)

    planes = groups // 2
    half = exp_train // 2
    send = lambda first, flat, beside=0: dispatch(
        first * capacity, half * capacity, slots, flat, pairs, groups, beside
    ).reshape(planes, -1, hidden_width)
    outbound = send(0, flat)
    first = lax.all_to_all(outbound, Z, 0, 0, tiled=True)

    chosen = jnp.arange(experts * capacity, dtype=jnp.int32)[:, None] == flat
    pair_row = jnp.arange(rows * fanout, dtype=jnp.int32) // fanout
    slot_gate = jnp.sum(jnp.where(chosen, gates.reshape(-1)[None, :], 0.0), axis=1).reshape(groups, slots)
    slot_row = jnp.sum(jnp.where(chosen, pair_row[None, :] + 1, 0), axis=1).reshape(groups, slots) - 1

    by_core = lambda v: v.astype(jnp.float32).reshape(planes, 2, slots).transpose(1, 0, 2).reshape(groups, slots)
    blocks = split_blocks(pos, own, after(by_core(slot_gate), outbound), by_core(slot_row), ny)
    blocks = [blocks[0]] + [shifted(blocks[d], "y", d) for d in range(1, ny)]
    joined, info = join_blocks(pos, blocks, exp_train, slice_rows, 4 * slots)
    weight = lax.all_gather(joined, "x")

    first_up, first_down = mirrored(first, "y", 1), mirrored(first, "y", -1)
    second = lax.all_to_all(send(half, after(flat, first, joined), BESIDE), Z, 0, 0, tiled=True)
    first_opposite = mirrored(after(first_up, first_down), "y", 1)
    second_late = after(second, first_opposite)
    second_up, second_down = mirrored(second_late, "y", 1), mirrored(second_late, "y", -1)
    info = lax.all_to_all(after(info, second).reshape(ny, 2, planes, 4 * slots), Z, 2, 2, tiled=True)
    gate = gates_call(after(info, second_up, second_down), slots)
    second_opposite = mirrored(after(second_up, second_down), "y", 1)
    other_weight = shifted(after(weight, gate), "c", 1)

    xs = [first, first_up, first_opposite, first_down], [second, second_up, second_opposite, second_down]
    near, every = (0, 1, 3), (0, 1, 2, 3)
    sums = (near, experts_call(0, near, pos, xs, weight, gate, rows))
    sums = (near, sums[1], wait_for(second_opposite, sums[1]))
    partial = experts_call(1, every, pos, xs, other_weight, gate, rows, (sums,), (2,), weight)
    partial = partial.reshape(-1, block_width)
    summed = lax.psum_scatter(partial, Z, scatter_dimension=0, tiled=True).reshape(ny, rows, block_width)
    final = [summed[0]] + [mirrored(summed[d], "y", -d) for d in range(1, ny)]
    return place_blocks(pos, final)


def solution(mesh):
    devices = mesh.devices.reshape(2, 2, 4, 4, 4)
    inner = Mesh(devices, AXES)
    rep, exp = ("zl", "c"), ("zh", "x", "y")
    return jax.shard_map(
        per_device,
        mesh=inner,
        in_specs=(
            P(rep, exp, None, None, None),
            P(),
            P(rep + exp, None),
            P(rep + exp, None),
            P(rep + exp, None, None),
        ),
        out_specs=P(rep + exp, None),
        check_vma=False,
    )
```

```python
import functools
import jax
import jax.numpy as jnp
from jax import lax
from jax.experimental import pallas as pl
from jax.experimental.pallas import tpu as pltpu
from jax.sharding import Mesh, PartitionSpec as P

AXES = ("zl", "c", "zh", "x", "y")
Z = ("zh", "zl")
VMEM = pl.BlockSpec(memory_space=pltpu.VMEM)
SMEM = pl.BlockSpec(memory_space=pltpu.SMEM)
BESIDE = 60_000_000_000
PARAMS = pltpu.CompilerParams(vmem_limit_bytes=48 << 20)


def shifted(value, axis, steps):
    count = lax.axis_size(axis)
    return lax.ppermute(value, axis, [(i, (i + steps) % count) for i in range(count)])


def mirrored(value, axis, steps):
    cores, count = lax.axis_size("c"), lax.axis_size(axis)
    pairs = [(c * count + i, c * count + (i + (1 - 2 * c) * steps) % count) for c in range(cores) for i in range(count)]
    return lax.ppermute(value, ("c", axis), pairs)


def after(value, *others):
    return lax.optimization_barrier((value, *others))[0]


def cost(flops, *arrays):
    size = sum(a.size * a.dtype.itemsize for a in arrays)
    return pl.CostEstimate(flops=flops, bytes_accessed=size, transcendentals=0)


def split_kernel(pos_ref, w_ref, gate_ref, row_ref, *out_refs):
    count = len(out_refs)
    exp_train, depth, _ = w_ref.shape
    groups, slots = gate_ref.shape
    size, width = exp_train * depth, out_refs[0].shape[1]
    gate = gate_ref[...]
    high = gate.astype(jnp.bfloat16)
    low = (gate - high.astype(jnp.float32)).astype(jnp.bfloat16)
    for d, out_ref in enumerate(out_refs):
        start = pl.multiple_of(lax.rem(pos_ref[2] + d, count) * width, 128)
        out_ref[:size] = w_ref[:, :, pl.ds(start, width)].reshape(size, width)
        out_ref[size:] = jnp.zeros((groups, width), jnp.bfloat16)
        for part, value in enumerate((high, low, row_ref[...].astype(jnp.bfloat16))):
            out_ref[size:, part * slots:(part + 1) * slots] = value


def split_blocks(pos, own, gate, row, count):
    exp_train, depth, width = own.shape
    shape = jax.ShapeDtypeStruct((exp_train * depth + gate.shape[0], width // count), own.dtype)
    return pl.pallas_call(
        split_kernel, out_shape=[shape] * count, in_specs=[SMEM] + [VMEM] * 3, out_specs=[VMEM] * count,
        compiler_params=PARAMS, cost_estimate=cost(0, own, own),
    )(pos, own, gate, row)


def join_kernel(pos_ref, *refs):
    *in_refs, out_ref, info_ref = refs
    count = len(in_refs)
    exp_train, hidden, width = out_ref.shape
    depth = hidden // count
    size, lanes = exp_train * depth, info_ref.shape[2]
    for d, in_ref in enumerate(in_refs):
        start = pl.multiple_of(lax.rem(pos_ref[2] + count - d, count) * depth, depth)
        out_ref[:, pl.ds(start, depth), :] = in_ref[:size].reshape(exp_train, depth, width)
        info_ref[d] = in_ref[size:, :lanes]


def join_blocks(pos, blocks, exp_train, depth, lanes):
    total, width = blocks[0].shape
    count = len(blocks)
    shape = jax.ShapeDtypeStruct((exp_train, depth * count, width), blocks[0].dtype)
    info = jax.ShapeDtypeStruct((count, total - exp_train * depth, lanes), blocks[0].dtype)
    return pl.pallas_call(
        join_kernel, out_shape=[shape, info], in_specs=[SMEM] + [VMEM] * count, out_specs=[VMEM] * 2,
        compiler_params=PARAMS, cost_estimate=cost(BESIDE // 8, shape, shape),
    )(pos, *blocks)


def dispatch_kernel(groups, whole, first_ref, flat_ref, hidden_ref, out_ref):
    slots, pairs = out_ref.shape[1], flat_ref.shape[1]
    number = lax.broadcasted_iota(jnp.int32, (groups * slots, pairs), 0)
    number = number // slots * whole + lax.rem(number, slots) + first_ref[0]
    chosen = jnp.where(number == flat_ref[...], 1.0, 0.0).astype(jnp.bfloat16)
    rows = jnp.dot(chosen, hidden_ref[...], preferred_element_type=jnp.float32).astype(jnp.bfloat16)
    out_ref[...] = rows.reshape(out_ref.shape)


def dispatch(first, slots, whole, flat, hidden, groups, beside=0):
    shape = jax.ShapeDtypeStruct((groups, slots, hidden.shape[1]), hidden.dtype)
    return pl.pallas_call(
        functools.partial(dispatch_kernel, groups, whole),
        out_shape=shape, in_specs=[SMEM, VMEM, VMEM], out_specs=VMEM,
        compiler_params=PARAMS, cost_estimate=cost(2 * groups * slots * hidden.size + beside, hidden, shape),
    )(jnp.full((1,), first, jnp.int32), flat, hidden)


def gates_kernel(info_ref, out_ref):
    shifts, cores, planes, _ = info_ref.shape
    slots = out_ref.shape[3] // 2
    out_ref[...] = jnp.zeros_like(out_ref)
    for d in range(shifts):
        for core in range(cores):
            info = info_ref[d, core].astype(jnp.float32)
            high, low, row = (info[:, i * slots:(i + 1) * slots] for i in range(3))
            for part, place, value in ((0, 0, high), (0, 1, high), (1, 0, low), (2, 0, row), (2, 1, row)):
                out_ref[core, part, d * planes:(d + 1) * planes, place * slots:(place + 1) * slots] = value


def gates_call(info, slots):
    shifts, cores, planes, _ = info.shape
    shape = jax.ShapeDtypeStruct((cores, 3, shifts * planes, 2 * slots), jnp.float32)
    return pl.pallas_call(
        gates_kernel, out_shape=shape, in_specs=[VMEM], out_specs=VMEM,
        compiler_params=PARAMS, cost_estimate=cost(BESIDE, info, shape),
    )(info)


def experts_kernel(core, shifts, given, early, pos_ref, *refs):
    turns = len(shifts)
    last = core == 1
    operands = []
    for count in (turns, len(early)):
        if count:
            operands.append((refs[:count], refs[count:2 * count], refs[2 * count]))
            refs = refs[2 * count + 1:]
    gate_ref, *refs = refs
    given_refs, out_ref = refs[:len(given)], refs[2 * len(given)]
    x_all, w_all, p_all, sums, out_all, x_sem, w_sem, sum_sem, out_sem = refs[1 + 2 * len(given):]
    _, _, planes, part_slots, hidden_width = x_all.shape
    blocks, experts, depth, width = operands[0][2].shape
    rows = sums.shape[2]
    slots = p_all.shape[1] // 2
    capacity = slots // experts
    c = pos_ref[1]
    number = lax.broadcasted_iota(jnp.int32, (rows, 2 * slots), 0).astype(jnp.float32)

    def stage(place, group, count):
        *x_refs, w_ref = operands[place]
        first, base = place * turns, place * experts

        def x_copy(part, turn):
            source = x_refs[part][turn].at[:, pl.ds(pl.multiple_of(group * part_slots, part_slots), part_slots), :]
            return pltpu.make_async_copy(source, x_all.at[part, first + turn], x_sem.at[part, first + turn])

        def w_copy(k, d):
            target = w_all.at[base + k, pl.ds(d * depth, depth), :]
            return pltpu.make_async_copy(w_ref.at[d, k], target, w_sem.at[base + k, d])

        def start():
            for k in range(experts):
                if k % 2 == 0:
                    for turn in range(count):
                        x_copy(k // 2, turn).start()
                for d in range(blocks):
                    w_copy(k, d).start()

        def multiply():
            for k in range(experts):
                if k % 2 == 0:
                    for turn in range(count):
                        x_copy(k // 2, turn).wait()
                for d in range(blocks):
                    w_copy(k, d).wait()
                held = k % 2 * capacity
                block = x_all[k // 2, first:first + count, :, held:held + capacity, :].reshape(-1, hidden_width)
                total = jnp.dot(block, w_all[base + k], preferred_element_type=jnp.float32)
                high = total.astype(jnp.bfloat16)
                low = (total - high.astype(jnp.float32)).astype(jnp.bfloat16)
                for segment, value in enumerate((high, low)):
                    start = segment * slots + k * capacity
                    p_all[:count * planes, start:start + capacity, :] = value.reshape(-1, capacity, width)

        def mixed(shift, source, plane):
            index = pl.ds(lax.rem(shift * (1 + 2 * c), 4) * planes + plane, 1)
            mine = number == gate_ref[group, 2, index, :]
            high, low = (jnp.where(mine, gate_ref[group, part, index, :], 0.0) for part in range(2))
            weights = jnp.concatenate([high, low], 0).astype(jnp.bfloat16)
            value = jnp.dot(weights, p_all[source], preferred_element_type=jnp.float32)
            return value[:rows] + value[rows:]

        return start, multiply, mixed

    def sum_copy(turn):
        source = given_refs[0].at[given[0].index(shifts[turn])]
        return pltpu.make_async_copy(source, sums.at[turn], sum_sem.at[turn])

    def out_copy(turn):
        if last:
            return pltpu.make_async_copy(out_all.at[turn], out_ref.at[:, turn], out_sem.at[turn])
        return pltpu.make_async_copy(sums.at[turn], out_ref.at[turn], out_sem.at[turn])

    start, multiply, mixed = stage(0, lax.rem(c + core, 2), turns)
    added = [turn for turn in range(turns) if given and shifts[turn] in given[0]]
    if early:
        start_early, multiply_early, mixed_early = stage(1, c, len(early))
        start_early()
    start()
    for turn in added:
        sum_copy(turn).start()
    if early:
        multiply_early()
        for place, shift in enumerate(early):
            turn = shifts.index(shift)

            def one(plane, _, place=place, shift=shift, turn=turn):
                sums[turn, plane] = mixed_early(shift, place * planes + plane, plane)
                return 0

            lax.fori_loop(0, planes, one, 0, unroll=8)
    multiply()
    for turn in added:
        sum_copy(turn).wait()

    def combine(turn, _):
        shift = shifts[0] + turn + turn // 2 * (shifts[-1] - shifts[0] + 1 - turns)

        def one(plane, _):
            value = mixed(shift, turn * planes + plane, plane)
            if last:
                out_all[turn, plane] = (sums[turn, plane] + value).astype(out_all.dtype)
            else:
                sums[turn, plane] = value
            return 0

        lax.fori_loop(0, planes, one, 0, unroll=8)
        out_copy(turn).start()
        return 0

    lax.fori_loop(0, turns, combine, 0, unroll=True)
    for turn in range(turns):
        out_copy(turn).wait()


def wait_for_kernel(in_ref, sums_ref, out_ref):
    out_ref[...] = in_ref[0]


def wait_for(value, sums):
    lanes = value.shape[2] // 8
    return pl.pallas_call(
        wait_for_kernel, grid=(1,), out_shape=jax.ShapeDtypeStruct((16, lanes), value.dtype),
        in_specs=[pl.BlockSpec((1, 16, lanes), lambda i: (0, 0, 0)), pl.BlockSpec(memory_space=pl.ANY)], out_specs=pl.BlockSpec((16, lanes), lambda i: (0, 0)),
        cost_estimate=pl.CostEstimate(flops=BESIDE, bytes_accessed=8192, transcendentals=0),
    )(value, sums)


def experts_call(core, shifts, pos, xs, weight, gate, rows, given=(), early=(), early_weight=None):
    turns = len(shifts)
    blocks, experts, depth, width = weight.shape
    planes, part_slots, hidden_width = xs[0][0].shape
    part_slots = part_slots // 2
    slots = 2 * part_slots
    total = jax.ShapeDtypeStruct((turns, planes, rows, width), jnp.float32)
    out = jax.ShapeDtypeStruct((planes, turns, rows, width), jnp.bfloat16) if core else total
    hbm = pl.BlockSpec(memory_space=pl.ANY)
    arrays = [xs[part][shift] for part in range(2) for shift in shifts] + [weight]
    if early:
        arrays += [xs[part][shift] for part in range(2) for shift in early] + [early_weight]
    stages = 1 + bool(early)
    flops = 2 * turns * planes * slots * hidden_width * width
    bf16 = lambda *shape: pltpu.VMEM(shape, jnp.bfloat16)
    return pl.pallas_call(
        functools.partial(experts_kernel, core, shifts, [v[0] for v in given], early),
        out_shape=out,
        in_specs=[SMEM] + [hbm] * len(arrays) + [VMEM] + [hbm] * (2 * len(given)),
        out_specs=hbm,
        scratch_shapes=[
            bf16(2, turns + len(early), planes, part_slots, hidden_width),
            bf16(stages * experts, blocks * depth, width),
            bf16(turns * planes, 2 * slots, width),
            pltpu.VMEM(total.shape, jnp.float32),
            bf16(turns, planes, rows, width),
            pltpu.SemaphoreType.DMA((2, turns + len(early))),
            pltpu.SemaphoreType.DMA((stages * experts, blocks)),
            pltpu.SemaphoreType.DMA((turns,)),
            pltpu.SemaphoreType.DMA((turns,)),
        ],
        compiler_params=pltpu.CompilerParams(vmem_limit_bytes=(54 if core else 60) << 20),
        cost_estimate=cost(flops, *arrays, total, out) if core else cost(BESIDE, gate),
    )(pos, *arrays, gate, *[v[1] for v in given], *[v[2] for v in given])


def place_kernel(pos_ref, *refs):
    in_refs, out_ref = refs[:-1], refs[-1]
    width = in_refs[0].shape[1]
    for d, in_ref in enumerate(in_refs):
        turned = lax.rem(pos_ref[2] + d * (1 + 2 * pos_ref[1]), len(in_refs))
        start = pl.multiple_of(turned * width, 128)
        out_ref[:, pl.ds(start, width)] = in_ref[...]


def place_blocks(pos, blocks):
    rows, width = blocks[0].shape
    shape = jax.ShapeDtypeStruct((rows, width * len(blocks)), blocks[0].dtype)
    return pl.pallas_call(
        place_kernel, out_shape=shape, in_specs=[SMEM] + [VMEM] * len(blocks), out_specs=VMEM,
        compiler_params=PARAMS, cost_estimate=cost(0, shape, shape),
    )(pos, *blocks)


def per_device(trainer_weight, owner, expert_ids, gates, hidden):
    experts = owner.shape[0]
    rows, fanout = expert_ids.shape
    hidden_width = hidden.shape[2]
    capacity = min(rows, 2 * rows * fanout // experts)
    own = trainer_weight[0, 0]
    exp_train, slice_rows, width = own.shape
    ny = lax.axis_size("y")
    groups = experts // exp_train
    slots = exp_train * capacity
    block_width = width // ny
    low = lax.axis_size("zl")
    z, c, y = lax.axis_index("zh") * low + lax.axis_index("zl"), lax.axis_index("c"), lax.axis_index("y")
    pos = jnp.stack([z, c, y, lax.axis_index("x")]).astype(jnp.int32)

    zl, cs, zh = (lax.axis_size(a) for a in ("zl", "c", "zh"))
    slot_of = owner.reshape(zl, cs, zh, exp_train).transpose(2, 0, 1, 3).reshape(experts)
    match = expert_ids[:, :, None] == slot_of[None, None, :]
    named = jnp.any(match, axis=1)
    position = jnp.cumsum(named.astype(jnp.int32), axis=0) - 1
    place = jnp.arange(experts, dtype=jnp.int32)[None, :] * capacity + position
    flat = jnp.sum(jnp.where(match, place[:, None, :], 0), axis=2).reshape(1, -1)
    pairs = hidden.reshape(-1, hidden_width)

    planes = groups // 2
    half = exp_train // 2
    send = lambda first, flat, beside=0: dispatch(
        first * capacity, half * capacity, slots, flat, pairs, groups, beside
    ).reshape(planes, -1, hidden_width)
    outbound = send(0, flat)
    first = lax.all_to_all(outbound, Z, 0, 0, tiled=True)

    chosen = jnp.arange(experts * capacity, dtype=jnp.int32)[:, None] == flat
    pair_row = jnp.arange(rows * fanout, dtype=jnp.int32) // fanout
    slot_gate = jnp.sum(jnp.where(chosen, gates.reshape(-1)[None, :], 0.0), axis=1).reshape(groups, slots)
    slot_row = jnp.sum(jnp.where(chosen, pair_row[None, :] + 1, 0), axis=1).reshape(groups, slots) - 1

    by_core = lambda v: v.astype(jnp.float32).reshape(planes, 2, slots).transpose(1, 0, 2).reshape(groups, slots)
    blocks = split_blocks(pos, own, after(by_core(slot_gate), outbound), by_core(slot_row), ny)
    blocks = [blocks[0]] + [shifted(blocks[d], "y", d) for d in range(1, ny)]
    joined, info = join_blocks(pos, blocks, exp_train, slice_rows, 4 * slots)
    weight = lax.all_gather(joined, "x")

    first_up, first_down = mirrored(first, "y", 1), mirrored(first, "y", -1)
    second = lax.all_to_all(send(half, after(flat, first, joined), BESIDE), Z, 0, 0, tiled=True)
    first_opposite = mirrored(after(first_up, first_down), "y", 1)
    second_late = after(second, first_opposite)
    second_up, second_down = mirrored(second_late, "y", 1), mirrored(second_late, "y", -1)
    info = lax.all_to_all(after(info, second).reshape(ny, 2, planes, 4 * slots), Z, 2, 2, tiled=True)
    gate = gates_call(after(info, second_up, second_down), slots)
    second_opposite = mirrored(after(second_up, second_down), "y", 1)
    other_weight = shifted(after(weight, gate), "c", 1)

    xs = [first, first_up, first_opposite, first_down], [second, second_up, second_opposite, second_down]
    near, every = (0, 1, 3), (0, 1, 2, 3)
    sums = (near, experts_call(0, near, pos, xs, weight, gate, rows))
    sums = (near, sums[1], wait_for(second_opposite, sums[1]))
    partial = experts_call(1, every, pos, xs, other_weight, gate, rows, (sums,), (2,), weight)
    partial = partial.reshape(-1, block_width)
    summed = lax.psum_scatter(partial, Z, scatter_dimension=0, tiled=True).reshape(ny, rows, block_width)
    final = [summed[0]] + [mirrored(summed[d], "y", -d) for d in range(1, ny)]
    return place_blocks(pos, final)


def solution(mesh):
    devices = mesh.devices.reshape(2, 2, 4, 4, 4)
    inner = Mesh(devices, AXES)
    rep, exp = ("zl", "c"), ("zh", "x", "y")
    return jax.shard_map(
        per_device,
        mesh=inner,
        in_specs=(
            P(rep, exp, None, None, None),
            P(),
            P(rep + exp, None),
            P(rep + exp, None),
            P(rep + exp, None, None),
        ),
        out_specs=P(rep + exp, None),
        check_vma=False,
    )
```
